32 devices in a mesh: dom: 2 (over y), row: 4 (over z), nbr: 4 (over x, core).
Axes of the slice: x: 2, y: 2, z: 4, core: 2. Of those that a mesh axis runs over, the one named last changes fastest.
Arguments:
- blocks: float32 [24, 12, 128, 128], P(('dom', 'row'), 'nbr'), parts along dimension 0, may hold values from -0.15625 to 0.15625
- partner_ids: int32 [24, 12], P(('dom', 'row'), 'nbr'), parts along dimension 0, may hold values from 0 to 11, as said below
- counts: int32 [24], P(('dom', 'row')), parts along dimension 0, may hold values from 1 to 12, as said below
- start: float32 [3072, 32], P(('dom', 'row')), parts along dimension 0, may hold values from -6 to 6
Outputs:
- basis: float32 [3072, 32], P(('dom', 'row')), parts along dimension 0
- ritz: float32 [64, 32], P('dom'), parts along dimension 0
The draws below stay inside these ranges and needn't reach their ends.
There are 2 independent parts, one for each index of `dom`. The reference program is written for one: setup_inputs(seed, part) draws one part's arguments, and reference() takes and returns one part's arrays. A program takes and returns all parts, laid end to end along the dimension named above; each array names one. Nothing has to cross between parts.
Inputs may be any that keep to these rules, and one draw needn't show every extreme that they name: partner_ids[i,0] == i; slots 1 to counts[i] - 1 hold distinct block columns greater than i; slots from counts[i] on hold i. counts[i] <= min(12, 12 - i); counts[0] == 12.
All inputs are finite; a program needn't handle non-finite values.
Results may differ from the reference program's by a relative error of at most 0.0001.
Values sent between devices are 32-bit elements; how exact they have to be, the bound alone decides.
No kernel may reach another device: no remote copies, remote signals or barrier semaphores. Data moves between devices by JAX's collectives and lax.ppermute only.
A program may use at most 64 MiB of HBM per device.

```python
import jax
import jax.numpy as jnp
from jax import lax

BS = 128
K = 32
ITERS = 2
NBLK = 12
SLOTS = 12
NROWS = 1536


def pattern(key):
    base = jax.random.fold_in(key, 7)
    count_key = jax.random.fold_in(base, 1)
    pick_key = jax.random.fold_in(base, 2)
    row_index = jnp.arange(NBLK, dtype=jnp.int32)
    room = jnp.minimum(SLOTS, NBLK - row_index)
    wanted = jax.random.randint(count_key, (NBLK,), 1, SLOTS + 1, dtype=jnp.int32)
    counts = jnp.where(row_index == 0, SLOTS, jnp.minimum(wanted, room)).astype(jnp.int32)
    scores = jax.random.randint(pick_key, (NBLK, NBLK), 0, 2 ** 20, dtype=jnp.int32)
    column = row_index[None, :]
    ranked = jnp.where(column > row_index[:, None], scores * NBLK + column, -1 - column)
    ranked_values, picks = lax.top_k(ranked, SLOTS - 1)
    partners = jnp.concatenate([row_index[:, None], picks.astype(jnp.int32)], axis=1)
    slot_index = jnp.arange(SLOTS, dtype=jnp.int32)
    partners = jnp.where(slot_index[None, :] < counts[:, None], partners, row_index[:, None])
    return (partners.astype(jnp.int32), counts)


def draw_partner_ids(key, part):
    return pattern(key)[0]


def draw_counts(key, part):
    return pattern(key)[1]


def level_of(rng, extent, pieces, low, top_value):
    gain = 1.0
    for position, parts in pieces:
        steps = jax.random.uniform(jax.random.fold_in(jax.random.fold_in(rng, 6), position), (parts,), jnp.float32, low / len(pieces), top_value / len(pieces))
        gain = gain * jnp.repeat(jnp.exp(steps), extent[position] // parts).reshape((-1,) + (1,) * (len(extent) - 1 - position))
    return gain


def centred(stream_key, dims, deviation, most, split=(), kind=jnp.bfloat16):
    values = jax.random.normal(stream_key, dims, jnp.float32) * deviation
    if len(split) > 0:
        values = level_of(stream_key, dims, split, -0.22, 0.18) * values
    return jnp.clip(values, min=-most, max=most).astype(kind)


def setup_inputs(seed: int = 0, part: int = 0) -> dict:
    splits = jax.random.split(jax.random.key(seed), 5)
    own_keys = jax.random.split(jax.random.fold_in(splits[4], part), 5)
    return {
        "blocks": centred(own_keys[0], (NBLK, SLOTS, BS, BS), (SLOTS * BS) ** -0.5, 0.15625, ((0, 4), (1, 4)), jnp.float32),
        "partner_ids": draw_partner_ids(jax.random.fold_in(jax.random.fold_in(splits[4], part), 71), part),
        "counts": draw_counts(jax.random.fold_in(jax.random.fold_in(splits[4], part), 71), part),
        "start": centred(own_keys[3], (NROWS, K), 1.0, 6.0, ((0, 4),), jnp.float32),
    }


HIGH = lax.Precision.HIGHEST

def apply_matrix(blocks, partner_ids, counts, basis):
    tiles = basis.reshape(NBLK, BS, K)
    slot_index = jnp.arange(SLOTS, dtype=jnp.int32)
    row_index = jnp.arange(NBLK, dtype=jnp.int32)
    valid = slot_index[None, :] < counts[:, None]
    weight = jnp.where(valid, jnp.where(partner_ids == row_index[:, None], 0.5, 1.0), 0.0).astype(jnp.float32)

    def per_row(packed):
        tile_block, ids_row, weight_row, own_tile = packed
        far = tiles[ids_row] * weight_row[:, None, None]
        direct = jnp.einsum('pab,pbk->ak', tile_block, far, precision=HIGH)
        transposed = jnp.einsum('pab,ak->pbk', tile_block, own_tile, precision=HIGH) * weight_row[:, None, None]
        return (direct, transposed)
    direct, transposed = lax.map(per_row, (blocks, partner_ids, weight, tiles))
    spread = jax.ops.segment_sum(transposed.reshape(NBLK * SLOTS, BS, K), partner_ids.reshape(-1), num_segments=NBLK)
    return (direct + spread).reshape(NROWS, K)

def reference(blocks, partner_ids, counts, start):
    prior = start
    cross = jnp.zeros((K, K), jnp.float32)
    for step in range(ITERS):
        image = apply_matrix(blocks, partner_ids, counts, prior)
        gram = jnp.dot(image.T, image, precision=HIGH) / NROWS
        cross = jnp.dot(prior.T, image, precision=HIGH) / NROWS
        lower = jnp.linalg.cholesky(gram)
        prior = lax.linalg.triangular_solve(lower, image, left_side=False, lower=True, transpose_a=True)
    return (prior, cross)
```

```python
import functools

import jax
import jax.numpy as jnp
from jax import lax
from jax.experimental import pallas as pl
from jax.experimental.pallas import tpu as pltpu
from jax.sharding import PartitionSpec as P

HIGH = lax.Precision.HIGHEST
F32 = jnp.float32
VMEM = pl.BlockSpec(memory_space=pltpu.VMEM)
SMEM = pl.BlockSpec(memory_space=pltpu.SMEM)
PANEL = 8


def tree(parts):
    while len(parts) > 1:
        parts = [parts[i] + parts[i + 1] for i in range(0, len(parts), 2)]
    return parts[0]


def swap(x, axis, distance):
    return lax.ppermute(x, axis, [(i, i ^ distance) for i in range(lax.axis_size(axis))])


def mm(a, b):
    return lax.dot_general(a, b, (((1,), (0,)), ((), ())), precision=HIGH, preferred_element_type=F32)


def mm_t(a, b):
    return lax.dot_general(a, b, (((1,), (1,)), ((), ())), precision=HIGH, preferred_element_type=F32)


def weight_of(ids, counts, i, p, first_row, first_slot):
    used = first_slot + p < counts[i]
    return jnp.where(used, jnp.where(ids[i, p] == first_row + i, 0.5, 1.0), 0.0).astype(F32)


def transposed_products(blocks, ids, counts, image, out, first_row, first_slot):
    out[...] = jnp.zeros_like(out)
    for i in range(blocks.shape[0]):
        tile = image[i]
        for p in range(blocks.shape[1]):
            w = weight_of(ids, counts, i, p, first_row, first_slot)
            out[ids[i, p]] += mm(tile, blocks[i, p]) * w


def direct_products(blocks, ids, counts, whole, i, first_row, first_slot):
    total = None
    for p in range(blocks.shape[1]):
        w = weight_of(ids, counts, i, p, first_row, first_slot)
        term = mm_t(whole[ids[i, p]] * w, blocks[i, p])
        total = term if total is None else total + term
    return total


def place(block_rows, slots):
    row = lax.axis_index("row")
    return row, row * block_rows, lax.axis_index("nbr") * slots


def fill(messages, products, tiles, row, block_rows):
    for s, out in enumerate(messages, 1):
        peer = row ^ s
        for i in range(block_rows):
            out[i] = jnp.where(row < peer, products[peer * block_rows + i], tiles[i])


def first_kernel(rows, blocks, ids, counts, start, *refs):
    messages, (own, tiles), (products,) = refs[: rows - 1], refs[rows - 1 : rows + 1], refs[rows + 1 :]
    block_rows, slots, size, _ = blocks.shape
    row, first_row, first_slot = place(block_rows, slots)
    for i in range(block_rows):
        tiles[i] = start[i * size : (i + 1) * size, :].T
    transposed_products(blocks, ids, counts, tiles, products, first_row, first_slot)
    fill(messages, products, tiles, row, block_rows)
    own[...] = products[pl.ds(first_row, block_rows)]


def direct_kernel(rows, with_gram, blocks, ids, counts, own, tiles, *refs):
    received, refs = refs[: rows - 1], refs[rows - 1 :]
    if with_gram:
        gram, out, total, whole = refs
    else:
        out, whole = refs
    block_rows, slots, size, _ = blocks.shape
    row, first_row, first_slot = place(block_rows, slots)
    whole[pl.ds(first_row, block_rows)] = tiles[...]
    for s, message in enumerate(received, 1):
        whole[pl.ds((row ^ s) * block_rows, block_rows)] = message[:block_rows]
    for i in range(block_rows):
        value = own[i]
        for s, message in enumerate(received, 1):
            value += jnp.where(row > (row ^ s), message[i], 0.0)
        out[i] = value + direct_products(blocks, ids, counts, whole, i, first_row, first_slot)
    if with_gram:
        total[...] = tree([gram[...]] + [m[block_rows] for m in received])


def second_kernel(rows, parts, blocks, ids, counts, *refs):
    images, refs = refs[:parts], refs[parts:]
    messages, (own, tiles, gram, products) = refs[: rows - 1], refs[rows - 1 :]
    block_rows, slots, size, _ = blocks.shape
    row, first_row, first_slot = place(block_rows, slots)
    partial = None
    for i in range(block_rows):
        tile = tree([image[i] for image in images])
        tiles[i] = tile
        term = mm_t(tile, tile)
        partial = term if partial is None else partial + term
    columns = partial.shape[0]
    gram[...] = jnp.zeros_like(gram)
    gram[:, :columns] = partial
    transposed_products(blocks, ids, counts, tiles, products, first_row, first_slot)
    fill(messages, products, tiles, row, block_rows)
    for message in messages:
        message[block_rows] = gram[...]
    own[...] = products[pl.ds(first_row, block_rows)]


def inverse_factor(gram):
    n = gram.shape[0]
    rows = lax.broadcasted_iota(jnp.int32, (n, 2 * n), 0)
    lanes = lax.broadcasted_iota(jnp.int32, (n, 2 * n), 1)
    both = jnp.concatenate([jnp.where(rows == lanes, 1.0, 0.0)[:, :n], gram], axis=1)
    groups = [both[g : g + 8] for g in range(0, n, 8)]
    height = lax.broadcasted_iota(jnp.int32, (8, 2 * n), 0)
    for first in range(0, n, PANEL):
        g0 = first // 8
        columns = [
            [
                jnp.broadcast_to(group[:, n + first + t : n + first + t + 1], (8, 2 * n))
                for group in groups
            ]
            for t in range(PANEL)
        ]
        for t in range(PANEL):
            k = first + t
            gk, sk = k // 8, k % 8
            pivot = columns[t][gk][sk : sk + 1]
            inverse = 1.0 / pivot
            root = lax.rsqrt(pivot)
            source = groups[gk][sk : sk + 1]
            steps = {}
            for g in range(gk, len(groups)):
                m = columns[t][g] * inverse
                steps[g] = jnp.where(height > sk, m, 0.0) if g == gk else m
            for u in range(t + 1, PANEL):
                head = columns[u][gk][sk : sk + 1]
                for g in range(gk, len(groups)):
                    columns[u][g] = columns[u][g] - steps[g] * head
            for g in range(gk, len(groups)):
                groups[g] = groups[g] - steps[g] * source
            groups[gk] = jnp.where(height == sk, groups[gk] * root, groups[gk])
    return jnp.concatenate(groups, axis=0)[:, :n]


def factor_kernel(total, gram, out):
    columns = gram.shape[0]
    out[...] = inverse_factor(gram[:, :columns] / total)


def gram_kernel(parts, inverse, tiles, *refs):
    images, (image, out) = refs[:parts], refs[parts:]
    lower = inverse[...]
    gram, cross = None, None
    for i in range(tiles.shape[0]):
        tile = mm(lower, tree([part[i] for part in images]))
        prior = mm(lower, tiles[i])
        image[i] = tile
        g, c = mm_t(tile, tile), mm_t(prior, tile)
        gram, cross = (g, c) if gram is None else (gram + g, cross + c)
    out[...] = jnp.concatenate([gram, cross], axis=1)


def last_kernel(rows, total, image, *refs):
    parts, (basis, ritz) = refs[:rows], refs[rows:]
    both = tree([part[...] for part in parts]) / total
    columns = both.shape[0]
    ritz[...] = both[:, columns:]
    lower = inverse_factor(both[:, :columns])
    size = image.shape[2]
    for i in range(image.shape[0]):
        basis[i * size : (i + 1) * size, :] = mm(lower, image[i]).T


def body(blocks, partner_ids, counts, start):
    block_rows, slots, size, _ = blocks.shape
    columns = start.shape[1]
    rows, parts = lax.axis_size("row"), lax.axis_size("nbr")
    all_blocks = block_rows * rows
    total = float(all_blocks * size)
    shape = jax.ShapeDtypeStruct
    tile = shape((block_rows, columns, size), F32)
    longer = shape((block_rows + 1, columns, size), F32)
    wide = shape((columns, size), F32)
    work = [pltpu.VMEM((all_blocks, columns, size), F32)]
    index = [VMEM, SMEM, SMEM]
    stored = (blocks, partner_ids, counts)

    def call(kernel, name, specs, outs, scratch=()):
        return pl.pallas_call(
            kernel, name=name, in_specs=specs, out_specs=[VMEM] * len(outs), out_shape=outs, scratch_shapes=scratch
        )

    *messages, own, tiles = call(
        functools.partial(first_kernel, rows), "start_products", index + [VMEM], [tile] * (rows + 1), work
    )(*stored, start)
    received = [swap(m, "row", s) for s, m in enumerate(messages, 1)]
    (image,) = call(
        functools.partial(direct_kernel, rows, False), "direct_first", index + [VMEM] * (rows + 1), [tile], work
    )(*stored, own, tiles, *received)
    images = [image] + [swap(image, "nbr", s) for s in range(1, parts)]
    *messages, own, tiles, gram = call(
        functools.partial(second_kernel, rows, parts),
        "second_products",
        index + [VMEM] * parts,
        [longer] * (rows - 1) + [tile, tile, wide],
        work,
    )(*stored, *images)
    received = [swap(m, "row", s) for s, m in enumerate(messages, 1)]
    image, gram = call(
        functools.partial(direct_kernel, rows, True), "direct_second", index + [VMEM] * (rows + 2), [tile, wide], work
    )(*stored, own, tiles, *received, gram)
    images = [image] + [swap(image, "nbr", s) for s in range(1, parts)]
    (inverse,) = call(
        functools.partial(factor_kernel, total), "factor", [VMEM], [shape((columns, columns), F32)]
    )(gram)
    image, both = call(
        functools.partial(gram_kernel, parts),
        "gram",
        [VMEM] * (parts + 2),
        [tile, shape((columns, 2 * columns), F32)],
    )(inverse, tiles, *images)
    boths = [both] + [swap(both, "row", s) for s in range(1, rows)]
    basis, ritz = call(
        functools.partial(last_kernel, rows, total),
        "last",
        [VMEM] * (rows + 1),
        [shape(start.shape, F32), shape((columns, columns), F32)],
    )(image, *boths)
    return basis, ritz


def solution(mesh):
    return jax.shard_map(
        body,
        mesh=mesh,
        in_specs=(
            P(("dom", "row"), "nbr", None, None),
            P(("dom", "row"), "nbr"),
            P(("dom", "row")),
            P(("dom", "row"), None),
        ),
        out_specs=(P(("dom", "row"), None), P("dom", None)),
        check_vma=False,
    )
```

```python
import functools

import jax
import jax.numpy as jnp
from jax import lax
from jax.experimental import pallas as pl
from jax.experimental.pallas import tpu as pltpu
from jax.sharding import PartitionSpec as P

HIGH = lax.Precision.HIGHEST
F32 = jnp.float32
VMEM = pl.BlockSpec(memory_space=pltpu.VMEM)
SMEM = pl.BlockSpec(memory_space=pltpu.SMEM)
PANEL = 8
PARAMS = pltpu.CompilerParams(vmem_limit_bytes=8 * 2**20)


def tree(parts):
    while len(parts) > 1:
        parts = [parts[i] + parts[i + 1] for i in range(0, len(parts), 2)]
    return parts[0]


def swap(x, axis, distance):
    return lax.ppermute(x, axis, [(i, i ^ distance) for i in range(lax.axis_size(axis))])


def mm(a, b):
    return lax.dot_general(a, b, (((1,), (0,)), ((), ())), precision=HIGH, preferred_element_type=F32)


def mm_t(a, b):
    return lax.dot_general(a, b, (((1,), (1,)), ((), ())), precision=HIGH, preferred_element_type=F32)


def weight_of(ids, counts, i, p, first_row, first_slot):
    used = first_slot + p < counts[i]
    return jnp.where(used, jnp.where(ids[i, p] == first_row + i, 0.5, 1.0), 0.0).astype(F32)


def transposed_products(blocks, ids, counts, image, out, first_row, first_slot):
    out[...] = jnp.zeros_like(out)
    for i in range(blocks.shape[0]):
        tile = image[i]
        for p in range(blocks.shape[1]):
            w = weight_of(ids, counts, i, p, first_row, first_slot)
            out[ids[i, p]] += mm(tile, blocks[i, p]) * w


def direct_products(blocks, ids, counts, whole, i, first_row, first_slot):
    total = None
    for p in range(blocks.shape[1]):
        w = weight_of(ids, counts, i, p, first_row, first_slot)
        term = mm_t(whole[ids[i, p]] * w, blocks[i, p])
        total = term if total is None else total + term
    return total


def place(block_rows, slots):
    row = lax.axis_index("row")
    return row, row * block_rows, lax.axis_index("nbr") * slots


def fill(messages, products, tiles, row, block_rows):
    for s, out in enumerate(messages, 1):
        peer = row ^ s
        for i in range(block_rows):
            out[i] = jnp.where(row < peer, products[peer * block_rows + i], tiles[i])


def first_kernel(rows, blocks, ids, counts, start, *refs):
    messages, (own, tiles), (products,) = refs[: rows - 1], refs[rows - 1 : rows + 1], refs[rows + 1 :]
    block_rows, slots, size, _ = blocks.shape
    row, first_row, first_slot = place(block_rows, slots)
    for i in range(block_rows):
        tiles[i] = start[:, i * size : (i + 1) * size]
    transposed_products(blocks, ids, counts, tiles, products, first_row, first_slot)
    fill(messages, products, tiles, row, block_rows)
    own[...] = products[pl.ds(first_row, block_rows)]


def direct_kernel(rows, with_gram, blocks, ids, counts, own, tiles, *refs):
    received, refs = refs[: rows - 1], refs[rows - 1 :]
    if with_gram:
        gram, out, total, whole = refs
    else:
        out, whole = refs
    block_rows, slots, size, _ = blocks.shape
    row, first_row, first_slot = place(block_rows, slots)
    whole[pl.ds(first_row, block_rows)] = tiles[...]
    for s, message in enumerate(received, 1):
        whole[pl.ds((row ^ s) * block_rows, block_rows)] = message[:block_rows]
    for i in range(block_rows):
        value = own[i]
        for s, message in enumerate(received, 1):
            value += jnp.where(row > (row ^ s), message[i], 0.0)
        out[i] = value + direct_products(blocks, ids, counts, whole, i, first_row, first_slot)
    if with_gram:
        total[...] = tree([gram[...]] + [m[block_rows] for m in received])


def second_kernel(rows, parts, blocks, ids, counts, *refs):
    images, refs = refs[:parts], refs[parts:]
    messages, (own, tiles, gram, products) = refs[: rows - 1], refs[rows - 1 :]
    block_rows, slots, size, _ = blocks.shape
    row, first_row, first_slot = place(block_rows, slots)
    partial = None
    for i in range(block_rows):
        tile = tree([image[i] for image in images])
        tiles[i] = tile
        term = mm_t(tile, tile)
        partial = term if partial is None else partial + term
    columns = partial.shape[0]
    gram[...] = jnp.zeros_like(gram)
    gram[:, :columns] = partial
    transposed_products(blocks, ids, counts, tiles, products, first_row, first_slot)
    fill(messages, products, tiles, row, block_rows)
    for message in messages:
        message[block_rows] = gram[...]
    own[...] = products[pl.ds(first_row, block_rows)]


def inverse_factor(gram):
    n = gram.shape[0]
    rows = lax.broadcasted_iota(jnp.int32, (n, 2 * n), 0)
    lanes = lax.broadcasted_iota(jnp.int32, (n, 2 * n), 1)
    both = jnp.concatenate([jnp.where(rows == lanes, 1.0, 0.0)[:, :n], gram], axis=1)
    groups = [both[g : g + 8] for g in range(0, n, 8)]
    height = lax.broadcasted_iota(jnp.int32, (8, 2 * n), 0)
    for first in range(0, n, PANEL):
        g0 = first // 8
        columns = [
            [
                jnp.broadcast_to(group[:, n + first + t : n + first + t + 1], (8, 2 * n))
                for group in groups
            ]
            for t in range(PANEL)
        ]
        for t in range(PANEL):
            k = first + t
            gk, sk = k // 8, k % 8
            pivot = columns[t][gk][sk : sk + 1]
            inverse = 1.0 / pivot
            root = lax.rsqrt(pivot)
            source = groups[gk][sk : sk + 1]
            steps = {}
            for g in range(gk, len(groups)):
                m = columns[t][g] * inverse
                steps[g] = jnp.where(height > sk, m, 0.0) if g == gk else m
            for u in range(t + 1, PANEL):
                head = columns[u][gk][sk : sk + 1]
                for g in range(gk, len(groups)):
                    columns[u][g] = columns[u][g] - steps[g] * head
            for g in range(gk, len(groups)):
                groups[g] = groups[g] - steps[g] * source
            groups[gk] = jnp.where(height == sk, groups[gk] * root, groups[gk])
    return jnp.concatenate(groups, axis=0)[:, :n]


def factor_kernel(total, gram, out):
    columns = gram.shape[0]
    out[...] = inverse_factor(gram[:, :columns] / total)


def gram_kernel(parts, inverse, tiles, *refs):
    images, (image, out) = refs[:parts], refs[parts:]
    lower = inverse[...]
    gram, cross = None, None
    for i in range(tiles.shape[0]):
        tile = mm(lower, tree([part[i] for part in images]))
        prior = mm(lower, tiles[i])
        image[i] = tile
        g, c = mm_t(tile, tile), mm_t(prior, tile)
        gram, cross = (g, c) if gram is None else (gram + g, cross + c)
    out[...] = jnp.concatenate([gram, cross], axis=1)


def last_kernel(rows, total, image, *refs):
    parts, (basis, ritz) = refs[:rows], refs[rows:]
    both = tree([part[...] for part in parts]) / total
    columns = both.shape[0]
    ritz[...] = both[:, columns:]
    lower = inverse_factor(both[:, :columns])
    size = image.shape[2]
    for i in range(image.shape[0]):
        basis[:, i * size : (i + 1) * size] = mm(lower, image[i])


def body(blocks, partner_ids, counts, start):
    block_rows, slots, size, _ = blocks.shape
    columns = start.shape[1]
    rows, parts = lax.axis_size("row"), lax.axis_size("nbr")
    all_blocks = block_rows * rows
    total = float(all_blocks * size)
    shape = jax.ShapeDtypeStruct
    tile = shape((block_rows, columns, size), F32)
    longer = shape((block_rows + 1, columns, size), F32)
    wide = shape((columns, size), F32)
    work = [pltpu.VMEM((all_blocks, columns, size), F32)]
    index = [VMEM, SMEM, SMEM]
    stored = (blocks, partner_ids, counts)

    def call(kernel, name, specs, outs, scratch=()):
        return pl.pallas_call(
            kernel,
            name=name,
            in_specs=specs,
            out_specs=[VMEM] * len(outs),
            out_shape=outs,
            scratch_shapes=scratch,
            compiler_params=PARAMS,
        )

    *messages, own, tiles = call(
        functools.partial(first_kernel, rows), "start_products", index + [VMEM], [tile] * (rows + 1), work
    )(*stored, start.T)
    received = [swap(m, "row", s) for s, m in enumerate(messages, 1)]
    (image,) = call(
        functools.partial(direct_kernel, rows, False), "direct_first", index + [VMEM] * (rows + 1), [tile], work
    )(*stored, own, tiles, *received)
    images = [image] + [swap(image, "nbr", s) for s in range(1, parts)]
    *messages, own, tiles, gram = call(
        functools.partial(second_kernel, rows, parts),
        "second_products",
        index + [VMEM] * parts,
        [longer] * (rows - 1) + [tile, tile, wide],
        work,
    )(*stored, *images)
    received = [swap(m, "row", s) for s, m in enumerate(messages, 1)]
    image, gram = call(
        functools.partial(direct_kernel, rows, True), "direct_second", index + [VMEM] * (rows + 2), [tile, wide], work
    )(*stored, own, tiles, *received, gram)
    images = [image] + [swap(image, "nbr", s) for s in range(1, parts)]
    (inverse,) = call(
        functools.partial(factor_kernel, total), "factor", [VMEM], [shape((columns, columns), F32)]
    )(gram)
    image, both = call(
        functools.partial(gram_kernel, parts),
        "gram",
        [VMEM] * (parts + 2),
        [tile, shape((columns, 2 * columns), F32)],
    )(inverse, tiles, *images)
    boths = [both] + [swap(both, "row", s) for s in range(1, rows)]
    basis, ritz = call(
        functools.partial(last_kernel, rows, total),
        "last",
        [VMEM] * (rows + 1),
        [shape(start.shape[::-1], F32), shape((columns, columns), F32)],
    )(image, *boths)
    return basis.T, ritz


def solution(mesh):
    return jax.shard_map(
        body,
        mesh=mesh,
        in_specs=(
            P(("dom", "row"), "nbr", None, None),
            P(("dom", "row"), "nbr"),
            P(("dom", "row")),
            P(("dom", "row"), None),
        ),
        out_specs=(P(("dom", "row"), None), P("dom", None)),
        check_vma=False,
    )
```

```python
import functools

import jax
import jax.numpy as jnp
from jax import lax
from jax.experimental import pallas as pl
from jax.experimental.pallas import tpu as pltpu
from jax.sharding import PartitionSpec as P

F32 = jnp.float32
BF16 = jnp.bfloat16
VMEM = pl.BlockSpec(memory_space=pltpu.VMEM)
SMEM = pl.BlockSpec(memory_space=pltpu.SMEM)
HBM = pl.BlockSpec(memory_space=pltpu.HBM)
DMA = pltpu.SemaphoreType.DMA
PANEL = 8
PARAMS = pltpu.CompilerParams(vmem_limit_bytes=8 * 2**20)


def tree(parts):
    while len(parts) > 1:
        parts = [parts[i] + parts[i + 1] for i in range(0, len(parts), 2)]
    return parts[0]


def split(x):
    high = x.astype(BF16)
    rest = x - high.astype(F32)
    middle = rest.astype(BF16)
    return high, middle, (rest - middle.astype(F32)).astype(BF16)


def product(a_parts, b_parts, contract=0):
    n = a_parts[0].shape[0]

    def dot(a, b):
        return lax.dot_general(a, b, (((1,), (contract,)), ((), ())), preferred_element_type=F32)

    stacked = jnp.concatenate(a_parts, axis=0)
    high = dot(stacked, b_parts[0])
    middle = dot(stacked[: 2 * n], b_parts[1])
    low = dot(a_parts[0], b_parts[2])
    return high[:n] + ((high[n : 2 * n] + middle[:n]) + ((high[2 * n :] + middle[n:]) + low))


def joined(parts, axis):
    return [jnp.concatenate(level, axis=axis) for level in zip(*parts)]


def swap(x, axis, distance):
    return lax.ppermute(x, axis, [(i, i ^ distance) for i in range(lax.axis_size(axis))])


def swap_rows(x, even, odd):
    rows, parts = lax.axis_size("row"), lax.axis_size("nbr")
    pairs = [
        (r * parts + n, (r ^ (odd if n % 2 else even)) * parts + n) for r in range(rows) for n in range(parts)
    ]
    return lax.ppermute(x, ("row", "nbr"), pairs)


class Place:
    def __init__(self, rows, block_rows, slots):
        self.row = lax.axis_index("row")
        self.part = lax.axis_index("nbr")
        self.odd = self.part & 1
        self.block_rows, self.slots = block_rows, slots
        self.first_row = self.row * block_rows
        self.half = rows // 2
        self.peers = [self.row ^ (k + self.odd * self.half) for k in range(1, self.half)]
        self.middle = self.row ^ self.half

    def weight(self, ids, counts, member, i, p):
        slot = (self.part ^ member) * self.slots + p
        used = slot < counts[i]
        return jnp.where(used, jnp.where(ids[i, p] == self.first_row + i, 0.5, 1.0), 0.0).astype(F32)


def transposed_products(place, blocks, ids, counts, tiles, out):
    out[...] = jnp.zeros_like(out)
    size = out.shape[2]
    for i in range(place.block_rows):
        stored = [split(b[i, p]) for b in blocks for p in range(place.slots)]
        value = product(split(tiles[i]), joined(stored, 1))
        for m in range(len(blocks)):
            for p in range(place.slots):
                at = (m * place.slots + p) * size
                out[ids[m][i, p]] += value[:, at : at + size] * place.weight(ids[m], counts, m, i, p)


def direct_products(place, blocks, ids, counts, whole, i):
    stored, far = [], []
    for m, b in enumerate(blocks):
        for p in range(place.slots):
            stored.append(split(b[i, p].T))
            far.append(split(whole[ids[m][i, p]] * place.weight(ids[m], counts, m, i, p)))
    return product(joined(far, 1), joined(stored, 0))


def fill(place, messages, shared, products, tiles):
    n = place.block_rows
    for peer, out in zip(place.peers, messages):
        for i in range(n):
            out[i] = jnp.where(place.row < peer, products[peer * n + i], tiles[i])
    height = shared.shape[1]
    columns = pl.ds(place.odd * height, height)
    for i in range(n):
        shared[i] = jnp.where(
            place.row < place.middle, products[place.middle * n + i, columns], tiles[i, columns]
        )


def own_products(place, products, own):
    mine = products[pl.ds(place.first_row, place.block_rows)]
    own[...] = jnp.where(place.odd == 0, mine, 0.0)


def first_kernel(rows, blocks, other, ids, other_ids, counts, start, *refs):
    half = rows // 2
    messages, refs = refs[: half - 1], refs[half - 1 :]
    shared, own, tiles, held, products, ids_s, other_s, counts_s, sems = refs
    block_rows, slots, size, _ = blocks.shape
    place = Place(rows, block_rows, slots)
    copies = [
        pltpu.make_async_copy(blocks, held, sems.at[0]),
        pltpu.make_async_copy(ids, ids_s, sems.at[1]),
        pltpu.make_async_copy(other_ids, other_s, sems.at[2]),
        pltpu.make_async_copy(counts, counts_s, sems.at[3]),
    ]
    for i in range(block_rows):
        copies.append(pltpu.make_async_copy(start.at[:, i * size : (i + 1) * size], tiles.at[i], sems.at[4 + i]))
    for copy in copies:
        copy.start()
    for copy in copies:
        copy.wait()
    transposed_products(place, (held, other), (ids_s, other_s), counts_s, tiles, products)
    fill(place, messages, shared, products, tiles)
    own_products(place, products, own)


def direct_kernel(rows, with_gram, held, other, ids, other_ids, counts, own, tiles, *refs):
    half = rows // 2
    received, shared, refs = refs[: half - 1], refs[half - 1], refs[half:]
    if with_gram:
        gram, out, longer, whole = refs
    else:
        out, whole = refs
    block_rows, slots, size, _ = held.shape
    place = Place(rows, block_rows, slots)
    whole[...] = jnp.zeros_like(whole)
    whole[pl.ds(place.first_row, block_rows)] = jnp.where(place.odd == 0, tiles[...], 0.0)
    for peer, message in zip(place.peers, received):
        whole[pl.ds(peer * block_rows, block_rows)] = message[:block_rows]
    height = shared.shape[1]
    columns = pl.ds(place.odd * height, height)
    for i in range(block_rows):
        whole[place.middle * block_rows + i, columns] = shared[i]
    for i in range(block_rows):
        value = own[i]
        for peer, message in zip(place.peers, received):
            value += jnp.where(place.row > peer, message[i], 0.0)
        out[i] = value + direct_products(place, (held, other), (ids, other_ids), counts, whole, i)
        out[i, columns] += jnp.where(place.row > place.middle, shared[i], 0.0)
    if with_gram:
        for i in range(block_rows):
            longer[i] = out[i]
        n = 2 * height
        packed = shared[block_rows]
        middle = jnp.concatenate([packed[:, :n], packed[:, n : 2 * n]], axis=0)
        first = jnp.where(place.odd == 0, gram[:, :n], middle)
        longer[block_rows] = jnp.zeros_like(longer[block_rows])
        longer[block_rows, :, :n] = tree([first] + [message[block_rows][:, :n] for message in received])


def second_kernel(rows, parts, held, other, ids, other_ids, counts, *refs):
    images, refs = refs[:parts], refs[parts:]
    half = rows // 2
    messages, refs = refs[: half - 1], refs[half - 1 :]
    shared, own, tiles, gram, products = refs
    block_rows, slots, size, _ = held.shape
    place = Place(rows, block_rows, slots)
    for i in range(block_rows):
        tiles[i] = tree([image[i] for image in images])
    transposed_products(place, (held, other), (ids, other_ids), counts, tiles, products)
    fill(place, messages, shared, products, tiles)
    own_products(place, products, own)
    whole = joined([split(tiles[i]) for i in range(block_rows)], 1)
    partial = product(whole, whole, 1)
    gram[...] = jnp.zeros_like(gram)
    gram[:, : partial.shape[0]] = partial
    for message in messages:
        message[block_rows] = gram[...]
    height = shared.shape[1]
    shared[block_rows] = jnp.zeros_like(shared[block_rows])
    shared[block_rows, :, : 4 * height] = jnp.concatenate([partial[:height], partial[height:]], axis=1)


def inverse_factor(gram):
    n = gram.shape[0]
    rows = lax.broadcasted_iota(jnp.int32, (n, 2 * n), 0)
    lanes = lax.broadcasted_iota(jnp.int32, (n, 2 * n), 1)
    both = jnp.concatenate([jnp.where(rows == lanes, 1.0, 0.0)[:, :n], gram], axis=1)
    groups = [both[g : g + 8] for g in range(0, n, 8)]
    height = lax.broadcasted_iota(jnp.int32, (8, 2 * n), 0)
    for first in range(0, n, PANEL):
        columns = [
            [
                jnp.broadcast_to(group[:, n + first + t : n + first + t + 1], (8, 2 * n))
                for group in groups
            ]
            for t in range(PANEL)
        ]
        for t in range(PANEL):
            k = first + t
            gk, sk = k // 8, k % 8
            pivot = columns[t][gk][sk : sk + 1]
            inverse = 1.0 / pivot
            root = lax.rsqrt(pivot)
            source = groups[gk][sk : sk + 1]
            steps = {}
            for g in range(gk, len(groups)):
                m = columns[t][g] * inverse
                steps[g] = jnp.where(height > sk, m, 0.0) if g == gk else m
            for u in range(t + 1, PANEL):
                head = columns[u][gk][sk : sk + 1]
                for g in range(gk, len(groups)):
                    columns[u][g] = columns[u][g] - steps[g] * head
            for g in range(gk, len(groups)):
                groups[g] = groups[g] - steps[g] * source
            groups[gk] = jnp.where(height == sk, groups[gk] * root, groups[gk])
    return jnp.concatenate(groups, axis=0)[:, :n]


def factor_kernel(total, mine, others, out):
    block_rows = mine.shape[0] - 1
    columns = mine.shape[1]
    gram = mine[block_rows] + others[block_rows]
    out[...] = inverse_factor(gram[:, :columns] / total)


def gram_kernel(parts, inverse, tiles, *refs):
    images, (image, out) = refs[:parts], refs[parts:]
    block_rows, columns, size = tiles.shape
    lower = split(inverse[...])
    new = [tree([part[i] for part in images]) for i in range(block_rows)]
    value = product(lower, joined([split(new[i]) for i in range(block_rows)], 1))
    prior = product(lower, joined([split(tiles[i]) for i in range(block_rows)], 1))
    for i in range(block_rows):
        image[i] = value[:, i * size : (i + 1) * size]
    value = split(value)
    out[:, :columns] = product(value, value, 1)
    out[:, columns:] = product(split(prior), value, 1)


def last_kernel(rows, total, image, *refs):
    parts, (basis, ritz) = refs[:rows], refs[rows:]
    both = tree([part[...] for part in parts]) / total
    columns = both.shape[0]
    ritz[...] = both[:, columns:]
    lower = split(inverse_factor(both[:, :columns]))
    basis[...] = product(lower, joined([split(image[i]) for i in range(image.shape[0])], 1))


def body(blocks, partner_ids, counts, start):
    block_rows, slots, size, _ = blocks.shape
    columns = start.shape[1]
    rows, parts = lax.axis_size("row"), lax.axis_size("nbr")
    half = rows // 2
    all_blocks = block_rows * rows
    total = float(all_blocks * size)
    shape = jax.ShapeDtypeStruct
    tile = shape((block_rows, columns, size), F32)
    longer = shape((block_rows + 1, columns, size), F32)
    shorter = shape((block_rows, columns // 2, size), F32)
    shorter_longer = shape((block_rows + 1, columns // 2, size), F32)
    wide = shape((columns, size), F32)
    work = pltpu.VMEM((all_blocks, columns, size), F32)

    def call(kernel, name, specs, outs, scratch=()):
        return pl.pallas_call(
            kernel,
            name=name,
            in_specs=specs,
            out_specs=[VMEM] * len(outs),
            out_shape=outs,
            scratch_shapes=scratch,
            compiler_params=PARAMS,
        )

    def round_over_rows(messages, shared):
        return [swap_rows(m, k, k + half) for k, m in enumerate(messages, 1)], swap(shared, "row", half)

    def sum_over_parts(image):
        return [image] + [swap(image, "nbr", s) for s in range(1, parts)]

    other = swap(blocks, "nbr", 1)
    other_ids = swap(partner_ids, "nbr", 1)
    *messages, shared, own, tiles, held = call(
        functools.partial(first_kernel, rows),
        "first_transposed",
        [HBM, VMEM, HBM, HBM, HBM, HBM],
        [tile] * (half - 1) + [shorter, tile, tile, shape(blocks.shape, F32)],
        [
            work,
            pltpu.SMEM(partner_ids.shape, jnp.int32),
            pltpu.SMEM(partner_ids.shape, jnp.int32),
            pltpu.SMEM(counts.shape, jnp.int32),
            DMA((4 + block_rows,)),
        ],
    )(blocks, other, partner_ids, other_ids, counts, start.T)
    stored = (held, other, partner_ids, other_ids, counts)
    index = [VMEM, VMEM, SMEM, SMEM, SMEM]
    received, shared = round_over_rows(messages, shared)
    (image,) = call(
        functools.partial(direct_kernel, rows, False), "first_direct", index + [VMEM] * (half + 2), [tile], [work]
    )(*stored, own, tiles, *received, shared)
    images = sum_over_parts(image)
    *messages, shared, own, tiles, gram = call(
        functools.partial(second_kernel, rows, parts),
        "second_transposed",
        index + [VMEM] * parts,
        [longer] * (half - 1) + [shorter_longer, tile, tile, wide],
        [work],
    )(*stored, *images)
    received, shared = round_over_rows(messages, shared)
    image, mine = call(
        functools.partial(direct_kernel, rows, True),
        "second_direct",
        index + [VMEM] * (half + 3),
        [tile, longer],
        [work],
    )(*stored, own, tiles, *received, shared, gram)
    pair = swap(mine, "nbr", 1)
    images = [image, pair] + [swap(image, "nbr", s) for s in range(2, parts)]
    (inverse,) = call(
        functools.partial(factor_kernel, total), "factor", [VMEM] * 2, [shape((columns, columns), F32)]
    )(mine, pair)
    image, both = call(
        functools.partial(gram_kernel, parts),
        "gram",
        [VMEM] * (parts + 2),
        [tile, shape((columns, 2 * columns), F32)],
    )(inverse, tiles, *images)
    boths = [both] + [swap(both, "row", s) for s in range(1, rows)]
    basis, ritz = call(
        functools.partial(last_kernel, rows, total),
        "last",
        [VMEM] * (rows + 1),
        [shape(start.shape[::-1], F32), shape((columns, columns), F32)],
    )(image, *boths)
    return basis.T, ritz


def solution(mesh):
    return jax.shard_map(
        body,
        mesh=mesh,
        in_specs=(
            P(("dom", "row"), "nbr", None, None),
            P(("dom", "row"), "nbr"),
            P(("dom", "row")),
            P(("dom", "row"), None),
        ),
        out_specs=(P(("dom", "row"), None), P("dom", None)),
        check_vma=False,
    )
```

```python
import functools

import jax
import jax.numpy as jnp
from jax import lax
from jax.experimental import pallas as pl
from jax.experimental.pallas import tpu as pltpu
from jax.sharding import PartitionSpec as P

F32 = jnp.float32
BF16 = jnp.bfloat16
VMEM = pl.BlockSpec(memory_space=pltpu.VMEM)
SMEM = pl.BlockSpec(memory_space=pltpu.SMEM)
HBM = pl.BlockSpec(memory_space=pltpu.HBM)
DMA = pltpu.SemaphoreType.DMA
PANEL = 8
PARAMS = pltpu.CompilerParams(vmem_limit_bytes=8 * 2**20)


def tree(parts):
    while len(parts) > 1:
        parts = [parts[i] + parts[i + 1] for i in range(0, len(parts), 2)]
    return parts[0]


def split(x):
    high = x.astype(BF16)
    rest = x - high.astype(F32)
    middle = rest.astype(BF16)
    return high, middle, (rest - middle.astype(F32)).astype(BF16)


def product(a_parts, b_parts, contract=0):
    n = a_parts[0].shape[0]

    def dot(a, b):
        return lax.dot_general(a, b, (((1,), (contract,)), ((), ())), preferred_element_type=F32)

    stacked = jnp.concatenate(a_parts, axis=0)
    high = dot(stacked, b_parts[0])
    middle = dot(stacked[: 2 * n], b_parts[1])
    low = dot(a_parts[0], b_parts[2])
    return high[:n] + ((high[n : 2 * n] + middle[:n]) + ((high[2 * n :] + middle[n:]) + low))


def joined(parts, axis):
    return [jnp.concatenate(level, axis=axis) for level in zip(*parts)]


def swap(x, axis, distance):
    return lax.ppermute(x, axis, [(i, i ^ distance) for i in range(lax.axis_size(axis))])


def swap_rows(x, even, odd):
    rows, parts = lax.axis_size("row"), lax.axis_size("nbr")
    pairs = [
        (r * parts + n, (r ^ (odd if n % 2 else even)) * parts + n) for r in range(rows) for n in range(parts)
    ]
    return lax.ppermute(x, ("row", "nbr"), pairs)


class Place:
    def __init__(self, rows, block_rows, slots):
        self.row = lax.axis_index("row")
        self.part = lax.axis_index("nbr")
        self.odd = self.part & 1
        self.block_rows, self.slots = block_rows, slots
        self.first_row = self.row * block_rows
        self.half = rows // 2
        self.peers = [self.row ^ (k + self.odd * self.half) for k in range(1, self.half)]
        self.middle = self.row ^ self.half

    def weight(self, ids, counts, member, i, p):
        slot = (self.part ^ member) * self.slots + p
        used = slot < counts[i]
        return jnp.where(used, jnp.where(ids[i, p] == self.first_row + i, 0.5, 1.0), 0.0).astype(F32)


def transposed_products(place, blocks, ids, counts, tiles, out, copy=None):
    out[...] = jnp.zeros_like(out)
    size = out.shape[2]
    values = []
    for i in range(place.block_rows):
        stored = [split(b[i, p]) for b in blocks for p in range(place.slots)]
        values.append(product(split(tiles[i]), joined(stored, 1)))
    if copy is not None:
        copy.wait()
    for i, value in enumerate(values):
        for m in range(len(blocks)):
            for p in range(place.slots):
                at = (m * place.slots + p) * size
                out[ids[m][i, p]] += value[:, at : at + size] * place.weight(ids[m], counts, m, i, p)


def direct_products(place, blocks, ids, counts, whole, i):
    stored, far = [], []
    for m, b in enumerate(blocks):
        for p in range(place.slots):
            stored.append(split(b[i, p].T))
            far.append(split(whole[ids[m][i, p]] * place.weight(ids[m], counts, m, i, p)))
    return product(joined(far, 1), joined(stored, 0))


def fill(place, messages, shared, products, tiles):
    n = place.block_rows
    for peer, out in zip(place.peers, messages):
        for i in range(n):
            out[i] = jnp.where(place.row < peer, products[peer * n + i], tiles[i])
    height = shared.shape[1]
    columns = pl.ds(place.odd * height, height)
    for i in range(n):
        shared[i] = jnp.where(
            place.row < place.middle, products[place.middle * n + i, columns], tiles[i, columns]
        )


def own_products(place, products, own):
    mine = products[pl.ds(place.first_row, place.block_rows)]
    own[...] = jnp.where(place.odd == 0, mine, 0.0)


def load_kernel(blocks, ids, counts, start, held, ids_s, counts_s, tiles, sems):
    size = blocks.shape[2]
    copies = [
        pltpu.make_async_copy(blocks, held, sems.at[0]),
        pltpu.make_async_copy(ids, ids_s, sems.at[1]),
        pltpu.make_async_copy(counts, counts_s, sems.at[2]),
    ]
    for i in range(blocks.shape[0]):
        copies.append(pltpu.make_async_copy(start.at[:, i * size : (i + 1) * size], tiles.at[i], sems.at[3 + i]))
    for copy in copies:
        copy.start()
    for copy in copies:
        copy.wait()


def first_kernel(rows, held, other, ids, other_ids, counts, tiles, *refs):
    half = rows // 2
    messages, refs = refs[: half - 1], refs[half - 1 :]
    shared, own, other_s, products, sem = refs
    block_rows, slots, size, _ = held.shape
    place = Place(rows, block_rows, slots)
    copy = pltpu.make_async_copy(other_ids, other_s, sem.at[0])
    copy.start()
    transposed_products(place, (held, other), (ids, other_s), counts, tiles, products, copy)
    fill(place, messages, shared, products, tiles)
    own_products(place, products, own)


def direct_kernel(rows, with_gram, held, other, ids, other_ids, counts, own, tiles, *refs):
    half = rows // 2
    received, shared, refs = refs[: half - 1], refs[half - 1], refs[half:]
    if with_gram:
        gram, out, longer, whole = refs
    else:
        out, whole = refs
    block_rows, slots, size, _ = held.shape
    place = Place(rows, block_rows, slots)
    whole[...] = jnp.zeros_like(whole)
    whole[pl.ds(place.first_row, block_rows)] = jnp.where(place.odd == 0, tiles[...], 0.0)
    for peer, message in zip(place.peers, received):
        whole[pl.ds(peer * block_rows, block_rows)] = message[:block_rows]
    height = shared.shape[1]
    columns = pl.ds(place.odd * height, height)
    for i in range(block_rows):
        whole[place.middle * block_rows + i, columns] = shared[i]
    for i in range(block_rows):
        value = own[i]
        for peer, message in zip(place.peers, received):
            value += jnp.where(place.row > peer, message[i], 0.0)
        out[i] = value + direct_products(place, (held, other), (ids, other_ids), counts, whole, i)
        out[i, columns] += jnp.where(place.row > place.middle, shared[i], 0.0)
    if with_gram:
        for i in range(block_rows):
            longer[i] = out[i]
        n = 2 * height
        packed = shared[block_rows]
        middle = jnp.concatenate([packed[:, :n], packed[:, n : 2 * n]], axis=0)
        first = jnp.where(place.odd == 0, gram[:, :n], middle)
        longer[block_rows] = jnp.zeros_like(longer[block_rows])
        longer[block_rows, :, :n] = tree([first] + [message[block_rows][:, :n] for message in received])


def second_kernel(rows, parts, held, other, ids, other_ids, counts, *refs):
    images, refs = refs[:parts], refs[parts:]
    half = rows // 2
    messages, refs = refs[: half - 1], refs[half - 1 :]
    shared, own, tiles, gram, products = refs
    block_rows, slots, size, _ = held.shape
    place = Place(rows, block_rows, slots)
    for i in range(block_rows):
        tiles[i] = tree([image[i] for image in images])
    transposed_products(place, (held, other), (ids, other_ids), counts, tiles, products)
    fill(place, messages, shared, products, tiles)
    own_products(place, products, own)
    whole = joined([split(tiles[i]) for i in range(block_rows)], 1)
    partial = product(whole, whole, 1)
    gram[...] = jnp.zeros_like(gram)
    gram[:, : partial.shape[0]] = partial
    for message in messages:
        message[block_rows] = gram[...]
    height = shared.shape[1]
    shared[block_rows] = jnp.zeros_like(shared[block_rows])
    shared[block_rows, :, : 4 * height] = jnp.concatenate([partial[:height], partial[height:]], axis=1)


def inverse_factor(gram):
    n = gram.shape[0]
    rows = lax.broadcasted_iota(jnp.int32, (n, 2 * n), 0)
    lanes = lax.broadcasted_iota(jnp.int32, (n, 2 * n), 1)
    both = jnp.concatenate([jnp.where(rows == lanes, 1.0, 0.0)[:, :n], gram], axis=1)
    groups = [both[g : g + 8] for g in range(0, n, 8)]
    height = lax.broadcasted_iota(jnp.int32, (8, 2 * n), 0)
    for first in range(0, n, PANEL):
        columns = [
            [
                jnp.broadcast_to(group[:, n + first + t : n + first + t + 1], (8, 2 * n))
                for group in groups
            ]
            for t in range(PANEL)
        ]
        for t in range(PANEL):
            k = first + t
            gk, sk = k // 8, k % 8
            pivot = columns[t][gk][sk : sk + 1]
            inverse = 1.0 / pivot
            root = lax.rsqrt(pivot)
            source = groups[gk][sk : sk + 1]
            steps = {}
            for g in range(gk, len(groups)):
                m = columns[t][g] * inverse
                steps[g] = jnp.where(height > sk, m, 0.0) if g == gk else m
            for u in range(t + 1, PANEL):
                head = columns[u][gk][sk : sk + 1]
                for g in range(gk, len(groups)):
                    columns[u][g] = columns[u][g] - steps[g] * head
            for g in range(gk, len(groups)):
                groups[g] = groups[g] - steps[g] * source
            groups[gk] = jnp.where(height == sk, groups[gk] * root, groups[gk])
    return jnp.concatenate(groups, axis=0)[:, :n]


def factor_kernel(total, mine, others, out):
    block_rows = mine.shape[0] - 1
    columns = mine.shape[1]
    gram = mine[block_rows] + others[block_rows]
    out[...] = inverse_factor(gram[:, :columns] / total)


def gram_kernel(parts, inverse, tiles, *refs):
    images, (image, out) = refs[:parts], refs[parts:]
    block_rows, columns, size = tiles.shape
    lower = split(inverse[...])
    new = [tree([part[i] for part in images]) for i in range(block_rows)]
    value = product(lower, joined([split(new[i]) for i in range(block_rows)], 1))
    prior = product(lower, joined([split(tiles[i]) for i in range(block_rows)], 1))
    for i in range(block_rows):
        image[i] = value[:, i * size : (i + 1) * size]
    value = split(value)
    out[:, :columns] = product(value, value, 1)
    out[:, columns:] = product(split(prior), value, 1)


def last_kernel(rows, total, image, *refs):
    parts, (basis, ritz) = refs[:rows], refs[rows:]
    both = tree([part[...] for part in parts]) / total
    columns = both.shape[0]
    ritz[...] = both[:, columns:]
    lower = split(inverse_factor(both[:, :columns]))
    basis[...] = product(lower, joined([split(image[i]) for i in range(image.shape[0])], 1))


def body(blocks, partner_ids, counts, start):
    block_rows, slots, size, _ = blocks.shape
    columns = start.shape[1]
    rows, parts = lax.axis_size("row"), lax.axis_size("nbr")
    half = rows // 2
    all_blocks = block_rows * rows
    total = float(all_blocks * size)
    shape = jax.ShapeDtypeStruct
    tile = shape((block_rows, columns, size), F32)
    longer = shape((block_rows + 1, columns, size), F32)
    shorter = shape((block_rows, columns // 2, size), F32)
    shorter_longer = shape((block_rows + 1, columns // 2, size), F32)
    wide = shape((columns, size), F32)
    work = pltpu.VMEM((all_blocks, columns, size), F32)

    def spec_of(out):
        return SMEM if out.dtype == jnp.int32 else VMEM

    def call(kernel, name, specs, outs, scratch=()):
        return pl.pallas_call(
            kernel,
            name=name,
            in_specs=specs,
            out_specs=[spec_of(out) for out in outs],
            out_shape=outs,
            scratch_shapes=scratch,
            compiler_params=PARAMS,
        )

    def round_over_rows(messages, shared):
        return [swap_rows(m, k, k + half) for k, m in enumerate(messages, 1)], swap(shared, "row", half)

    def sum_over_parts(image):
        return [image] + [swap(image, "nbr", s) for s in range(1, parts)]

    other = swap(blocks, "nbr", 1)
    other_ids = swap(partner_ids, "nbr", 1)
    table = pltpu.SMEM(partner_ids.shape, jnp.int32)
    held, ids, counts, tiles = call(
        load_kernel,
        "load",
        [HBM] * 4,
        [shape(blocks.shape, F32), table, pltpu.SMEM(counts.shape, jnp.int32), tile],
        [DMA((3 + block_rows,))],
    )(*[pltpu.with_memory_space_constraint(x, pltpu.HBM) for x in (blocks, partner_ids, counts, start.T)])
    *messages, shared, own, other_ids = call(
        functools.partial(first_kernel, rows),
        "first_transposed",
        [VMEM, VMEM, SMEM, VMEM, SMEM, VMEM],
        [tile] * (half - 1) + [shorter, tile, table],
        [work, DMA((1,))],
    )(held, other, ids, other_ids, counts, tiles)
    stored = (held, other, ids, other_ids, counts)
    index = [VMEM, VMEM, SMEM, SMEM, SMEM]
    received, shared = round_over_rows(messages, shared)
    (image,) = call(
        functools.partial(direct_kernel, rows, False), "first_direct", index + [VMEM] * (half + 2), [tile], [work]
    )(*stored, own, tiles, *received, shared)
    images = sum_over_parts(image)
    *messages, shared, own, tiles, gram = call(
        functools.partial(second_kernel, rows, parts),
        "second_transposed",
        index + [VMEM] * parts,
        [longer] * (half - 1) + [shorter_longer, tile, tile, wide],
        [work],
    )(*stored, *images)
    received, shared = round_over_rows(messages, shared)
    image, mine = call(
        functools.partial(direct_kernel, rows, True),
        "second_direct",
        index + [VMEM] * (half + 3),
        [tile, longer],
        [work],
    )(*stored, own, tiles, *received, shared, gram)
    pair = swap(mine, "nbr", 1)
    images = [image, pair] + [swap(image, "nbr", s) for s in range(2, parts)]
    (inverse,) = call(
        functools.partial(factor_kernel, total), "factor", [VMEM] * 2, [shape((columns, columns), F32)]
    )(mine, pair)
    image, both = call(
        functools.partial(gram_kernel, parts),
        "gram",
        [VMEM] * (parts + 2),
        [tile, shape((columns, 2 * columns), F32)],
    )(inverse, tiles, *images)
    boths = [both] + [swap(both, "row", s) for s in range(1, rows)]
    basis, ritz = call(
        functools.partial(last_kernel, rows, total),
        "last",
        [VMEM] * (rows + 1),
        [shape(start.shape[::-1], F32), shape((columns, columns), F32)],
    )(image, *boths)
    return basis.T, ritz


def solution(mesh):
    return jax.shard_map(
        body,
        mesh=mesh,
        in_specs=(
            P(("dom", "row"), "nbr", None, None),
            P(("dom", "row"), "nbr"),
            P(("dom", "row")),
            P(("dom", "row"), None),
        ),
        out_specs=(P(("dom", "row"), None), P("dom", None)),
        check_vma=False,
    )
```

```python
import functools

import jax
import jax.numpy as jnp
from jax import lax
from jax.experimental import pallas as pl
from jax.experimental.pallas import tpu as pltpu
from jax.sharding import PartitionSpec as P

F32 = jnp.float32
BF16 = jnp.bfloat16
VMEM = pl.BlockSpec(memory_space=pltpu.VMEM)
SMEM = pl.BlockSpec(memory_space=pltpu.SMEM)
HBM = pl.BlockSpec(memory_space=pltpu.HBM)
DMA = pltpu.SemaphoreType.DMA
PANEL = 8
PARAMS = pltpu.CompilerParams(vmem_limit_bytes=8 * 2**20)


def tree(parts):
    while len(parts) > 1:
        parts = [parts[i] + parts[i + 1] for i in range(0, len(parts), 2)]
    return parts[0]


def split(x):
    high = x.astype(BF16)
    rest = x - high.astype(F32)
    middle = rest.astype(BF16)
    return high, middle, (rest - middle.astype(F32)).astype(BF16)


def product(a_parts, b_parts, contract=0):
    n = a_parts[0].shape[0]

    def dot(a, b):
        return lax.dot_general(a, b, (((1,), (contract,)), ((), ())), preferred_element_type=F32)

    stacked = jnp.concatenate(a_parts, axis=0)
    high = dot(stacked, b_parts[0])
    middle = dot(stacked[: 2 * n], b_parts[1])
    low = dot(a_parts[0], b_parts[2])
    return high[:n] + ((high[n : 2 * n] + middle[:n]) + ((high[2 * n :] + middle[n:]) + low))


def joined(parts, axis):
    return [jnp.concatenate(level, axis=axis) for level in zip(*parts)]


def swap(x, axis, distance):
    return lax.ppermute(x, axis, [(i, i ^ distance) for i in range(lax.axis_size(axis))])


def swap_rows(x, even, odd):
    rows, parts = lax.axis_size("row"), lax.axis_size("nbr")
    pairs = [
        (r * parts + n, (r ^ (odd if n % 2 else even)) * parts + n) for r in range(rows) for n in range(parts)
    ]
    return lax.ppermute(x, ("row", "nbr"), pairs)


class Place:
    def __init__(self, rows, block_rows, slots):
        self.row = lax.axis_index("row")
        self.part = lax.axis_index("nbr")
        self.odd = self.part & 1
        self.block_rows, self.slots = block_rows, slots
        self.first_row = self.row * block_rows
        self.peers = [self.row ^ (k + self.odd) for k in range(2, rows, 2)]
        self.middle = self.row ^ 1

    def weight(self, ids, counts, member, i, p):
        slot = (self.part ^ member) * self.slots + p
        used = slot < counts[i]
        return jnp.where(used, jnp.where(ids[i, p] == self.first_row + i, 0.5, 1.0), 0.0).astype(F32)


def transposed_products(place, blocks, ids, counts, tiles, out, copy=None):
    out[...] = jnp.zeros_like(out)
    size = out.shape[2]
    values = []
    for i in range(place.block_rows):
        stored = [split(b[i, p]) for b in blocks for p in range(place.slots)]
        values.append(product(split(tiles[i]), joined(stored, 1)))
    if copy is not None:
        copy.wait()
    for i, value in enumerate(values):
        for m in range(len(blocks)):
            for p in range(place.slots):
                at = (m * place.slots + p) * size
                out[ids[m][i, p]] += value[:, at : at + size] * place.weight(ids[m], counts, m, i, p)


def direct_products(place, blocks, ids, counts, whole, i):
    stored, far = [], []
    for m, b in enumerate(blocks):
        for p in range(place.slots):
            stored.append(split(b[i, p].T))
            far.append(split(whole[ids[m][i, p]] * place.weight(ids[m], counts, m, i, p)))
    return product(joined(far, 1), joined(stored, 0))


def fill(place, messages, shared, products, tiles):
    n = place.block_rows
    for peer, out in zip(place.peers, messages):
        for i in range(n):
            out[i] = jnp.where(place.row < peer, products[peer * n + i], tiles[i])
    height = shared.shape[1]
    columns = pl.ds(place.odd * height, height)
    for i in range(n):
        shared[i] = jnp.where(
            place.row < place.middle, products[place.middle * n + i, columns], tiles[i, columns]
        )


def own_products(place, products, own):
    mine = products[pl.ds(place.first_row, place.block_rows)]
    own[...] = jnp.where(place.odd == 0, mine, 0.0)


def load_kernel(blocks, ids, counts, start, held, ids_s, counts_s, tiles, sems):
    size = blocks.shape[2]
    copies = [
        pltpu.make_async_copy(blocks, held, sems.at[0]),
        pltpu.make_async_copy(ids, ids_s, sems.at[1]),
        pltpu.make_async_copy(counts, counts_s, sems.at[2]),
    ]
    for i in range(blocks.shape[0]):
        copies.append(pltpu.make_async_copy(start.at[:, i * size : (i + 1) * size], tiles.at[i], sems.at[3 + i]))
    for copy in copies:
        copy.start()
    for copy in copies:
        copy.wait()


def first_kernel(rows, held, other, ids, other_ids, counts, tiles, *refs):
    half = rows // 2
    messages, refs = refs[: half - 1], refs[half - 1 :]
    shared, own, other_s, products, sem = refs
    block_rows, slots, size, _ = held.shape
    place = Place(rows, block_rows, slots)
    copy = pltpu.make_async_copy(other_ids, other_s, sem.at[0])
    copy.start()
    transposed_products(place, (held, other), (ids, other_s), counts, tiles, products, copy)
    fill(place, messages, shared, products, tiles)
    own_products(place, products, own)


def direct_kernel(rows, with_gram, held, other, ids, other_ids, counts, own, tiles, *refs):
    half = rows // 2
    received, shared, refs = refs[: half - 1], refs[half - 1], refs[half:]
    if with_gram:
        gram, out, longer, whole = refs
    else:
        out, whole = refs
    block_rows, slots, size, _ = held.shape
    place = Place(rows, block_rows, slots)
    whole[...] = jnp.zeros_like(whole)
    whole[pl.ds(place.first_row, block_rows)] = jnp.where(place.odd == 0, tiles[...], 0.0)
    for peer, message in zip(place.peers, received):
        whole[pl.ds(peer * block_rows, block_rows)] = message[:block_rows]
    height = shared.shape[1]
    columns = pl.ds(place.odd * height, height)
    for i in range(block_rows):
        whole[place.middle * block_rows + i, columns] = shared[i]
    for i in range(block_rows):
        value = own[i]
        for peer, message in zip(place.peers, received):
            value += jnp.where(place.row > peer, message[i], 0.0)
        out[i] = value + direct_products(place, (held, other), (ids, other_ids), counts, whole, i)
        out[i, columns] += jnp.where(place.row > place.middle, shared[i], 0.0)
    if with_gram:
        for i in range(block_rows):
            longer[i] = out[i]
        n = 2 * height
        packed = shared[block_rows]
        middle = jnp.concatenate([packed[:, :n], packed[:, n : 2 * n]], axis=0)
        first = jnp.where(place.odd == 0, gram[:, :n], middle)
        longer[block_rows] = jnp.zeros_like(longer[block_rows])
        longer[block_rows, :, :n] = tree([first] + [message[block_rows][:, :n] for message in received])


def second_kernel(rows, parts, held, other, ids, other_ids, counts, *refs):
    images, refs = refs[:parts], refs[parts:]
    half = rows // 2
    messages, refs = refs[: half - 1], refs[half - 1 :]
    shared, own, tiles, gram, products = refs
    block_rows, slots, size, _ = held.shape
    place = Place(rows, block_rows, slots)
    for i in range(block_rows):
        tiles[i] = tree([image[i] for image in images])
    transposed_products(place, (held, other), (ids, other_ids), counts, tiles, products)
    fill(place, messages, shared, products, tiles)
    own_products(place, products, own)
    whole = joined([split(tiles[i]) for i in range(block_rows)], 1)
    partial = product(whole, whole, 1)
    gram[...] = jnp.zeros_like(gram)
    gram[:, : partial.shape[0]] = partial
    for message in messages:
        message[block_rows] = gram[...]
    height = shared.shape[1]
    shared[block_rows] = jnp.zeros_like(shared[block_rows])
    shared[block_rows, :, : 4 * height] = jnp.concatenate([partial[:height], partial[height:]], axis=1)


def inverse_factor(gram):
    n = gram.shape[0]
    rows = lax.broadcasted_iota(jnp.int32, (n, 2 * n), 0)
    lanes = lax.broadcasted_iota(jnp.int32, (n, 2 * n), 1)
    both = jnp.concatenate([jnp.where(rows == lanes, 1.0, 0.0)[:, :n], gram], axis=1)
    groups = [both[g : g + 8] for g in range(0, n, 8)]
    height = lax.broadcasted_iota(jnp.int32, (8, 2 * n), 0)
    for first in range(0, n, PANEL):
        columns = [
            [
                jnp.broadcast_to(group[:, n + first + t : n + first + t + 1], (8, 2 * n))
                for group in groups
            ]
            for t in range(PANEL)
        ]
        for t in range(PANEL):
            k = first + t
            gk, sk = k // 8, k % 8
            pivot = columns[t][gk][sk : sk + 1]
            inverse = 1.0 / pivot
            root = lax.rsqrt(pivot)
            source = groups[gk][sk : sk + 1]
            steps = {}
            for g in range(gk, len(groups)):
                m = columns[t][g] * inverse
                steps[g] = jnp.where(height > sk, m, 0.0) if g == gk else m
            for u in range(t + 1, PANEL):
                head = columns[u][gk][sk : sk + 1]
                for g in range(gk, len(groups)):
                    columns[u][g] = columns[u][g] - steps[g] * head
            for g in range(gk, len(groups)):
                groups[g] = groups[g] - steps[g] * source
            groups[gk] = jnp.where(height == sk, groups[gk] * root, groups[gk])
    return jnp.concatenate(groups, axis=0)[:, :n]


def factor_kernel(total, mine, others, out):
    block_rows = mine.shape[0] - 1
    columns = mine.shape[1]
    gram = mine[block_rows] + others[block_rows]
    out[...] = inverse_factor(gram[:, :columns] / total)


def gram_kernel(parts, inverse, tiles, *refs):
    images, (image, out) = refs[:parts], refs[parts:]
    block_rows, columns, size = tiles.shape
    lower = split(inverse[...])
    new = [tree([part[i] for part in images]) for i in range(block_rows)]
    value = product(lower, joined([split(new[i]) for i in range(block_rows)], 1))
    prior = product(lower, joined([split(tiles[i]) for i in range(block_rows)], 1))
    for i in range(block_rows):
        image[i] = value[:, i * size : (i + 1) * size]
    value = split(value)
    out[:, :columns] = product(value, value, 1)
    out[:, columns:] = product(split(prior), value, 1)


def half_sum_kernel(mine, shared, *refs):
    received, out = refs[:-1], refs[-1]
    first = jnp.where((lax.axis_index("nbr") & 1) == 0, mine[...], shared[...])
    out[...] = tree([first] + [part[...] for part in received])


def last_kernel(total, image, mine, others, basis, ritz):
    both = (mine[...] + others[...]) / total
    columns = both.shape[0]
    ritz[...] = both[:, columns:]
    lower = split(inverse_factor(both[:, :columns]))
    basis[...] = product(lower, joined([split(image[i]) for i in range(image.shape[0])], 1))


def body(blocks, partner_ids, counts, start):
    block_rows, slots, size, _ = blocks.shape
    columns = start.shape[1]
    rows, parts = lax.axis_size("row"), lax.axis_size("nbr")
    half = rows // 2
    all_blocks = block_rows * rows
    total = float(all_blocks * size)
    shape = jax.ShapeDtypeStruct
    tile = shape((block_rows, columns, size), F32)
    longer = shape((block_rows + 1, columns, size), F32)
    shorter = shape((block_rows, columns // 2, size), F32)
    shorter_longer = shape((block_rows + 1, columns // 2, size), F32)
    wide = shape((columns, size), F32)
    work = pltpu.VMEM((all_blocks, columns, size), F32)

    def spec_of(out):
        return SMEM if out.dtype == jnp.int32 else VMEM

    def call(kernel, name, specs, outs, scratch=()):
        return pl.pallas_call(
            kernel,
            name=name,
            in_specs=specs,
            out_specs=[spec_of(out) for out in outs],
            out_shape=outs,
            scratch_shapes=scratch,
            compiler_params=PARAMS,
        )

    def round_over_rows(messages, shared):
        return [swap_rows(m, 2 * k, 2 * k + 1) for k, m in enumerate(messages, 1)], swap(shared, "row", 1)

    def sum_over_parts(image):
        return [image] + [swap(image, "nbr", s) for s in range(1, parts)]

    other = swap(blocks, "nbr", 1)
    other_ids = swap(partner_ids, "nbr", 1)
    table = pltpu.SMEM(partner_ids.shape, jnp.int32)
    held, ids, counts, tiles = call(
        load_kernel,
        "load",
        [HBM] * 4,
        [shape(blocks.shape, F32), table, pltpu.SMEM(counts.shape, jnp.int32), tile],
        [DMA((3 + block_rows,))],
    )(*[pltpu.with_memory_space_constraint(x, pltpu.HBM) for x in (blocks, partner_ids, counts, start.T)])
    *messages, shared, own, other_ids = call(
        functools.partial(first_kernel, rows),
        "first_transposed",
        [VMEM, VMEM, SMEM, VMEM, SMEM, VMEM],
        [tile] * (half - 1) + [shorter, tile, table],
        [work, DMA((1,))],
    )(held, other, ids, other_ids, counts, tiles)
    stored = (held, other, ids, other_ids, counts)
    index = [VMEM, VMEM, SMEM, SMEM, SMEM]
    received, shared = round_over_rows(messages, shared)
    (image,) = call(
        functools.partial(direct_kernel, rows, False), "first_direct", index + [VMEM] * (half + 2), [tile], [work]
    )(*stored, own, tiles, *received, shared)
    images = sum_over_parts(image)
    *messages, shared, own, tiles, gram = call(
        functools.partial(second_kernel, rows, parts),
        "second_transposed",
        index + [VMEM] * parts,
        [longer] * (half - 1) + [shorter_longer, tile, tile, wide],
        [work],
    )(*stored, *images)
    received, shared = round_over_rows(messages, shared)
    image, mine = call(
        functools.partial(direct_kernel, rows, True),
        "second_direct",
        index + [VMEM] * (half + 3),
        [tile, longer],
        [work],
    )(*stored, own, tiles, *received, shared, gram)
    pair = swap(mine, "nbr", 1)
    images = [image, pair] + [swap(image, "nbr", s) for s in range(2, parts)]
    (inverse,) = call(
        functools.partial(factor_kernel, total), "factor", [VMEM] * 2, [shape((columns, columns), F32)]
    )(mine, pair)
    image, both = call(
        functools.partial(gram_kernel, parts),
        "gram",
        [VMEM] * (parts + 2),
        [tile, shape((columns, 2 * columns), F32)],
    )(inverse, tiles, *images)
    received, shared = round_over_rows([both] * (half - 1), both)
    (both,) = call(
        half_sum_kernel, "half_sum", [VMEM] * (half + 1), [shape((columns, 2 * columns), F32)]
    )(both, shared, *received)
    basis, ritz = call(
        functools.partial(last_kernel, total),
        "last",
        [VMEM] * 3,
        [shape(start.shape[::-1], F32), shape((columns, columns), F32)],
    )(image, both, swap(both, "nbr", 1))
    return basis.T, ritz


def solution(mesh):
    return jax.shard_map(
        body,
        mesh=mesh,
        in_specs=(
            P(("dom", "row"), "nbr", None, None),
            P(("dom", "row"), "nbr"),
            P(("dom", "row")),
            P(("dom", "row"), None),
        ),
        out_specs=(P(("dom", "row"), None), P("dom", None)),
        check_vma=False,
    )
```

```python
import functools

import jax
import jax.numpy as jnp
from jax import lax
from jax.experimental import pallas as pl
from jax.experimental.pallas import tpu as pltpu
from jax.sharding import PartitionSpec as P

F32 = jnp.float32
BF16 = jnp.bfloat16
VMEM = pl.BlockSpec(memory_space=pltpu.VMEM)
SMEM = pl.BlockSpec(memory_space=pltpu.SMEM)
HBM = pl.BlockSpec(memory_space=pltpu.HBM)
DMA = pltpu.SemaphoreType.DMA
PARAMS = pltpu.CompilerParams(vmem_limit_bytes=8 * 2**20)
PANEL = 16


def tree(parts):
    while len(parts) > 1:
        parts = [parts[i] + parts[i + 1] for i in range(0, len(parts), 2)]
    return parts[0]


def split(x):
    high = x.astype(BF16)
    rest = x - high.astype(F32)
    middle = rest.astype(BF16)
    return high, middle, (rest - middle.astype(F32)).astype(BF16)


def product(a_parts, b_parts, contract=0):
    n = a_parts[0].shape[0]

    def dot(a, b):
        return lax.dot_general(a, b, (((1,), (contract,)), ((), ())), preferred_element_type=F32)

    stacked = jnp.concatenate(a_parts, axis=0)
    high = dot(stacked, b_parts[0])
    middle = dot(stacked[: 2 * n], b_parts[1])
    low = dot(a_parts[0], b_parts[2])
    return high[:n] + ((high[n : 2 * n] + middle[:n]) + ((high[2 * n :] + middle[n:]) + low))


def joined(parts, axis):
    return [jnp.concatenate(level, axis=axis) for level in zip(*parts)]


def folded(x, lanes):
    fold = lanes // x.shape[1]
    height = x.shape[0] // fold
    return jnp.concatenate([x[g * height : (g + 1) * height] for g in range(fold)], axis=1)


def unfolded(x, columns):
    return jnp.concatenate([x[:, g : g + columns] for g in range(0, x.shape[1], columns)], axis=0)


def swap(x, axis, distance):
    return lax.ppermute(x, axis, [(i, i ^ distance) for i in range(lax.axis_size(axis))])


def swap_rows(x, even, odd):
    rows, parts = lax.axis_size("row"), lax.axis_size("nbr")
    pairs = [
        (r * parts + n, (r ^ (odd if n % 2 else even)) * parts + n) for r in range(rows) for n in range(parts)
    ]
    return lax.ppermute(x, ("row", "nbr"), pairs)


class Place:
    def __init__(self, rows, blocks, columns):
        self.row = lax.axis_index("row")
        self.part = lax.axis_index("nbr")
        self.odd = self.part & 1
        self.block_rows, self.slots = blocks.shape[:2]
        self.first_row = self.row * self.block_rows
        self.peers = [self.row ^ (k + self.odd) for k in range(2, rows, 2)]
        self.middle = self.row ^ 1
        self.columns = columns
        self.height = columns // 2
        self.half = pl.ds(pl.multiple_of(self.odd * self.height, self.height), self.height)

    def weight(self, ids, counts, member, i, p):
        used = (self.part ^ member) * self.slots + p < counts[i]
        return jnp.where(used, jnp.where(ids[i, p] == self.first_row + i, 0.5, 1.0), 0.0).astype(F32)

    def tile(self, i):
        return slice(i * self.columns, (i + 1) * self.columns)

    def half_tile(self, i):
        return slice(i * self.height, (i + 1) * self.height)


def transposed_products(place, blocks, ids, counts, tiles, out, copies=()):
    out[...] = jnp.zeros_like(out)
    size = out.shape[2]
    values = []
    for i in range(place.block_rows):
        stored = [split(b[i, p]) for b in blocks for p in range(place.slots)]
        values.append(product(split(tiles[place.tile(i)]), joined(stored, 1)))
    for copy in copies:
        copy.wait()
    for i, value in enumerate(values):
        for m in range(len(blocks)):
            for p in range(place.slots):
                at = (m * place.slots + p) * size
                out[ids[m][i, p]] += value[:, at : at + size] * place.weight(ids[m], counts, m, i, p)


def direct_products(place, blocks, ids, counts, whole, i):
    stored, far = [], []
    for m, b in enumerate(blocks):
        for p in range(place.slots):
            stored.append(split(b[i, p].T))
            far.append(split(whole[ids[m][i, p]] * place.weight(ids[m], counts, m, i, p)))
    return product(joined(far, 1), joined(stored, 0))


def fill(place, messages, shared, products, tiles, own):
    n = place.block_rows
    for i in range(n):
        tile = tiles[place.tile(i)]
        for peer, out in zip(place.peers, messages):
            out[place.tile(i)] = jnp.where(place.row < peer, products[peer * n + i], tile)
        shared[place.half_tile(i)] = jnp.where(
            place.row < place.middle,
            products[place.middle * n + i, place.half],
            tiles[pl.ds(pl.multiple_of(i * place.columns + place.odd * place.height, 8), place.height)],
        )
        own[place.tile(i)] = jnp.where(place.odd == 0, products[place.first_row + i], 0.0)


def load_kernel(blocks, ids, counts, start, held, ids_s, counts_s, tiles, sems):
    size, columns = blocks.shape[2], start.shape[0]
    copies = [
        pltpu.make_async_copy(blocks, held, sems.at[0]),
        pltpu.make_async_copy(ids, ids_s, sems.at[1]),
        pltpu.make_async_copy(counts, counts_s, sems.at[2]),
    ]
    for i in range(blocks.shape[0]):
        source = start.at[:, i * size : (i + 1) * size]
        copies.append(pltpu.make_async_copy(source, tiles.at[i * columns : (i + 1) * columns], sems.at[3 + i]))
    for copy in copies:
        copy.start()
    for copy in copies:
        copy.wait()


def first_kernel(rows, held, other, ids, other_ids, counts, tiles, *refs):
    messages, refs = refs[: rows // 2 - 1], refs[rows // 2 - 1 :]
    shared, own, other_s, products, sem = refs
    place = Place(rows, held, products.shape[1])
    copy = pltpu.make_async_copy(other_ids, other_s, sem.at[0])
    copy.start()
    transposed_products(place, (held, other), (ids, other_s), counts, tiles, products, [copy])
    fill(place, messages, shared, products, tiles, own)


def direct_kernel(rows, held, other, ids, other_ids, counts, own, tiles, *refs):
    received, refs = refs[: rows // 2 - 1], refs[rows // 2 - 1 :]
    shared, *gram, out, whole = refs
    n, columns, size = held.shape[0], whole.shape[1], whole.shape[2]
    place = Place(rows, held, columns)
    whole[...] = jnp.zeros_like(whole)
    for i in range(n):
        whole[place.first_row + i] = jnp.where(place.odd == 0, tiles[place.tile(i)], 0.0)
        for peer, message in zip(place.peers, received):
            whole[peer * n + i] = message[place.tile(i)]
        whole[place.middle * n + i, place.half] = shared[place.half_tile(i)]
    for i in range(n):
        value = own[place.tile(i)]
        for peer, message in zip(place.peers, received):
            value += jnp.where(place.row > peer, message[place.tile(i)], 0.0)
        out[place.tile(i)] = value + direct_products(place, (held, other), (ids, other_ids), counts, whole, i)
        mine = pl.ds(pl.multiple_of(i * columns + place.odd * place.height, 8), place.height)
        out[mine] += jnp.where(place.row > place.middle, shared[place.half_tile(i)], 0.0)
    if gram:
        first = jnp.where(place.odd == 0, gram[0][...], shared[n * place.height :])
        out[n * columns :] = tree([first] + [message[n * columns :] for message in received])


def second_kernel(rows, parts, held, other, ids, other_ids, counts, *refs):
    images, refs = refs[:parts], refs[parts:]
    messages, refs = refs[: rows // 2 - 1], refs[rows // 2 - 1 :]
    shared, own, tiles, gram, products = refs
    n, columns, size = held.shape[0], products.shape[1], products.shape[2]
    place = Place(rows, held, columns)
    tiles[...] = tree([image[...] for image in images])
    transposed_products(place, (held, other), (ids, other_ids), counts, tiles, products)
    fill(place, messages, shared, products, tiles, own)
    whole = joined([split(tiles[place.tile(i)]) for i in range(n)], 1)
    packed = folded(product(whole, whole, 1), size)
    gram[...] = packed
    for message in messages:
        message[n * columns :] = packed
    shared[n * place.height :] = packed


def eliminated(gram, rest):
    n, width = gram.shape[0], rest.shape[1]
    groups = [[gram[g : g + 8], rest[g : g + 8]] for g in range(0, n, 8)]
    height = lax.broadcasted_iota(jnp.int32, (8, 1), 0)
    for first in range(0, n, PANEL):
        columns = [
            [jnp.broadcast_to(group[0][:, first + t : first + t + 1], (8, 128)) for group in groups]
            for t in range(PANEL)
        ]
        for t in range(PANEL):
            k = first + t
            gk, sk = k // 8, k % 8
            pivot = columns[t][gk][sk : sk + 1]
            inverse = 1.0 / pivot
            root = lax.rsqrt(pivot)
            source = [x[sk : sk + 1] for x in groups[gk]]
            steps = {}
            for g in range(gk, len(groups)):
                m = columns[t][g] * inverse
                steps[g] = jnp.where(height > sk, m, 0.0) if g == gk else m
            for u in range(t + 1, PANEL):
                head = columns[u][gk][sk : sk + 1]
                for g in range(gk, len(groups)):
                    columns[u][g] = columns[u][g] - steps[g] * head
            for g in range(gk, len(groups)):
                groups[g] = [x - wide(steps[g], x.shape[1]) * s for x, s in zip(groups[g], source)]
            groups[gk][1] = jnp.where(height == sk, groups[gk][1] * wide(root, width), groups[gk][1])
    return jnp.concatenate([group[1] for group in groups], axis=0)


def wide(x, lanes):
    if lanes <= x.shape[1]:
        return x[:, :lanes]
    return jnp.concatenate([x] * (lanes // x.shape[1]), axis=1)


def identity(n):
    rows = lax.broadcasted_iota(jnp.int32, (n, n), 0)
    return jnp.where(rows == lax.broadcasted_iota(jnp.int32, (n, n), 1), 1.0, 0.0)


def pair_kernel(mine, others, image, gram):
    tall = image.shape[0]
    image[...] = mine[:tall] + others[:tall]
    gram[...] = unfolded(mine[tall:] + others[tall:], gram.shape[0])


def factor_kernel(total, gram, tiles, inverse, prior):
    columns = gram.shape[0]
    lower = eliminated(gram[...] / total, identity(columns))
    inverse[...] = lower
    parts = [split(tiles[i : i + columns]) for i in range(0, tiles.shape[0], columns)]
    prior[...] = product(split(lower), joined(parts, 1))


def gram_kernel(inverse, prior, *refs):
    images, (image, out) = refs[:-2], refs[-2:]
    columns = inverse.shape[0]
    new = split(tree([part[...] for part in images]))
    rows = range(0, new[0].shape[0], columns)
    value = product(split(inverse[...]), [jnp.concatenate([x[i : i + columns] for i in rows], axis=1) for x in new])
    image[...] = value
    value = split(value)
    both = product(joined([value, split(prior[...])], 0), value, 1)
    out[...] = folded(both, out.shape[1])


def half_sum_kernel(mine, shared, *refs):
    received, out = refs[:-1], refs[-1]
    first = jnp.where((lax.axis_index("nbr") & 1) == 0, mine[...], shared[...])
    out[...] = tree([first] + [part[...] for part in received])


def last_kernel(total, image, mine, others, basis, ritz):
    columns = ritz.shape[0]
    both = unfolded((mine[...] + others[...]) / total, columns)
    ritz[...] = both[columns:]
    basis[...] = eliminated(both[:columns], image[...])


def body(blocks, partner_ids, counts, start):
    block_rows, slots, size, _ = blocks.shape
    columns = start.shape[1]
    rows, parts = lax.axis_size("row"), lax.axis_size("nbr")
    half = rows // 2
    all_blocks = block_rows * rows
    total = float(all_blocks * size)
    extra = columns * columns // size

    def flat(height):
        return jax.ShapeDtypeStruct((height, size), F32)

    tall = block_rows * columns
    tile, square = flat(tall), jax.ShapeDtypeStruct((columns, columns), F32)
    across = jax.ShapeDtypeStruct(start.shape[::-1], F32)
    table = pltpu.SMEM(partner_ids.shape, jnp.int32)
    work = pltpu.VMEM((all_blocks, columns, size), F32)

    def call(kernel, name, specs, outs, scratch=()):
        return pl.pallas_call(
            kernel,
            name=name,
            in_specs=specs,
            out_specs=[VMEM if isinstance(out, jax.ShapeDtypeStruct) else SMEM for out in outs],
            out_shape=outs,
            scratch_shapes=scratch,
            compiler_params=PARAMS,
        )

    def round_over_rows(messages, shared):
        return [swap_rows(m, 2 * k, 2 * k + 1) for k, m in enumerate(messages, 1)], swap(shared, "row", 1)

    def sum_over_pairs(image):
        return [image] + [swap(image, "nbr", s) for s in range(2, parts, 2)]

    other = swap(blocks, "nbr", 1)
    other_ids = swap(partner_ids, "nbr", 1)
    held, ids, counts, tiles = call(
        load_kernel,
        "load",
        [HBM] * 4,
        [jax.ShapeDtypeStruct(blocks.shape, F32), table, pltpu.SMEM(counts.shape, jnp.int32), tile],
        [DMA((3 + block_rows,))],
    )(*[pltpu.with_memory_space_constraint(x, pltpu.HBM) for x in (blocks, partner_ids, counts, start.T)])
    *messages, shared, own, other_ids = call(
        functools.partial(first_kernel, rows),
        "first_transposed",
        [VMEM, VMEM, SMEM, VMEM, SMEM, VMEM],
        [tile] * (half - 1) + [flat(tall // 2), tile, table],
        [work, DMA((1,))],
    )(held, other, ids, other_ids, counts, tiles)
    stored = (held, other, ids, other_ids, counts)
    index = [VMEM, VMEM, SMEM, SMEM, SMEM]
    received, shared = round_over_rows(messages, shared)
    (image,) = call(
        functools.partial(direct_kernel, rows), "first_direct", index + [VMEM] * (half + 2), [tile], [work]
    )(*stored, own, tiles, *received, shared)
    images = sum_over_pairs(image + swap(image, "nbr", 1))
    *messages, shared, own, tiles, gram = call(
        functools.partial(second_kernel, rows, parts // 2),
        "second_transposed",
        index + [VMEM] * (parts // 2),
        [flat(tall + extra)] * (half - 1) + [flat(tall // 2 + extra), tile, tile, flat(extra)],
        [work],
    )(*stored, *images)
    received, shared = round_over_rows(messages, shared)
    (mine,) = call(
        functools.partial(direct_kernel, rows),
        "second_direct",
        index + [VMEM] * (half + 3),
        [flat(tall + extra)],
        [work],
    )(*stored, own, tiles, *received, shared, gram)
    image, gram = call(pair_kernel, "pair", [VMEM] * 2, [tile, square])(mine, swap(mine, "nbr", 1))
    images = sum_over_pairs(image)
    inverse, prior = call(functools.partial(factor_kernel, total), "factor", [VMEM] * 2, [square, across])(gram, tiles)
    image, both = call(gram_kernel, "gram", [VMEM] * (parts // 2 + 2), [across, flat(2 * extra)])(
        inverse, prior, *images
    )
    received, shared = round_over_rows([both] * (half - 1), both)
    (both,) = call(half_sum_kernel, "half_sum", [VMEM] * (half + 1), [flat(2 * extra)])(both, shared, *received)
    basis, ritz = call(functools.partial(last_kernel, total), "last", [VMEM] * 3, [across, square])(
        image, both, swap(both, "nbr", 1)
    )
    return basis.T, ritz


def solution(mesh):
    return jax.shard_map(
        body,
        mesh=mesh,
        in_specs=(
            P(("dom", "row"), "nbr", None, None),
            P(("dom", "row"), "nbr"),
            P(("dom", "row")),
            P(("dom", "row"), None),
        ),
        out_specs=(P(("dom", "row"), None), P("dom", None)),
        check_vma=False,
    )
```

```python
import functools

import jax
import jax.numpy as jnp
from jax import lax
from jax.experimental import pallas as pl
from jax.experimental.pallas import tpu as pltpu
from jax.sharding import PartitionSpec as P

F32 = jnp.float32
BF16 = jnp.bfloat16
VMEM = pl.BlockSpec(memory_space=pltpu.VMEM)
SMEM = pl.BlockSpec(memory_space=pltpu.SMEM)
HBM = pl.BlockSpec(memory_space=pltpu.HBM)
DMA = pltpu.SemaphoreType.DMA
PARAMS = pltpu.CompilerParams(vmem_limit_bytes=8 * 2**20)
PANEL = 16


def tree(parts):
    while len(parts) > 1:
        parts = [parts[i] + parts[i + 1] for i in range(0, len(parts), 2)]
    return parts[0]


def split(x):
    high = x.astype(BF16)
    rest = x - high.astype(F32)
    middle = rest.astype(BF16)
    return high, middle, (rest - middle.astype(F32)).astype(BF16)


def dot(a, b, contract=0):
    return lax.dot_general(a, b, (((1,), (contract,)), ((), ())), preferred_element_type=F32)


def product(a_parts, b_parts, contract=0):
    n = a_parts[0].shape[0]
    stacked = jnp.concatenate(a_parts, axis=0)
    high = dot(stacked, b_parts[0], contract)
    middle = dot(stacked[: 2 * n], b_parts[1], contract)
    low = dot(a_parts[0], b_parts[2], contract)
    return high[:n] + ((high[n : 2 * n] + middle[:n]) + ((high[2 * n :] + middle[n:]) + low))


def shallow_product(a_parts, b_parts):
    n = a_parts[0].shape[0]
    stacked = jnp.concatenate(a_parts, axis=0)
    most = dot(jnp.concatenate([stacked, stacked], axis=1), jnp.concatenate(b_parts[:2], axis=0))
    low = dot(a_parts[0], b_parts[2])
    return most[:n] + (most[n : 2 * n] + (most[2 * n :] + low))


def narrow_product(a_parts, b_pair, b_low):
    n, width = a_parts[0].shape[0], b_low.shape[1]
    most = dot(jnp.concatenate(a_parts, axis=0), b_pair)
    high, middle = most[:, :width], most[:, width:]
    low = dot(a_parts[0], b_low)
    return high[:n] + ((high[n : 2 * n] + middle[:n]) + ((high[2 * n :] + middle[n : 2 * n]) + low))


def joined(parts, axis):
    return [jnp.concatenate(level, axis=axis) for level in zip(*parts)]


def folded(x, lanes):
    fold = lanes // x.shape[1]
    height = x.shape[0] // fold
    return jnp.concatenate([x[g * height : (g + 1) * height] for g in range(fold)], axis=1)


def unfolded(x, columns):
    return jnp.concatenate([x[:, g : g + columns] for g in range(0, x.shape[1], columns)], axis=0)


def swap(x, axis, distance):
    return lax.ppermute(x, axis, [(i, i ^ distance) for i in range(lax.axis_size(axis))])


def swap_rows(x, even, odd):
    rows, parts = lax.axis_size("row"), lax.axis_size("nbr")
    pairs = [
        (r * parts + n, (r ^ (odd if n % 2 else even)) * parts + n) for r in range(rows) for n in range(parts)
    ]
    return lax.ppermute(x, ("row", "nbr"), pairs)


class Place:
    def __init__(self, rows, block_rows, slots, columns):
        self.row = lax.axis_index("row")
        self.part = lax.axis_index("nbr")
        self.odd = self.part & 1
        self.block_rows, self.slots = block_rows, slots
        self.first_row = self.row * self.block_rows
        self.peers = [self.row ^ (k + self.odd) for k in range(2, rows, 2)]
        self.middle = self.row ^ 1
        self.columns = columns
        self.height = columns // 2
        self.half = pl.ds(pl.multiple_of(self.odd * self.height, self.height), self.height)

    def weight(self, ids, counts, member, i, p):
        used = (self.part ^ member) * self.slots + p < counts[i]
        return jnp.where(used, jnp.where(ids[i, p] == self.first_row + i, 0.5, 1.0), 0.0).astype(F32)

    def tile(self, i):
        return slice(i * self.columns, (i + 1) * self.columns)

    def half_tile(self, i):
        return slice(i * self.height, (i + 1) * self.height)


def transposed_products(place, blocks, ids, counts, tiles, out, copies=()):
    out[...] = jnp.zeros_like(out)
    size = out.shape[2]
    values = []
    for i in range(place.block_rows):
        stored = [split(b[i, p]) for b in blocks for p in range(place.slots)]
        values.append(shallow_product(split(tiles[place.tile(i)]), joined(stored, 1)))
    for copy in copies:
        copy.wait()
    for i, value in enumerate(values):
        for m in range(len(blocks)):
            for p in range(place.slots):
                at = (m * place.slots + p) * size
                out[ids[m][i, p]] += value[:, at : at + size] * place.weight(ids[m], counts, m, i, p)


def direct_products(place, pair, low, ids, counts, whole, i):
    far = []
    for m in range(len(ids)):
        for p in range(place.slots):
            far.append(split(whole[ids[m][i, p]] * place.weight(ids[m], counts, m, i, p)))
    at = slice(i * len(far) * pair.shape[1] // 2, (i + 1) * len(far) * pair.shape[1] // 2)
    return narrow_product(joined(far, 1), pair[at], low[at])


def fill(place, messages, shared, products, tiles, own):
    n = place.block_rows
    for i in range(n):
        tile = tiles[place.tile(i)]
        for peer, out in zip(place.peers, messages):
            out[place.tile(i)] = jnp.where(place.row < peer, products[peer * n + i], tile)
        shared[place.half_tile(i)] = jnp.where(
            place.row < place.middle,
            products[place.middle * n + i, place.half],
            tiles[pl.ds(pl.multiple_of(i * place.columns + place.odd * place.height, 8), place.height)],
        )
        own[place.tile(i)] = jnp.where(place.odd == 0, products[place.first_row + i], 0.0)


def load_kernel(blocks, ids, counts, start, held, ids_s, counts_s, tiles, sems):
    size, columns = blocks.shape[2], start.shape[0]
    copies = [
        pltpu.make_async_copy(blocks, held, sems.at[0]),
        pltpu.make_async_copy(ids, ids_s, sems.at[1]),
        pltpu.make_async_copy(counts, counts_s, sems.at[2]),
    ]
    for i in range(blocks.shape[0]):
        source = start.at[:, i * size : (i + 1) * size]
        copies.append(pltpu.make_async_copy(source, tiles.at[i * columns : (i + 1) * columns], sems.at[3 + i]))
    for copy in copies:
        copy.start()
    for copy in copies:
        copy.wait()


def first_kernel(rows, held, other, ids, other_ids, counts, tiles, *refs):
    messages, refs = refs[: rows // 2 - 1], refs[rows // 2 - 1 :]
    shared, own, other_s, products, sem = refs
    place = Place(rows, *held.shape[:2], products.shape[1])
    copy = pltpu.make_async_copy(other_ids, other_s, sem.at[0])
    copy.start()
    transposed_products(place, (held, other), (ids, other_s), counts, tiles, products, [copy])
    fill(place, messages, shared, products, tiles, own)


def split_kernel(held, other, after, pair, low):
    block_rows, slots, size, _ = held.shape
    at = 0
    for i in range(block_rows):
        for b in (held, other):
            for p in range(slots):
                high, middle, rest = split(b[i, p].T)
                pair[at : at + size, :size] = high
                pair[at : at + size, size:] = middle
                low[at : at + size] = rest
                at += size


def direct_kernel(rows, block_rows, slots, pair, low, ids, other_ids, counts, own, tiles, *refs):
    received, refs = refs[: rows // 2 - 1], refs[rows // 2 - 1 :]
    shared, *gram, out, whole = refs
    n, columns = block_rows, whole.shape[1]
    place = Place(rows, block_rows, slots, columns)
    whole[...] = jnp.zeros_like(whole)
    for i in range(n):
        whole[place.first_row + i] = jnp.where(place.odd == 0, tiles[place.tile(i)], 0.0)
        for peer, message in zip(place.peers, received):
            whole[peer * n + i] = message[place.tile(i)]
        whole[place.middle * n + i, place.half] = shared[place.half_tile(i)]
    for i in range(n):
        value = own[place.tile(i)]
        for peer, message in zip(place.peers, received):
            value += jnp.where(place.row > peer, message[place.tile(i)], 0.0)
        out[place.tile(i)] = value + direct_products(
            place, pair, low, (ids, other_ids), counts, whole, i
        )
        mine = pl.ds(pl.multiple_of(i * columns + place.odd * place.height, 8), place.height)
        out[mine] += jnp.where(place.row > place.middle, shared[place.half_tile(i)], 0.0)
    if gram:
        first = jnp.where(place.odd == 0, gram[0][...], shared[n * place.height :])
        out[n * columns :] = tree([first] + [message[n * columns :] for message in received])


def second_kernel(rows, parts, held, other, ids, other_ids, counts, *refs):
    images, refs = refs[:parts], refs[parts:]
    messages, refs = refs[: rows // 2 - 1], refs[rows // 2 - 1 :]
    shared, own, tiles, gram, products = refs
    n, columns, size = held.shape[0], products.shape[1], products.shape[2]
    place = Place(rows, *held.shape[:2], columns)
    tiles[...] = tree([image[...] for image in images])
    transposed_products(place, (held, other), (ids, other_ids), counts, tiles, products)
    fill(place, messages, shared, products, tiles, own)
    whole = joined([split(tiles[place.tile(i)]) for i in range(n)], 1)
    packed = folded(product(whole, whole, 1), size)
    gram[...] = packed
    for message in messages:
        message[n * columns :] = packed
    shared[n * place.height :] = packed


def eliminated(gram, rest):
    n, width = gram.shape[0], rest.shape[1]
    groups = [[gram[g : g + 8], rest[g : g + 8]] for g in range(0, n, 8)]
    height = lax.broadcasted_iota(jnp.int32, (8, 1), 0)
    for first in range(0, n, PANEL):
        columns = [
            [jnp.broadcast_to(group[0][:, first + t : first + t + 1], (8, 128)) for group in groups]
            for t in range(PANEL)
        ]
        for t in range(PANEL):
            k = first + t
            gk, sk = k // 8, k % 8
            pivot = columns[t][gk][sk : sk + 1]
            inverse = 1.0 / pivot
            root = lax.rsqrt(pivot)
            source = [x[sk : sk + 1] for x in groups[gk]]
            steps = {}
            for g in range(gk, len(groups)):
                m = columns[t][g] * inverse
                steps[g] = jnp.where(height > sk, m, 0.0) if g == gk else m
            for u in range(t + 1, PANEL):
                head = columns[u][gk][sk : sk + 1]
                for g in range(gk, len(groups)):
                    columns[u][g] = columns[u][g] - steps[g] * head
            for g in range(gk, len(groups)):
                groups[g] = [x - wide(steps[g], x.shape[1]) * s for x, s in zip(groups[g], source)]
            groups[gk][1] = jnp.where(height == sk, groups[gk][1] * wide(root, width), groups[gk][1])
    return jnp.concatenate([group[1] for group in groups], axis=0)


def wide(x, lanes):
    if lanes <= x.shape[1]:
        return x[:, :lanes]
    return jnp.concatenate([x] * (lanes // x.shape[1]), axis=1)


def identity(n):
    rows = lax.broadcasted_iota(jnp.int32, (n, n), 0)
    return jnp.where(rows == lax.broadcasted_iota(jnp.int32, (n, n), 1), 1.0, 0.0)


def pair_kernel(mine, others, image, gram):
    tall = image.shape[0]
    image[...] = mine[:tall] + others[:tall]
    gram[...] = mine[tall:] + others[tall:]


def factor_kernel(total, gram, tiles, inverse, prior):
    columns = inverse.shape[0]
    lower = eliminated(unfolded(gram[...], columns) / total, identity(columns))
    inverse[...] = lower
    parts = [split(tiles[i : i + columns]) for i in range(0, tiles.shape[0], columns)]
    prior[...] = product(split(lower), joined(parts, 1))


def gram_kernel(inverse, prior, *refs):
    images, (image, out) = refs[:-2], refs[-2:]
    columns = inverse.shape[0]
    new = split(tree([part[...] for part in images]))
    rows = range(0, new[0].shape[0], columns)
    value = product(split(inverse[...]), [jnp.concatenate([x[i : i + columns] for i in rows], axis=1) for x in new])
    image[...] = value
    value = split(value)
    both = product(joined([value, split(prior[...])], 0), value, 1)
    out[...] = folded(both, out.shape[1])


def half_sum_kernel(mine, shared, *refs):
    received, out = refs[:-1], refs[-1]
    first = jnp.where((lax.axis_index("nbr") & 1) == 0, mine[...], shared[...])
    out[...] = tree([first] + [part[...] for part in received])


def last_kernel(total, image, mine, others, basis, ritz):
    columns = ritz.shape[0]
    both = unfolded((mine[...] + others[...]) / total, columns)
    ritz[...] = both[columns:]
    basis[...] = eliminated(both[:columns], image[...])


def body(blocks, partner_ids, counts, start):
    block_rows, slots, size, _ = blocks.shape
    columns = start.shape[1]
    rows, parts = lax.axis_size("row"), lax.axis_size("nbr")
    half = rows // 2
    all_blocks = block_rows * rows
    total = float(all_blocks * size)
    extra = columns * columns // size

    def flat(height):
        return jax.ShapeDtypeStruct((height, size), F32)

    tall = block_rows * columns
    tile, square = flat(tall), jax.ShapeDtypeStruct((columns, columns), F32)
    across = jax.ShapeDtypeStruct(start.shape[::-1], F32)
    table = pltpu.SMEM(partner_ids.shape, jnp.int32)
    work = pltpu.VMEM((all_blocks, columns, size), F32)

    def call(kernel, name, specs, outs, scratch=()):
        return pl.pallas_call(
            kernel,
            name=name,
            in_specs=specs,
            out_specs=[VMEM if isinstance(out, jax.ShapeDtypeStruct) else SMEM for out in outs],
            out_shape=outs,
            scratch_shapes=scratch,
            compiler_params=PARAMS,
        )

    def round_over_rows(messages, shared):
        return [swap_rows(m, 2 * k, 2 * k + 1) for k, m in enumerate(messages, 1)], swap(shared, "row", 1)

    def sum_over_pairs(image):
        return [image] + [swap(image, "nbr", s) for s in range(2, parts, 2)]

    other = swap(blocks, "nbr", 1)
    other_ids = swap(partner_ids, "nbr", 1)
    held, ids, counts, tiles = call(
        load_kernel,
        "load",
        [HBM] * 4,
        [jax.ShapeDtypeStruct(blocks.shape, F32), table, pltpu.SMEM(counts.shape, jnp.int32), tile],
        [DMA((3 + block_rows,))],
    )(*[pltpu.with_memory_space_constraint(x, pltpu.HBM) for x in (blocks, partner_ids, counts, start.T)])
    *messages, shared, own, other_ids = call(
        functools.partial(first_kernel, rows),
        "first_transposed",
        [VMEM, VMEM, SMEM, VMEM, SMEM, VMEM],
        [tile] * (half - 1) + [flat(tall // 2), tile, table],
        [work, DMA((1,))],
    )(held, other, ids, other_ids, counts, tiles)
    stored = (held, other, ids, other_ids, counts)
    index = [VMEM, VMEM, SMEM, SMEM, SMEM]
    received, shared = round_over_rows(messages, shared)
    deep = 2 * block_rows * slots * size
    pair, low = call(
        split_kernel,
        "split",
        [VMEM] * 3,
        [jax.ShapeDtypeStruct((deep, 2 * size), BF16), jax.ShapeDtypeStruct((deep, size), BF16)],
    )(held, other, own)
    parted = (pair, low, ids, other_ids, counts)
    direct = functools.partial(direct_kernel, rows, block_rows, slots)
    (image,) = call(direct, "first_direct", index + [VMEM] * (half + 2), [tile], [work])(
        *parted, own, tiles, *received, shared
    )
    images = sum_over_pairs(image + swap(image, "nbr", 1))
    *messages, shared, own, tiles, gram = call(
        functools.partial(second_kernel, rows, parts // 2),
        "second_transposed",
        index + [VMEM] * (parts // 2),
        [flat(tall + extra)] * (half - 1) + [flat(tall // 2 + extra), tile, tile, flat(extra)],
        [work],
    )(*stored, *images)
    received, shared = round_over_rows(messages, shared)
    (mine,) = call(direct, "second_direct", index + [VMEM] * (half + 3), [flat(tall + extra)], [work])(
        *parted, own, tiles, *received, shared, gram
    )
    image, gram = call(pair_kernel, "pair", [VMEM] * 2, [tile, flat(extra)])(mine, swap(mine, "nbr", 1))
    images = sum_over_pairs(image)
    inverse, prior = call(functools.partial(factor_kernel, total), "factor", [VMEM] * 2, [square, across])(gram, tiles)
    image, both = call(gram_kernel, "gram", [VMEM] * (parts // 2 + 2), [across, flat(2 * extra)])(
        inverse, prior, *images
    )
    received, shared = round_over_rows([both] * (half - 1), both)
    (both,) = call(half_sum_kernel, "half_sum", [VMEM] * (half + 1), [flat(2 * extra)])(both, shared, *received)
    basis, ritz = call(functools.partial(last_kernel, total), "last", [VMEM] * 3, [across, square])(
        image, both, swap(both, "nbr", 1)
    )
    return basis.T, ritz


def solution(mesh):
    return jax.shard_map(
        body,
        mesh=mesh,
        in_specs=(
            P(("dom", "row"), "nbr", None, None),
            P(("dom", "row"), "nbr"),
            P(("dom", "row")),
            P(("dom", "row"), None),
        ),
        out_specs=(P(("dom", "row"), None), P("dom", None)),
        check_vma=False,
    )
```

```python
import functools

import jax
import jax.numpy as jnp
from jax import lax
from jax.experimental import pallas as pl
from jax.experimental.pallas import tpu as pltpu
from jax.sharding import PartitionSpec as P

F32 = jnp.float32
BF16 = jnp.bfloat16
VMEM = pl.BlockSpec(memory_space=pltpu.VMEM)
SMEM = pl.BlockSpec(memory_space=pltpu.SMEM)
HBM = pl.BlockSpec(memory_space=pltpu.HBM)
DMA = pltpu.SemaphoreType.DMA
PARAMS = pltpu.CompilerParams(vmem_limit_bytes=8 * 2**20)
PANEL = 16


def tree(parts):
    while len(parts) > 1:
        parts = [parts[i] + parts[i + 1] for i in range(0, len(parts), 2)]
    return parts[0]


def split(x):
    high = x.astype(BF16)
    rest = x - high.astype(F32)
    middle = rest.astype(BF16)
    return high, middle, (rest - middle.astype(F32)).astype(BF16)


def dot(a, b, contract=0):
    return lax.dot_general(a, b, (((1,), (contract,)), ((), ())), preferred_element_type=F32)


def product(a_parts, b_parts, contract=0):
    n = a_parts[0].shape[0]
    stacked = jnp.concatenate(a_parts, axis=0)
    high = dot(stacked, b_parts[0], contract)
    middle = dot(stacked[: 2 * n], b_parts[1], contract)
    low = dot(a_parts[0], b_parts[2], contract)
    return high[:n] + ((high[n : 2 * n] + middle[:n]) + ((high[2 * n :] + middle[n:]) + low))


def shallow_product(a_parts, b_pair, b_low):
    n = a_parts[0].shape[0]
    stacked = jnp.concatenate(a_parts, axis=0)
    most = dot(jnp.concatenate([stacked, stacked], axis=1), b_pair)
    low = dot(a_parts[0], b_low)
    return most[:n] + (most[n : 2 * n] + (most[2 * n :] + low))


def narrow_product(a_parts, b_pair, b_low):
    n, width = a_parts[0].shape[0], b_low.shape[1]
    most = dot(jnp.concatenate(a_parts, axis=0), b_pair)
    high, middle = most[:, :width], most[:, width:]
    low = dot(a_parts[0], b_low)
    return high[:n] + ((high[n : 2 * n] + middle[:n]) + ((high[2 * n :] + middle[n : 2 * n]) + low))


def joined(parts, axis):
    return [jnp.concatenate(level, axis=axis) for level in zip(*parts)]


def folded(x, lanes):
    fold = lanes // x.shape[1]
    height = x.shape[0] // fold
    return jnp.concatenate([x[g * height : (g + 1) * height] for g in range(fold)], axis=1)


def unfolded(x, columns):
    return jnp.concatenate([x[:, g : g + columns] for g in range(0, x.shape[1], columns)], axis=0)


def swap(x, axis, distance):
    return lax.ppermute(x, axis, [(i, i ^ distance) for i in range(lax.axis_size(axis))])


def swap_rows(x, even, odd):
    rows, parts = lax.axis_size("row"), lax.axis_size("nbr")
    pairs = [
        (r * parts + n, (r ^ (odd if n % 2 else even)) * parts + n) for r in range(rows) for n in range(parts)
    ]
    return lax.ppermute(x, ("row", "nbr"), pairs)


class Place:
    def __init__(self, rows, block_rows, slots, columns):
        self.row = lax.axis_index("row")
        self.part = lax.axis_index("nbr")
        self.odd = self.part & 1
        self.block_rows, self.slots = block_rows, slots
        self.first_row = self.row * self.block_rows
        self.peers = [self.row ^ (k + self.odd) for k in range(2, rows, 2)]
        self.middle = self.row ^ 1
        self.columns = columns
        self.height = columns // 2
        self.half = pl.ds(pl.multiple_of(self.odd * self.height, self.height), self.height)

    def weight(self, ids, counts, member, i, p):
        used = (self.part ^ member) * self.slots + p < counts[i]
        return jnp.where(used, jnp.where(ids[i, p] == self.first_row + i, 0.5, 1.0), 0.0).astype(F32)

    def tile(self, i):
        return slice(i * self.columns, (i + 1) * self.columns)

    def half_tile(self, i):
        return slice(i * self.height, (i + 1) * self.height)


def stacked_blocks(blocks, i):
    slots = range(blocks[0].shape[1])
    high, middle, low = joined([split(b[i, p]) for b in blocks for p in slots], 1)
    return jnp.concatenate([high, middle], axis=0), low


def scatter(place, value, ids, counts, i, out):
    size = out.shape[2]
    for m, table in enumerate(ids):
        for p in range(place.slots):
            at = (m * place.slots + p) * size
            out[table[i, p]] += value[:, at : at + size] * place.weight(table, counts, m, i, p)


def direct_products(place, pair, low, ids, counts, whole, i):
    far = []
    for m in range(len(ids)):
        for p in range(place.slots):
            far.append(split(whole[ids[m][i, p]] * place.weight(ids[m], counts, m, i, p)))
    at = slice(i * len(far) * pair.shape[1] // 2, (i + 1) * len(far) * pair.shape[1] // 2)
    return narrow_product(joined(far, 1), pair[at], low[at])


def fill(place, messages, shared, products, tiles, own):
    n = place.block_rows
    for i in range(n):
        tile = tiles[place.tile(i)]
        for peer, out in zip(place.peers, messages):
            out[place.tile(i)] = jnp.where(place.row < peer, products[peer * n + i], tile)
        shared[place.half_tile(i)] = jnp.where(
            place.row < place.middle,
            products[place.middle * n + i, place.half],
            tiles[pl.ds(pl.multiple_of(i * place.columns + place.odd * place.height, 8), place.height)],
        )
        own[place.tile(i)] = jnp.where(place.odd == 0, products[place.first_row + i], 0.0)


def load_kernel(blocks, ids, counts, start, held, ids_s, counts_s, tiles, sems):
    size, columns = blocks.shape[2], start.shape[0]
    copies = [
        pltpu.make_async_copy(blocks, held, sems.at[0]),
        pltpu.make_async_copy(ids, ids_s, sems.at[1]),
        pltpu.make_async_copy(counts, counts_s, sems.at[2]),
    ]
    for i in range(blocks.shape[0]):
        source = start.at[:, i * size : (i + 1) * size]
        copies.append(pltpu.make_async_copy(source, tiles.at[i * columns : (i + 1) * columns], sems.at[3 + i]))
    for copy in copies:
        copy.start()
    for copy in copies:
        copy.wait()


def own_kernel(rows, held, ids, counts, tiles, products):
    place = Place(rows, *held.shape[:2], products.shape[1])
    products[...] = jnp.zeros_like(products)
    for i in range(place.block_rows):
        value = shallow_product(split(tiles[place.tile(i)]), *stacked_blocks((held,), i))
        scatter(place, value, (ids,), counts, i, products)


def first_kernel(rows, other, other_ids, counts, tiles, started, *refs):
    messages, refs = refs[: rows // 2 - 1], refs[rows // 2 - 1 :]
    shared, own, products = refs
    size = products.shape[2]
    place = Place(rows, *other.shape[:2], products.shape[1])
    terms = []
    for i in range(place.block_rows):
        value = shallow_product(split(tiles[place.tile(i)]), *stacked_blocks((other,), i))
        for p in range(place.slots):
            used = (place.part ^ 1) * place.slots + p < counts[i]
            j = jnp.broadcast_to(other_ids[i : i + 1, p : p + 1], (8, size))
            c = jnp.where(j == place.first_row + i, 0.5, 1.0)
            terms.append((jnp.where(used, j, -1), c, value[:, p * size : (p + 1) * size]))
    copies = place.columns // 8
    for block in range(products.shape[0]):
        total = started[block]
        for j, c, value in terms:
            total += jnp.concatenate([jnp.where(j == block, c, 0.0)] * copies, axis=0) * value
        products[block] = total
    fill(place, messages, shared, products, tiles, own)


def split_kernel(held, other, other_ids, after, direct_pair, direct_low, pair, low, other_s, sem):
    block_rows, slots, size, _ = held.shape
    copy = pltpu.make_async_copy(other_ids, other_s, sem.at[0])
    copy.start()
    at = 0
    for i in range(block_rows):
        for b in (held, other):
            for p in range(slots):
                high, middle, rest = split(b[i, p].T)
                direct_pair[at : at + size, :size] = high
                direct_pair[at : at + size, size:] = middle
                direct_low[at : at + size] = rest
                at += size
        pair[2 * i * size : 2 * (i + 1) * size], low[i * size : (i + 1) * size] = stacked_blocks((held, other), i)
    copy.wait()


def direct_kernel(rows, block_rows, slots, pair, low, ids, other_ids, counts, own, tiles, *refs):
    received, refs = refs[: rows // 2 - 1], refs[rows // 2 - 1 :]
    shared, *gram, out, whole = refs
    n, columns = block_rows, whole.shape[1]
    place = Place(rows, block_rows, slots, columns)
    whole[...] = jnp.zeros_like(whole)
    for i in range(n):
        whole[place.first_row + i] = jnp.where(place.odd == 0, tiles[place.tile(i)], 0.0)
        for peer, message in zip(place.peers, received):
            whole[peer * n + i] = message[place.tile(i)]
        whole[place.middle * n + i, place.half] = shared[place.half_tile(i)]
    for i in range(n):
        value = own[place.tile(i)]
        for peer, message in zip(place.peers, received):
            value += jnp.where(place.row > peer, message[place.tile(i)], 0.0)
        out[place.tile(i)] = value + direct_products(
            place, pair, low, (ids, other_ids), counts, whole, i
        )
        mine = pl.ds(pl.multiple_of(i * columns + place.odd * place.height, 8), place.height)
        out[mine] += jnp.where(place.row > place.middle, shared[place.half_tile(i)], 0.0)
    if gram:
        first = jnp.where(place.odd == 0, gram[0][...], shared[n * place.height :])
        out[n * columns :] = tree([first] + [message[n * columns :] for message in received])


def second_kernel(rows, parts, block_rows, slots, pair, low, ids, other_ids, counts, *refs):
    images, refs = refs[:parts], refs[parts:]
    messages, refs = refs[: rows // 2 - 1], refs[rows // 2 - 1 :]
    shared, own, tiles, gram, products = refs
    n, columns, size = block_rows, products.shape[1], products.shape[2]
    place = Place(rows, block_rows, slots, columns)
    tiles[...] = tree([image[...] for image in images])
    products[...] = jnp.zeros_like(products)
    for i in range(n):
        value = shallow_product(
            split(tiles[place.tile(i)]),
            pair[2 * i * size : 2 * (i + 1) * size],
            low[i * size : (i + 1) * size],
        )
        scatter(place, value, (ids, other_ids), counts, i, products)
    fill(place, messages, shared, products, tiles, own)
    whole = joined([split(tiles[place.tile(i)]) for i in range(n)], 1)
    packed = folded(product(whole, whole, 1), size)
    gram[...] = packed
    for message in messages:
        message[n * columns :] = packed
    shared[n * place.height :] = packed


def eliminated(gram, rest):
    n, width = gram.shape[0], rest.shape[1]
    groups = [[gram[g : g + 8], rest[g : g + 8]] for g in range(0, n, 8)]
    height = lax.broadcasted_iota(jnp.int32, (8, 1), 0)
    for first in range(0, n, PANEL):
        columns = [
            [jnp.broadcast_to(group[0][:, first + t : first + t + 1], (8, 128)) for group in groups]
            for t in range(PANEL)
        ]
        for t in range(PANEL):
            k = first + t
            gk, sk = k // 8, k % 8
            pivot = columns[t][gk][sk : sk + 1]
            inverse = 1.0 / pivot
            root = lax.rsqrt(pivot)
            source = [x[sk : sk + 1] for x in groups[gk]]
            steps = {}
            for g in range(gk, len(groups)):
                m = columns[t][g] * inverse
                steps[g] = jnp.where(height > sk, m, 0.0) if g == gk else m
            for u in range(t + 1, PANEL):
                head = columns[u][gk][sk : sk + 1]
                for g in range(gk, len(groups)):
                    columns[u][g] = columns[u][g] - steps[g] * head
            for g in range(gk, len(groups)):
                groups[g] = [x - wide(steps[g], x.shape[1]) * s for x, s in zip(groups[g], source)]
            groups[gk][1] = jnp.where(height == sk, groups[gk][1] * wide(root, width), groups[gk][1])
    return jnp.concatenate([group[1] for group in groups], axis=0)


def wide(x, lanes):
    if lanes <= x.shape[1]:
        return x[:, :lanes]
    return jnp.concatenate([x] * (lanes // x.shape[1]), axis=1)


def identity(n):
    rows = lax.broadcasted_iota(jnp.int32, (n, n), 0)
    return jnp.where(rows == lax.broadcasted_iota(jnp.int32, (n, n), 1), 1.0, 0.0)


def pair_kernel(mine, others, image, gram):
    tall = image.shape[0]
    image[...] = mine[:tall] + others[:tall]
    gram[...] = mine[tall:] + others[tall:]


def factor_kernel(total, gram, tiles, inverse, prior):
    columns = inverse.shape[0]
    lower = eliminated(unfolded(gram[...], columns) / total, identity(columns))
    inverse[...] = lower
    parts = [split(tiles[i : i + columns]) for i in range(0, tiles.shape[0], columns)]
    prior[...] = product(split(lower), joined(parts, 1))


def gram_kernel(inverse, prior, *refs):
    images, (image, out) = refs[:-2], refs[-2:]
    columns = inverse.shape[0]
    new = split(tree([part[...] for part in images]))
    rows = range(0, new[0].shape[0], columns)
    value = product(split(inverse[...]), [jnp.concatenate([x[i : i + columns] for i in rows], axis=1) for x in new])
    image[...] = value
    value = split(value)
    both = product(joined([value, split(prior[...])], 0), value, 1)
    out[...] = folded(both, out.shape[1])


def half_sum_kernel(mine, shared, *refs):
    received, out = refs[:-1], refs[-1]
    first = jnp.where((lax.axis_index("nbr") & 1) == 0, mine[...], shared[...])
    out[...] = tree([first] + [part[...] for part in received])


def last_kernel(total, image, mine, others, basis, ritz):
    columns = ritz.shape[0]
    both = unfolded((mine[...] + others[...]) / total, columns)
    ritz[...] = both[columns:]
    basis[...] = eliminated(both[:columns], image[...])


def body(blocks, partner_ids, counts, start):
    block_rows, slots, size, _ = blocks.shape
    columns = start.shape[1]
    rows, parts = lax.axis_size("row"), lax.axis_size("nbr")
    half = rows // 2
    all_blocks = block_rows * rows
    total = float(all_blocks * size)
    extra = columns * columns // size

    def flat(height):
        return jax.ShapeDtypeStruct((height, size), F32)

    tall = block_rows * columns
    tile, square = flat(tall), jax.ShapeDtypeStruct((columns, columns), F32)
    across = jax.ShapeDtypeStruct(start.shape[::-1], F32)
    table = pltpu.SMEM(partner_ids.shape, jnp.int32)
    work = pltpu.VMEM((all_blocks, columns, size), F32)

    def call(kernel, name, specs, outs, scratch=()):
        return pl.pallas_call(
            kernel,
            name=name,
            in_specs=specs,
            out_specs=[VMEM if isinstance(out, jax.ShapeDtypeStruct) else SMEM for out in outs],
            out_shape=outs,
            scratch_shapes=scratch,
            compiler_params=PARAMS,
        )

    def round_over_rows(messages, shared):
        return [swap_rows(m, 2 * k, 2 * k + 1) for k, m in enumerate(messages, 1)], swap(shared, "row", 1)

    def sum_over_pairs(image):
        return [image] + [swap(image, "nbr", s) for s in range(2, parts, 2)]

    other = swap(blocks, "nbr", 1)
    other_ids = swap(partner_ids, "nbr", 1)
    held, ids, counts, tiles = call(
        load_kernel,
        "load",
        [HBM] * 4,
        [jax.ShapeDtypeStruct(blocks.shape, F32), table, pltpu.SMEM(counts.shape, jnp.int32), tile],
        [DMA((3 + block_rows,))],
    )(*[pltpu.with_memory_space_constraint(x, pltpu.HBM) for x in (blocks, partner_ids, counts, start.T)])
    (started,) = call(
        functools.partial(own_kernel, rows),
        "own_transposed",
        [VMEM, SMEM, SMEM, VMEM],
        [jax.ShapeDtypeStruct(work.shape, F32)],
    )(held, ids, counts, tiles)
    *messages, shared, own = call(
        functools.partial(first_kernel, rows),
        "first_transposed",
        [VMEM, VMEM, SMEM, VMEM, VMEM],
        [tile] * (half - 1) + [flat(tall // 2), tile],
        [work],
    )(other, other_ids, counts, tiles, started)
    index = [VMEM, VMEM, SMEM, SMEM, SMEM]
    received, shared = round_over_rows(messages, shared)
    deep = 2 * block_rows * slots * size
    wide_row = 2 * slots * size
    direct_pair, direct_low, pair, low, other_ids = call(
        split_kernel,
        "split",
        [VMEM] * 4,
        [
            jax.ShapeDtypeStruct((deep, 2 * size), BF16),
            jax.ShapeDtypeStruct((deep, size), BF16),
            jax.ShapeDtypeStruct((2 * block_rows * size, wide_row), BF16),
            jax.ShapeDtypeStruct((block_rows * size, wide_row), BF16),
            table,
        ],
        [DMA((1,))],
    )(held, other, other_ids, own)
    parted = (direct_pair, direct_low, ids, other_ids, counts)
    direct = functools.partial(direct_kernel, rows, block_rows, slots)
    (image,) = call(direct, "first_direct", index + [VMEM] * (half + 2), [tile], [work])(
        *parted, own, tiles, *received, shared
    )
    images = sum_over_pairs(image + swap(image, "nbr", 1))
    *messages, shared, own, tiles, gram = call(
        functools.partial(second_kernel, rows, parts // 2, block_rows, slots),
        "second_transposed",
        index + [VMEM] * (parts // 2),
        [flat(tall + extra)] * (half - 1) + [flat(tall // 2 + extra), tile, tile, flat(extra)],
        [work],
    )(pair, low, ids, other_ids, counts, *images)
    received, shared = round_over_rows(messages, shared)
    (mine,) = call(direct, "second_direct", index + [VMEM] * (half + 3), [flat(tall + extra)], [work])(
        *parted, own, tiles, *received, shared, gram
    )
    image, gram = call(pair_kernel, "pair", [VMEM] * 2, [tile, flat(extra)])(mine, swap(mine, "nbr", 1))
    images = sum_over_pairs(image)
    inverse, prior = call(functools.partial(factor_kernel, total), "factor", [VMEM] * 2, [square, across])(gram, tiles)
    image, both = call(gram_kernel, "gram", [VMEM] * (parts // 2 + 2), [across, flat(2 * extra)])(
        inverse, prior, *images
    )
    received, shared = round_over_rows([both] * (half - 1), both)
    (both,) = call(half_sum_kernel, "half_sum", [VMEM] * (half + 1), [flat(2 * extra)])(both, shared, *received)
    basis, ritz = call(functools.partial(last_kernel, total), "last", [VMEM] * 3, [across, square])(
        image, both, swap(both, "nbr", 1)
    )
    return basis.T, ritz


def solution(mesh):
    return jax.shard_map(
        body,
        mesh=mesh,
        in_specs=(
            P(("dom", "row"), "nbr", None, None),
            P(("dom", "row"), "nbr"),
            P(("dom", "row")),
            P(("dom", "row"), None),
        ),
        out_specs=(P(("dom", "row"), None), P("dom", None)),
        check_vma=False,
    )
```

```python
import functools

import jax
import jax.numpy as jnp
from jax import lax
from jax.experimental import pallas as pl
from jax.experimental.pallas import tpu as pltpu
from jax.sharding import PartitionSpec as P

F32 = jnp.float32
BF16 = jnp.bfloat16
VMEM = pl.BlockSpec(memory_space=pltpu.VMEM)
SMEM = pl.BlockSpec(memory_space=pltpu.SMEM)
HBM = pl.BlockSpec(memory_space=pltpu.HBM)
DMA = pltpu.SemaphoreType.DMA
PARAMS = pltpu.CompilerParams(vmem_limit_bytes=8 * 2**20)
PANEL = 16


def tree(parts):
    while len(parts) > 1:
        parts = [parts[i] + parts[i + 1] for i in range(0, len(parts), 2)]
    return parts[0]


def split(x):
    high = x.astype(BF16)
    rest = x - high.astype(F32)
    middle = rest.astype(BF16)
    return high, middle, (rest - middle.astype(F32)).astype(BF16)


def dot(a, b, contract=0):
    return lax.dot_general(a, b, (((1,), (contract,)), ((), ())), preferred_element_type=F32)


def product(a_parts, b_parts, contract=0):
    n = a_parts[0].shape[0]
    stacked = jnp.concatenate(a_parts, axis=0)
    high = dot(stacked, b_parts[0], contract)
    middle = dot(stacked[: 2 * n], b_parts[1], contract)
    low = dot(a_parts[0], b_parts[2], contract)
    return high[:n] + ((high[n : 2 * n] + middle[:n]) + ((high[2 * n :] + middle[n:]) + low))


def shallow_product(a_parts, b_pair, b_low):
    n = a_parts[0].shape[0]
    stacked = jnp.concatenate(a_parts, axis=0)
    most = dot(jnp.concatenate([stacked, stacked], axis=1), b_pair)
    low = dot(a_parts[0], b_low)
    return most[:n] + (most[n : 2 * n] + (most[2 * n :] + low))


def narrow_product(a_parts, b_pair, b_low):
    n, width = a_parts[0].shape[0], b_low.shape[1]
    most = dot(jnp.concatenate(a_parts, axis=0), b_pair)
    high, middle = most[:, :width], most[:, width:]
    low = dot(a_parts[0], b_low)
    return high[:n] + ((high[n : 2 * n] + middle[:n]) + ((high[2 * n :] + middle[n : 2 * n]) + low))


def joined(parts, axis):
    return [jnp.concatenate(level, axis=axis) for level in zip(*parts)]


def folded(x, lanes):
    fold = lanes // x.shape[1]
    height = x.shape[0] // fold
    return jnp.concatenate([x[g * height : (g + 1) * height] for g in range(fold)], axis=1)


def unfolded(x, columns):
    return jnp.concatenate([x[:, g : g + columns] for g in range(0, x.shape[1], columns)], axis=0)


def swap(x, axis, distance):
    return lax.ppermute(x, axis, [(i, i ^ distance) for i in range(lax.axis_size(axis))])


def swap_rows(x, even, odd):
    rows, parts = lax.axis_size("row"), lax.axis_size("nbr")
    pairs = [
        (r * parts + n, (r ^ (odd if n % 2 else even)) * parts + n) for r in range(rows) for n in range(parts)
    ]
    return lax.ppermute(x, ("row", "nbr"), pairs)


class Place:
    def __init__(self, rows, block_rows, slots, columns):
        self.row = lax.axis_index("row")
        self.part = lax.axis_index("nbr")
        self.odd = self.part & 1
        self.block_rows, self.slots = block_rows, slots
        self.first_row = self.row * self.block_rows
        self.peers = [self.row ^ 1] + [self.row ^ (k + self.odd) for k in range(2, rows, 2)]
        self.others_peers = [self.row ^ (k + 1 - self.odd) for k in range(2, rows, 2)]
        self.columns = columns

    def weight(self, ids, counts, member, i, p):
        used = (self.part ^ member) * self.slots + p < counts[i]
        return jnp.where(used, jnp.where(ids[i, p] == self.first_row + i, 0.5, 1.0), 0.0).astype(F32)

    def tile(self, i):
        return slice(i * self.columns, (i + 1) * self.columns)

    def by_distance(self, mine, received, handed):
        both = [(jnp.where(self.odd == 0, a, b), jnp.where(self.odd == 0, b, a)) for a, b in zip(received[1:], handed)]
        return [mine, received[0]] + [x for pair in both for x in pair]


def stacked_blocks(blocks, i):
    slots = range(blocks[0].shape[1])
    high, middle, low = joined([split(b[i, p]) for b in blocks for p in slots], 1)
    return jnp.concatenate([high, middle], axis=0), low


def scatter(place, value, ids, counts, i, out):
    size = out.shape[2]
    for m, table in enumerate(ids):
        for p in range(place.slots):
            at = (m * place.slots + p) * size
            out[table[i, p]] += value[:, at : at + size] * place.weight(table, counts, m, i, p)


def direct_products(place, pair, low, ids, counts, whole, i):
    far = []
    for m in range(len(ids)):
        for p in range(place.slots):
            far.append(split(whole[ids[m][i, p]] * place.weight(ids[m], counts, m, i, p)))
    at = slice(i * len(far) * pair.shape[1] // 2, (i + 1) * len(far) * pair.shape[1] // 2)
    return narrow_product(joined(far, 1), pair[at], low[at])


def fill(place, messages, products, tiles, own):
    n = place.block_rows
    for i in range(n):
        tile = tiles[place.tile(i)]
        for peer, out in zip(place.peers, messages):
            out[place.tile(i)] = jnp.where(place.row < peer, products[peer * n + i], tile)
        own[place.tile(i)] = products[place.first_row + i]


def load_kernel(blocks, ids, counts, start, held, ids_s, counts_s, tiles, sems):
    size, columns = blocks.shape[2], start.shape[0]
    copies = [
        pltpu.make_async_copy(blocks, held, sems.at[0]),
        pltpu.make_async_copy(ids, ids_s, sems.at[1]),
        pltpu.make_async_copy(counts, counts_s, sems.at[2]),
    ]
    for i in range(blocks.shape[0]):
        source = start.at[:, i * size : (i + 1) * size]
        copies.append(pltpu.make_async_copy(source, tiles.at[i * columns : (i + 1) * columns], sems.at[3 + i]))
    for copy in copies:
        copy.start()
    for copy in copies:
        copy.wait()


def own_kernel(rows, held, ids, counts, tiles, products):
    place = Place(rows, *held.shape[:2], products.shape[1])
    products[...] = jnp.zeros_like(products)
    for i in range(place.block_rows):
        value = shallow_product(split(tiles[place.tile(i)]), *stacked_blocks((held,), i))
        scatter(place, value, (ids,), counts, i, products)


def first_kernel(rows, other, other_ids, counts, tiles, started, *refs):
    messages, (own, products) = refs[:-2], refs[-2:]
    size = products.shape[2]
    place = Place(rows, *other.shape[:2], products.shape[1])
    terms = []
    for i in range(place.block_rows):
        value = shallow_product(split(tiles[place.tile(i)]), *stacked_blocks((other,), i))
        for p in range(place.slots):
            used = (place.part ^ 1) * place.slots + p < counts[i]
            j = jnp.broadcast_to(other_ids[i : i + 1, p : p + 1], (8, size))
            c = jnp.where(j == place.first_row + i, 0.5, 1.0)
            terms.append((jnp.where(used, j, -1), c, value[:, p * size : (p + 1) * size]))
    copies = place.columns // 8
    for block in range(products.shape[0]):
        total = started[block]
        for j, c, value in terms:
            total += jnp.concatenate([jnp.where(j == block, c, 0.0)] * copies, axis=0) * value
        products[block] = total
    fill(place, messages, products, tiles, own)


def split_kernel(held, other, other_ids, after, direct_pair, direct_low, pair, low, other_s, sem):
    block_rows, slots, size, _ = held.shape
    copy = pltpu.make_async_copy(other_ids, other_s, sem.at[0])
    copy.start()
    at = 0
    for i in range(block_rows):
        for b in (held, other):
            for p in range(slots):
                high, middle, rest = split(b[i, p].T)
                direct_pair[at : at + size, :size] = high
                direct_pair[at : at + size, size:] = middle
                direct_low[at : at + size] = rest
                at += size
        pair[2 * i * size : 2 * (i + 1) * size], low[i * size : (i + 1) * size] = stacked_blocks((held, other), i)
    copy.wait()


def direct_kernel(rows, block_rows, slots, pair, low, ids, other_ids, counts, own, tiles, *refs):
    half = rows // 2
    received, handed, refs = refs[:half], refs[half : rows - 1], refs[rows - 1 :]
    *gram, whole = refs
    n, columns = block_rows, whole.shape[1]
    place = Place(rows, block_rows, slots, columns)
    for i in range(n):
        whole[place.first_row + i] = tiles[place.tile(i)]
        for peer, message in zip(place.peers + place.others_peers, received + handed):
            whole[peer * n + i] = message[place.tile(i)]
    if len(gram) == 1:
        (out,) = gram
    else:
        mine, out, total = gram
        tall = n * columns
        total[...] = tree(place.by_distance(mine[...], [m[tall:] for m in received], [m[tall:] for m in handed]))
    for i in range(n):
        at = place.tile(i)
        arrived = place.by_distance(own[at], [m[at] for m in received], [m[at] for m in handed])
        value = arrived[0]
        for s in range(1, rows):
            value += jnp.where(place.row > (place.row ^ s), arrived[s], 0.0)
        out[at] = value + direct_products(place, pair, low, (ids, other_ids), counts, whole, i)


def second_kernel(rows, parts, block_rows, slots, pair, low, ids, other_ids, counts, *refs):
    images, refs = refs[:parts], refs[parts:]
    messages, (own, tiles, gram, products) = refs[: rows // 2], refs[rows // 2 :]
    n, columns, size = block_rows, products.shape[1], products.shape[2]
    place = Place(rows, block_rows, slots, columns)
    tiles[...] = tree([image[...] for image in images])
    products[...] = jnp.zeros_like(products)
    for i in range(n):
        value = shallow_product(
            split(tiles[place.tile(i)]),
            pair[2 * i * size : 2 * (i + 1) * size],
            low[i * size : (i + 1) * size],
        )
        scatter(place, value, (ids, other_ids), counts, i, products)
    fill(place, messages, products, tiles, own)
    whole = joined([split(tiles[place.tile(i)]) for i in range(n)], 1)
    packed = folded(product(whole, whole, 1), size)
    gram[...] = packed
    for message in messages:
        message[n * columns :] = packed


def eliminated(gram, rest):
    n, width = gram.shape[0], rest.shape[1]
    groups = [[gram[g : g + 8], rest[g : g + 8]] for g in range(0, n, 8)]
    height = lax.broadcasted_iota(jnp.int32, (8, 1), 0)
    for first in range(0, n, PANEL):
        columns = [
            [jnp.broadcast_to(group[0][:, first + t : first + t + 1], (8, 128)) for group in groups]
            for t in range(PANEL)
        ]
        for t in range(PANEL):
            k = first + t
            gk, sk = k // 8, k % 8
            pivot = columns[t][gk][sk : sk + 1]
            inverse = 1.0 / pivot
            root = lax.rsqrt(pivot)
            source = [x[sk : sk + 1] for x in groups[gk]]
            steps = {}
            for g in range(gk, len(groups)):
                m = columns[t][g] * inverse
                steps[g] = jnp.where(height > sk, m, 0.0) if g == gk else m
            for u in range(t + 1, PANEL):
                head = columns[u][gk][sk : sk + 1]
                for g in range(gk, len(groups)):
                    columns[u][g] = columns[u][g] - steps[g] * head
            for g in range(gk, len(groups)):
                groups[g] = [x - wide(steps[g], x.shape[1]) * s for x, s in zip(groups[g], source)]
            groups[gk][1] = jnp.where(height == sk, groups[gk][1] * wide(root, width), groups[gk][1])
    return jnp.concatenate([group[1] for group in groups], axis=0)


def wide(x, lanes):
    if lanes <= x.shape[1]:
        return x[:, :lanes]
    return jnp.concatenate([x] * (lanes // x.shape[1]), axis=1)


def identity(n):
    rows = lax.broadcasted_iota(jnp.int32, (n, n), 0)
    return jnp.where(rows == lax.broadcasted_iota(jnp.int32, (n, n), 1), 1.0, 0.0)


def factor_kernel(total, gram, tiles, inverse, prior):
    columns = inverse.shape[0]
    lower = eliminated(unfolded(gram[...], columns) / total, identity(columns))
    inverse[...] = lower
    parts = [split(tiles[i : i + columns]) for i in range(0, tiles.shape[0], columns)]
    prior[...] = product(split(lower), joined(parts, 1))


def gram_kernel(inverse, prior, *refs):
    images, (image, out) = refs[:-2], refs[-2:]
    columns = inverse.shape[0]
    new = split(tree([part[...] for part in images]))
    rows = range(0, new[0].shape[0], columns)
    value = product(split(inverse[...]), [jnp.concatenate([x[i : i + columns] for i in rows], axis=1) for x in new])
    image[...] = value
    value = split(value)
    both = product(joined([value, split(prior[...])], 0), value, 1)
    out[...] = folded(both, out.shape[1])


def last_kernel(rows, total, image, mine, *refs):
    half = rows // 2
    received, handed, (basis, ritz) = refs[:half], refs[half : rows - 1], refs[rows - 1 :]
    columns = ritz.shape[0]
    place = Place(rows, 0, 0, columns)
    parts = place.by_distance(mine[...], [m[...] for m in received], [m[...] for m in handed])
    both = unfolded(tree(parts) / total, columns)
    ritz[...] = both[columns:]
    basis[...] = eliminated(both[:columns], image[...])


def body(blocks, partner_ids, counts, start):
    block_rows, slots, size, _ = blocks.shape
    columns = start.shape[1]
    rows, parts = lax.axis_size("row"), lax.axis_size("nbr")
    half = rows // 2
    all_blocks = block_rows * rows
    total = float(all_blocks * size)
    extra = columns * columns // size

    def flat(height):
        return jax.ShapeDtypeStruct((height, size), F32)

    tall = block_rows * columns
    tile, square = flat(tall), jax.ShapeDtypeStruct((columns, columns), F32)
    across = jax.ShapeDtypeStruct(start.shape[::-1], F32)
    table = pltpu.SMEM(partner_ids.shape, jnp.int32)
    work = pltpu.VMEM((all_blocks, columns, size), F32)

    def call(kernel, name, specs, outs, scratch=()):
        return pl.pallas_call(
            kernel,
            name=name,
            in_specs=specs,
            out_specs=[VMEM if isinstance(out, jax.ShapeDtypeStruct) else SMEM for out in outs],
            out_shape=outs,
            scratch_shapes=scratch,
            compiler_params=PARAMS,
        )

    def round_over_rows(messages):
        received = [swap_rows(m, 2 * k, 2 * k + 1) for k, m in enumerate(messages[1:], 1)]
        near = swap(messages[0], "row", 1)
        return [near] + received + [swap(m, "nbr", 1) for m in received]

    def sum_over_pairs(image):
        return [image] + [swap(image, "nbr", s) for s in range(2, parts, 2)]

    other = swap(blocks, "nbr", 1)
    other_ids = swap(partner_ids, "nbr", 1)
    held, ids, counts, tiles = call(
        load_kernel,
        "load",
        [HBM] * 4,
        [jax.ShapeDtypeStruct(blocks.shape, F32), table, pltpu.SMEM(counts.shape, jnp.int32), tile],
        [DMA((3 + block_rows,))],
    )(*[pltpu.with_memory_space_constraint(x, pltpu.HBM) for x in (blocks, partner_ids, counts, start.T)])
    (started,) = call(
        functools.partial(own_kernel, rows),
        "own_transposed",
        [VMEM, SMEM, SMEM, VMEM],
        [jax.ShapeDtypeStruct(work.shape, F32)],
    )(held, ids, counts, tiles)
    *messages, own = call(
        functools.partial(first_kernel, rows),
        "first_transposed",
        [VMEM, VMEM, SMEM, VMEM, VMEM],
        [tile] * (half + 1),
        [work],
    )(other, other_ids, counts, tiles, started)
    index = [VMEM, VMEM, SMEM, SMEM, SMEM]
    arrived = round_over_rows(messages)
    deep = 2 * block_rows * slots * size
    wide_row = 2 * slots * size
    direct_pair, direct_low, pair, low, other_ids = call(
        split_kernel,
        "split",
        [VMEM] * 4,
        [
            jax.ShapeDtypeStruct((deep, 2 * size), BF16),
            jax.ShapeDtypeStruct((deep, size), BF16),
            jax.ShapeDtypeStruct((2 * block_rows * size, wide_row), BF16),
            jax.ShapeDtypeStruct((block_rows * size, wide_row), BF16),
            table,
        ],
        [DMA((1,))],
    )(held, other, other_ids, own)
    parted = (direct_pair, direct_low, ids, other_ids, counts)
    direct = functools.partial(direct_kernel, rows, block_rows, slots)
    (image,) = call(direct, "first_direct", index + [VMEM] * (rows + 1), [tile], [work])(
        *parted, own, tiles, *arrived
    )
    images = sum_over_pairs(image)
    *messages, own, tiles, gram = call(
        functools.partial(second_kernel, rows, parts // 2, block_rows, slots),
        "second_transposed",
        index + [VMEM] * (parts // 2),
        [flat(tall + extra)] * half + [tile, tile, flat(extra)],
        [work],
    )(pair, low, ids, other_ids, counts, *images)
    arrived = round_over_rows(messages)
    image, gram = call(direct, "second_direct", index + [VMEM] * (rows + 2), [tile, flat(extra)], [work])(
        *parted, own, tiles, *arrived, gram
    )
    images = sum_over_pairs(image)
    inverse, prior = call(functools.partial(factor_kernel, total), "factor", [VMEM] * 2, [square, across])(gram, tiles)
    image, both = call(gram_kernel, "gram", [VMEM] * (parts // 2 + 2), [across, flat(2 * extra)])(
        inverse, prior, *images
    )
    arrived = round_over_rows([both] * half)
    basis, ritz = call(
        functools.partial(last_kernel, rows, total), "last", [VMEM] * (rows + 1), [across, square]
    )(image, both, *arrived)
    return basis.T, ritz


def solution(mesh):
    return jax.shard_map(
        body,
        mesh=mesh,
        in_specs=(
            P(("dom", "row"), "nbr", None, None),
            P(("dom", "row"), "nbr"),
            P(("dom", "row")),
            P(("dom", "row"), None),
        ),
        out_specs=(P(("dom", "row"), None), P("dom", None)),
        check_vma=False,
    )
```

```python
import functools

import jax
import jax.numpy as jnp
from jax import lax
from jax.experimental import pallas as pl
from jax.experimental.pallas import tpu as pltpu
from jax.sharding import PartitionSpec as P

F32 = jnp.float32
BF16 = jnp.bfloat16
VMEM = pl.BlockSpec(memory_space=pltpu.VMEM)
SMEM = pl.BlockSpec(memory_space=pltpu.SMEM)
HBM = pl.BlockSpec(memory_space=pltpu.HBM)
DMA = pltpu.SemaphoreType.DMA
PARAMS = pltpu.CompilerParams(vmem_limit_bytes=8 * 2**20)
PANEL = 16


def tree(parts):
    while len(parts) > 1:
        parts = [parts[i] + parts[i + 1] for i in range(0, len(parts), 2)]
    return parts[0]


def split(x):
    high = x.astype(BF16)
    rest = x - high.astype(F32)
    middle = rest.astype(BF16)
    return high, middle, (rest - middle.astype(F32)).astype(BF16)


def dot(a, b, contract=0):
    return lax.dot_general(a, b, (((1,), (contract,)), ((), ())), preferred_element_type=F32)


def product(a_parts, b_parts, contract=0):
    n = a_parts[0].shape[0]
    stacked = jnp.concatenate(a_parts, axis=0)
    high = dot(stacked, b_parts[0], contract)
    middle = dot(stacked[: 2 * n], b_parts[1], contract)
    low = dot(a_parts[0], b_parts[2], contract)
    return high[:n] + ((high[n : 2 * n] + middle[:n]) + ((high[2 * n :] + middle[n:]) + low))


def shallow_product(a_parts, b_pair, b_low):
    n = a_parts[0].shape[0]
    stacked = jnp.concatenate(a_parts, axis=0)
    most = dot(jnp.concatenate([stacked, stacked], axis=1), b_pair)
    low = dot(a_parts[0], b_low)
    return most[:n] + (most[n : 2 * n] + (most[2 * n :] + low))


def narrow_product(a_parts, b_pair, b_low):
    n, width = a_parts[0].shape[0], b_low.shape[1]
    most = dot(jnp.concatenate(a_parts, axis=0), b_pair)
    high, middle = most[:, :width], most[:, width:]
    low = dot(a_parts[0], b_low)
    return high[:n] + ((high[n : 2 * n] + middle[:n]) + ((high[2 * n :] + middle[n : 2 * n]) + low))


def joined(parts, axis):
    return [jnp.concatenate(level, axis=axis) for level in zip(*parts)]


def folded(x, lanes):
    fold = lanes // x.shape[1]
    height = x.shape[0] // fold
    return jnp.concatenate([x[g * height : (g + 1) * height] for g in range(fold)], axis=1)


def unfolded(x, columns):
    return jnp.concatenate([x[:, g : g + columns] for g in range(0, x.shape[1], columns)], axis=0)


def swap(x, axis, distance):
    return lax.ppermute(x, axis, [(i, i ^ distance) for i in range(lax.axis_size(axis))])


def swap_rows(x, even, odd):
    rows, parts = lax.axis_size("row"), lax.axis_size("nbr")
    pairs = [
        (r * parts + n, (r ^ (odd if n % 2 else even)) * parts + n) for r in range(rows) for n in range(parts)
    ]
    return lax.ppermute(x, ("row", "nbr"), pairs)


class Place:
    def __init__(self, rows, block_rows, slots, columns):
        self.row = lax.axis_index("row")
        self.part = lax.axis_index("nbr")
        self.odd = self.part & 1
        self.block_rows, self.slots = block_rows, slots
        self.first_row = self.row * self.block_rows
        self.peers = [self.row ^ 1] + [self.row ^ (k + self.odd) for k in range(2, rows, 2)]
        self.others_peers = [self.row ^ (k + 1 - self.odd) for k in range(2, rows, 2)]
        self.columns = columns

    def column(self, ids, m, i, p):
        own, other = ids
        return jnp.where(self.odd == m, own[i, p], other[i, p])

    def weight(self, column, counts, m, i, p):
        used = (self.part - self.odd + m) * self.slots + p < counts[i]
        return jnp.where(used, jnp.where(column == self.first_row + i, 0.5, 1.0), 0.0).astype(F32)

    def tile(self, i):
        return slice(i * self.columns, (i + 1) * self.columns)

    def by_distance(self, mine, received, handed):
        both = [(jnp.where(self.odd == 0, a, b), jnp.where(self.odd == 0, b, a)) for a, b in zip(received[1:], handed)]
        return [mine, received[0]] + [x for pair in both for x in pair]


def stacked_blocks(blocks):
    high, middle, low = joined([split(b) for b in blocks], 1)
    return jnp.concatenate([high, middle], axis=0), low


def scatter(place, value, ids, counts, i, out):
    size = out.shape[2]
    for m in range(2):
        for p in range(place.slots):
            at = (m * place.slots + p) * size
            j = place.column(ids, m, i, p)
            out[j] += value[:, at : at + size] * place.weight(j, counts, m, i, p)


def direct_products(place, pair, low, ids, counts, whole, i):
    far = []
    for m in range(2):
        for p in range(place.slots):
            j = place.column(ids, m, i, p)
            far.append(split(whole[j] * place.weight(j, counts, m, i, p)))
    at = slice(i * len(far) * pair.shape[1] // 2, (i + 1) * len(far) * pair.shape[1] // 2)
    return narrow_product(joined(far, 1), pair[at], low[at])


def fill(place, messages, products, tiles, own):
    n = place.block_rows
    for i in range(n):
        tile = tiles[place.tile(i)]
        for peer, out in zip(place.peers, messages):
            out[place.tile(i)] = jnp.where(place.row < peer, products[peer * n + i], tile)
        own[place.tile(i)] = products[place.first_row + i]


def load_kernel(blocks, ids, counts, start, held, ids_s, counts_s, tiles, sems):
    size, columns = blocks.shape[2], start.shape[0]
    copies = [
        pltpu.make_async_copy(blocks, held, sems.at[0]),
        pltpu.make_async_copy(ids, ids_s, sems.at[1]),
        pltpu.make_async_copy(counts, counts_s, sems.at[2]),
    ]
    for i in range(blocks.shape[0]):
        source = start.at[:, i * size : (i + 1) * size]
        copies.append(pltpu.make_async_copy(source, tiles.at[i * columns : (i + 1) * columns], sems.at[3 + i]))
    for copy in copies:
        copy.start()
    for copy in copies:
        copy.wait()


def own_kernel(rows, held, ids, counts, tiles, products):
    place = Place(rows, *held.shape[:2], products.shape[1])
    size = products.shape[2]
    products[...] = jnp.zeros_like(products)
    for i in range(place.block_rows):
        stored = stacked_blocks([held[i, p] for p in range(place.slots)])
        value = shallow_product(split(tiles[place.tile(i)]), *stored)
        for p in range(place.slots):
            j = ids[i, p]
            products[j] += value[:, p * size : (p + 1) * size] * place.weight(j, counts, place.odd, i, p)


def first_kernel(rows, other, other_ids, counts, tiles, started, *refs):
    messages, (own, products) = refs[:-2], refs[-2:]
    size = products.shape[2]
    place = Place(rows, *other.shape[:2], products.shape[1])
    terms = []
    for i in range(place.block_rows):
        stored = stacked_blocks([other[i, p] for p in range(place.slots)])
        value = shallow_product(split(tiles[place.tile(i)]), *stored)
        for p in range(place.slots):
            used = (place.part + 1 - 2 * place.odd) * place.slots + p < counts[i]
            j = jnp.broadcast_to(other_ids[i : i + 1, p : p + 1], (8, size))
            c = jnp.where(j == place.first_row + i, 0.5, 1.0)
            terms.append((jnp.where(used, j, -1), c, value[:, p * size : (p + 1) * size]))
    copies = place.columns // 8
    for block in range(products.shape[0]):
        total = jnp.zeros_like(started[block])
        for j, c, value in terms:
            total += jnp.concatenate([jnp.where(j == block, c, 0.0)] * copies, axis=0) * value
        products[block] = started[block] + total
    fill(place, messages, products, tiles, own)


def split_kernel(held, other, other_ids, after, direct_pair, direct_low, pair, low, other_s, sem):
    block_rows, slots, size, _ = held.shape
    odd = lax.axis_index("nbr") & 1
    copy = pltpu.make_async_copy(other_ids, other_s, sem.at[0])
    copy.start()
    at = 0
    for i in range(block_rows):
        stored = [jnp.where(odd == m, held[i, p], other[i, p]) for m in range(2) for p in range(slots)]
        for b in stored:
            high, middle, rest = split(b.T)
            direct_pair[at : at + size, :size] = high
            direct_pair[at : at + size, size:] = middle
            direct_low[at : at + size] = rest
            at += size
        pair[2 * i * size : 2 * (i + 1) * size], low[i * size : (i + 1) * size] = stacked_blocks(stored)
    copy.wait()


def direct_kernel(rows, block_rows, slots, pair, low, ids, other_ids, counts, own, tiles, *refs):
    half = rows // 2
    received, handed, refs = refs[:half], refs[half : rows - 1], refs[rows - 1 :]
    *gram, whole = refs
    n, columns = block_rows, whole.shape[1]
    place = Place(rows, block_rows, slots, columns)
    for i in range(n):
        whole[place.first_row + i] = tiles[place.tile(i)]
        for peer, message in zip(place.peers + place.others_peers, received + handed):
            whole[peer * n + i] = message[place.tile(i)]
    if len(gram) == 1:
        (out,) = gram
    else:
        mine, out, total = gram
        tall = n * columns
        total[...] = tree(place.by_distance(mine[...], [m[tall:] for m in received], [m[tall:] for m in handed]))
    for i in range(n):
        at = place.tile(i)
        arrived = place.by_distance(own[at], [m[at] for m in received], [m[at] for m in handed])
        value = arrived[0]
        for s in range(1, rows):
            value += jnp.where(place.row > (place.row ^ s), arrived[s], 0.0)
        out[at] = value + direct_products(place, pair, low, (ids, other_ids), counts, whole, i)


def second_kernel(rows, parts, block_rows, slots, pair, low, ids, other_ids, counts, *refs):
    images, refs = refs[:parts], refs[parts:]
    messages, (own, tiles, gram, products) = refs[: rows // 2], refs[rows // 2 :]
    n, columns, size = block_rows, products.shape[1], products.shape[2]
    place = Place(rows, block_rows, slots, columns)
    tiles[...] = tree([image[...] for image in images])
    products[...] = jnp.zeros_like(products)
    for i in range(n):
        value = shallow_product(
            split(tiles[place.tile(i)]),
            pair[2 * i * size : 2 * (i + 1) * size],
            low[i * size : (i + 1) * size],
        )
        scatter(place, value, (ids, other_ids), counts, i, products)
    fill(place, messages, products, tiles, own)
    whole = joined([split(tiles[place.tile(i)]) for i in range(n)], 1)
    packed = folded(product(whole, whole, 1), size)
    gram[...] = packed
    for message in messages:
        message[n * columns :] = packed


def eliminated(gram, rest):
    n, width = gram.shape[0], rest.shape[1]
    groups = [[gram[g : g + 8], rest[g : g + 8]] for g in range(0, n, 8)]
    height = lax.broadcasted_iota(jnp.int32, (8, 1), 0)
    for first in range(0, n, PANEL):
        columns = [
            [jnp.broadcast_to(group[0][:, first + t : first + t + 1], (8, 128)) for group in groups]
            for t in range(PANEL)
        ]
        for t in range(PANEL):
            k = first + t
            gk, sk = k // 8, k % 8
            pivot = columns[t][gk][sk : sk + 1]
            inverse = 1.0 / pivot
            root = lax.rsqrt(pivot)
            source = [x[sk : sk + 1] for x in groups[gk]]
            steps = {}
            for g in range(gk, len(groups)):
                m = columns[t][g] * inverse
                steps[g] = jnp.where(height > sk, m, 0.0) if g == gk else m
            for u in range(t + 1, PANEL):
                head = columns[u][gk][sk : sk + 1]
                for g in range(gk, len(groups)):
                    columns[u][g] = columns[u][g] - steps[g] * head
            for g in range(gk, len(groups)):
                groups[g] = [x - wide(steps[g], x.shape[1]) * s for x, s in zip(groups[g], source)]
            groups[gk][1] = jnp.where(height == sk, groups[gk][1] * wide(root, width), groups[gk][1])
    return jnp.concatenate([group[1] for group in groups], axis=0)


def wide(x, lanes):
    if lanes <= x.shape[1]:
        return x[:, :lanes]
    return jnp.concatenate([x] * (lanes // x.shape[1]), axis=1)


def identity(n):
    rows = lax.broadcasted_iota(jnp.int32, (n, n), 0)
    return jnp.where(rows == lax.broadcasted_iota(jnp.int32, (n, n), 1), 1.0, 0.0)


def factor_kernel(total, gram, tiles, inverse, prior):
    columns = inverse.shape[0]
    lower = eliminated(unfolded(gram[...], columns) / total, identity(columns))
    inverse[...] = lower
    parts = [split(tiles[i : i + columns]) for i in range(0, tiles.shape[0], columns)]
    prior[...] = product(split(lower), joined(parts, 1))


def gram_kernel(inverse, prior, *refs):
    images, (image, out) = refs[:-2], refs[-2:]
    columns = inverse.shape[0]
    new = split(tree([part[...] for part in images]))
    rows = range(0, new[0].shape[0], columns)
    value = product(split(inverse[...]), [jnp.concatenate([x[i : i + columns] for i in rows], axis=1) for x in new])
    image[...] = value
    value = split(value)
    both = product(joined([value, split(prior[...])], 0), value, 1)
    out[...] = folded(both, out.shape[1])


def last_kernel(rows, total, image, mine, *refs):
    half = rows // 2
    received, handed, (basis, ritz) = refs[:half], refs[half : rows - 1], refs[rows - 1 :]
    columns = ritz.shape[0]
    place = Place(rows, 0, 0, columns)
    parts = place.by_distance(mine[...], [m[...] for m in received], [m[...] for m in handed])
    both = unfolded(tree(parts) / total, columns)
    ritz[...] = both[columns:]
    basis[...] = eliminated(both[:columns], image[...])


def body(blocks, partner_ids, counts, start):
    block_rows, slots, size, _ = blocks.shape
    columns = start.shape[1]
    rows, parts = lax.axis_size("row"), lax.axis_size("nbr")
    half = rows // 2
    all_blocks = block_rows * rows
    total = float(all_blocks * size)
    extra = columns * columns // size

    def flat(height):
        return jax.ShapeDtypeStruct((height, size), F32)

    tall = block_rows * columns
    tile, square = flat(tall), jax.ShapeDtypeStruct((columns, columns), F32)
    across = jax.ShapeDtypeStruct(start.shape[::-1], F32)
    table = pltpu.SMEM(partner_ids.shape, jnp.int32)
    work = pltpu.VMEM((all_blocks, columns, size), F32)

    def call(kernel, name, specs, outs, scratch=()):
        return pl.pallas_call(
            kernel,
            name=name,
            in_specs=specs,
            out_specs=[VMEM if isinstance(out, jax.ShapeDtypeStruct) else SMEM for out in outs],
            out_shape=outs,
            scratch_shapes=scratch,
            compiler_params=PARAMS,
        )

    def round_over_rows(messages):
        received = [swap_rows(m, 2 * k, 2 * k + 1) for k, m in enumerate(messages[1:], 1)]
        near = swap(messages[0], "row", 1)
        return [near] + received + [swap(m, "nbr", 1) for m in received]

    def sum_over_pairs(image):
        return [image] + [swap(image, "nbr", s) for s in range(2, parts, 2)]

    other = swap(blocks, "nbr", 1)
    other_ids = swap(partner_ids, "nbr", 1)
    held, ids, counts, tiles = call(
        load_kernel,
        "load",
        [HBM] * 4,
        [jax.ShapeDtypeStruct(blocks.shape, F32), table, pltpu.SMEM(counts.shape, jnp.int32), tile],
        [DMA((3 + block_rows,))],
    )(*[pltpu.with_memory_space_constraint(x, pltpu.HBM) for x in (blocks, partner_ids, counts, start.T)])
    (started,) = call(
        functools.partial(own_kernel, rows),
        "own_transposed",
        [VMEM, SMEM, SMEM, VMEM],
        [jax.ShapeDtypeStruct(work.shape, F32)],
    )(held, ids, counts, tiles)
    *messages, own = call(
        functools.partial(first_kernel, rows),
        "first_transposed",
        [VMEM, VMEM, SMEM, VMEM, VMEM],
        [tile] * (half + 1),
        [work],
    )(other, other_ids, counts, tiles, started)
    index = [VMEM, VMEM, SMEM, SMEM, SMEM]
    arrived = round_over_rows(messages)
    deep = 2 * block_rows * slots * size
    wide_row = 2 * slots * size
    direct_pair, direct_low, pair, low, other_ids = call(
        split_kernel,
        "split",
        [VMEM] * 4,
        [
            jax.ShapeDtypeStruct((deep, 2 * size), BF16),
            jax.ShapeDtypeStruct((deep, size), BF16),
            jax.ShapeDtypeStruct((2 * block_rows * size, wide_row), BF16),
            jax.ShapeDtypeStruct((block_rows * size, wide_row), BF16),
            table,
        ],
        [DMA((1,))],
    )(held, other, other_ids, own)
    parted = (direct_pair, direct_low, ids, other_ids, counts)
    direct = functools.partial(direct_kernel, rows, block_rows, slots)
    (image,) = call(direct, "first_direct", index + [VMEM] * (rows + 1), [tile], [work])(
        *parted, own, tiles, *arrived
    )
    images = sum_over_pairs(image)
    *messages, own, tiles, gram = call(
        functools.partial(second_kernel, rows, parts // 2, block_rows, slots),
        "second_transposed",
        index + [VMEM] * (parts // 2),
        [flat(tall + extra)] * half + [tile, tile, flat(extra)],
        [work],
    )(pair, low, ids, other_ids, counts, *images)
    arrived = round_over_rows(messages)
    image, gram = call(direct, "second_direct", index + [VMEM] * (rows + 2), [tile, flat(extra)], [work])(
        *parted, own, tiles, *arrived, gram
    )
    images = sum_over_pairs(image)
    inverse, prior = call(functools.partial(factor_kernel, total), "factor", [VMEM] * 2, [square, across])(gram, tiles)
    image, both = call(gram_kernel, "gram", [VMEM] * (parts // 2 + 2), [across, flat(2 * extra)])(
        inverse, prior, *images
    )
    arrived = round_over_rows([both] * half)
    basis, ritz = call(
        functools.partial(last_kernel, rows, total), "last", [VMEM] * (rows + 1), [across, square]
    )(image, both, *arrived)
    return basis.T, ritz


def solution(mesh):
    return jax.shard_map(
        body,
        mesh=mesh,
        in_specs=(
            P(("dom", "row"), "nbr", None, None),
            P(("dom", "row"), "nbr"),
            P(("dom", "row")),
            P(("dom", "row"), None),
        ),
        out_specs=(P(("dom", "row"), None), P("dom", None)),
        check_vma=False,
    )
```

```python
import functools

import jax
import jax.numpy as jnp
from jax import lax
from jax.experimental import pallas as pl
from jax.experimental.pallas import tpu as pltpu
from jax.sharding import PartitionSpec as P

F32 = jnp.float32
BF16 = jnp.bfloat16
VMEM = pl.BlockSpec(memory_space=pltpu.VMEM)
SMEM = pl.BlockSpec(memory_space=pltpu.SMEM)
HBM = pl.BlockSpec(memory_space=pltpu.HBM)
DMA = pltpu.SemaphoreType.DMA
PARAMS = pltpu.CompilerParams(vmem_limit_bytes=8 * 2**20)
PANEL = 16


def tree(parts):
    while len(parts) > 1:
        parts = [parts[i] + parts[i + 1] for i in range(0, len(parts), 2)]
    return parts[0]


def split(x):
    high = x.astype(BF16)
    rest = x - high.astype(F32)
    middle = rest.astype(BF16)
    return high, middle, (rest - middle.astype(F32)).astype(BF16)


def dot(a, b, contract=0):
    return lax.dot_general(a, b, (((1,), (contract,)), ((), ())), preferred_element_type=F32)


def product(a_parts, b_parts, contract=0):
    n = a_parts[0].shape[0]
    stacked = jnp.concatenate(a_parts, axis=0)
    high = dot(stacked, b_parts[0], contract)
    middle = dot(stacked[: 2 * n], b_parts[1], contract)
    low = dot(a_parts[0], b_parts[2], contract)
    return high[:n] + ((high[n : 2 * n] + middle[:n]) + ((high[2 * n :] + middle[n:]) + low))


def shallow_product(a_parts, b_pair, b_low):
    n = a_parts[0].shape[0]
    stacked = jnp.concatenate(a_parts, axis=0)
    most = dot(jnp.concatenate([stacked, stacked], axis=1), b_pair)
    low = dot(a_parts[0], b_low)
    return most[:n] + (most[n : 2 * n] + (most[2 * n :] + low))


def narrow_product(a_parts, b_pair, b_low):
    n, width = a_parts[0].shape[0], b_low.shape[1]
    most = dot(jnp.concatenate(a_parts, axis=0), b_pair)
    high, middle = most[:, :width], most[:, width:]
    low = dot(a_parts[0], b_low)
    return high[:n] + ((high[n : 2 * n] + middle[:n]) + ((high[2 * n :] + middle[n : 2 * n]) + low))


def joined(parts, axis):
    return [jnp.concatenate(level, axis=axis) for level in zip(*parts)]


def folded(x, lanes):
    fold = lanes // x.shape[1]
    height = x.shape[0] // fold
    return jnp.concatenate([x[g * height : (g + 1) * height] for g in range(fold)], axis=1)


def unfolded(x, columns):
    return jnp.concatenate([x[:, g : g + columns] for g in range(0, x.shape[1], columns)], axis=0)


def swap(x, axis, distance):
    return lax.ppermute(x, axis, [(i, i ^ distance) for i in range(lax.axis_size(axis))])


def swap_rows(x, even, odd, across=0):
    rows, parts = lax.axis_size("row"), lax.axis_size("nbr")
    pairs = [
        (r * parts + n, (r ^ (odd if n % 2 else even)) * parts + (n ^ across)) for r in range(rows) for n in range(parts)
    ]
    return lax.ppermute(x, ("row", "nbr"), pairs)


class Place:
    def __init__(self, rows, block_rows, slots, columns):
        self.row = lax.axis_index("row")
        self.part = lax.axis_index("nbr")
        self.odd = self.part & 1
        self.block_rows, self.slots = block_rows, slots
        self.first_row = self.row * self.block_rows
        self.peers = [self.row ^ (k + self.odd) for k in range(1, rows - 1, 2)] + [self.row ^ (rows - 1)]
        self.others_peers = [self.row ^ (k + 1 - self.odd) for k in range(1, rows - 1, 2)]
        self.columns = columns

    def column(self, ids, m, i, p):
        own, other = ids
        return jnp.where(self.odd == m, own[i, p], other[i, p])

    def weight(self, column, counts, m, i, p):
        used = (self.part - self.odd + m) * self.slots + p < counts[i]
        return jnp.where(used, jnp.where(column == self.first_row + i, 0.5, 1.0), 0.0).astype(F32)

    def tile(self, i):
        return slice(i * self.columns, (i + 1) * self.columns)

    def by_distance(self, mine, received, handed):
        both = [(jnp.where(self.odd == 0, a, b), jnp.where(self.odd == 0, b, a)) for a, b in zip(received, handed)]
        return [mine] + [x for pair in both for x in pair] + [received[-1]]


def stacked_blocks(blocks):
    high, middle, low = joined([split(b) for b in blocks], 1)
    return jnp.concatenate([high, middle], axis=0), low


def scatter(place, value, ids, counts, i, out):
    size = out.shape[2]
    for m in range(2):
        for p in range(place.slots):
            at = (m * place.slots + p) * size
            j = place.column(ids, m, i, p)
            out[j] += value[:, at : at + size] * place.weight(j, counts, m, i, p)


def direct_products(place, pair, low, ids, counts, whole, i):
    far = []
    for m in range(2):
        for p in range(place.slots):
            j = place.column(ids, m, i, p)
            far.append(split(whole[j] * place.weight(j, counts, m, i, p)))
    at = slice(i * len(far) * pair.shape[1] // 2, (i + 1) * len(far) * pair.shape[1] // 2)
    return narrow_product(joined(far, 1), pair[at], low[at])


def fill(place, messages, products, tiles, own):
    n = place.block_rows
    for i in range(n):
        tile = tiles[place.tile(i)]
        for peer, out in zip(place.peers, messages):
            out[place.tile(i)] = jnp.where(place.row < peer, products[peer * n + i], tile)
        own[place.tile(i)] = products[place.first_row + i]


def load_kernel(blocks, ids, counts, start, held, ids_s, counts_s, tiles, sems):
    size, columns = blocks.shape[2], start.shape[0]
    copies = [
        pltpu.make_async_copy(blocks, held, sems.at[0]),
        pltpu.make_async_copy(ids, ids_s, sems.at[1]),
        pltpu.make_async_copy(counts, counts_s, sems.at[2]),
    ]
    for i in range(blocks.shape[0]):
        source = start.at[:, i * size : (i + 1) * size]
        copies.append(pltpu.make_async_copy(source, tiles.at[i * columns : (i + 1) * columns], sems.at[3 + i]))
    for copy in copies:
        copy.start()
    for copy in copies:
        copy.wait()


def own_kernel(rows, held, ids, counts, tiles, products):
    place = Place(rows, *held.shape[:2], products.shape[1])
    size = products.shape[2]
    products[...] = jnp.zeros_like(products)
    for i in range(place.block_rows):
        stored = stacked_blocks([held[i, p] for p in range(place.slots)])
        value = shallow_product(split(tiles[place.tile(i)]), *stored)
        for p in range(place.slots):
            j = ids[i, p]
            products[j] += value[:, p * size : (p + 1) * size] * place.weight(j, counts, place.odd, i, p)


def first_kernel(rows, other, other_ids, counts, tiles, started, *refs):
    messages, (own, products) = refs[:-2], refs[-2:]
    size = products.shape[2]
    place = Place(rows, *other.shape[:2], products.shape[1])
    terms = []
    for i in range(place.block_rows):
        stored = stacked_blocks([other[i, p] for p in range(place.slots)])
        value = shallow_product(split(tiles[place.tile(i)]), *stored)
        for p in range(place.slots):
            used = (place.part + 1 - 2 * place.odd) * place.slots + p < counts[i]
            j = jnp.broadcast_to(other_ids[i : i + 1, p : p + 1], (8, size))
            c = jnp.where(j == place.first_row + i, 0.5, 1.0)
            terms.append((jnp.where(used, j, -1), c, value[:, p * size : (p + 1) * size]))
    copies = place.columns // 8
    for block in range(products.shape[0]):
        total = jnp.zeros_like(started[block])
        for j, c, value in terms:
            total += jnp.concatenate([jnp.where(j == block, c, 0.0)] * copies, axis=0) * value
        products[block] = started[block] + total
    fill(place, messages, products, tiles, own)


def split_kernel(held, other, other_ids, after, direct_pair, direct_low, pair, low, other_s, sem):
    block_rows, slots, size, _ = held.shape
    odd = lax.axis_index("nbr") & 1
    copy = pltpu.make_async_copy(other_ids, other_s, sem.at[0])
    copy.start()
    at = 0
    for i in range(block_rows):
        stored = [jnp.where(odd == m, held[i, p], other[i, p]) for m in range(2) for p in range(slots)]
        for b in stored:
            high, middle, rest = split(b.T)
            direct_pair[at : at + size, :size] = high
            direct_pair[at : at + size, size:] = middle
            direct_low[at : at + size] = rest
            at += size
        pair[2 * i * size : 2 * (i + 1) * size], low[i * size : (i + 1) * size] = stacked_blocks(stored)
    copy.wait()


def direct_kernel(rows, block_rows, slots, pair, low, ids, other_ids, counts, own, tiles, *refs):
    half = rows // 2
    received, handed, refs = refs[:half], refs[half : rows - 1], refs[rows - 1 :]
    *gram, whole = refs
    n, columns = block_rows, whole.shape[1]
    place = Place(rows, block_rows, slots, columns)
    for i in range(n):
        whole[place.first_row + i] = tiles[place.tile(i)]
        for peer, message in zip(place.peers + place.others_peers, received + handed):
            whole[peer * n + i] = message[place.tile(i)]
    if len(gram) == 1:
        (out,) = gram
    else:
        mine, out, total = gram
        tall = n * columns
        total[...] = tree(place.by_distance(mine[...], [m[tall:] for m in received], [m[tall:] for m in handed]))
    for i in range(n):
        at = place.tile(i)
        arrived = place.by_distance(own[at], [m[at] for m in received], [m[at] for m in handed])
        value = arrived[0]
        for s in range(1, rows):
            value += jnp.where(place.row > (place.row ^ s), arrived[s], 0.0)
        out[at] = value + direct_products(place, pair, low, (ids, other_ids), counts, whole, i)


def second_kernel(rows, parts, block_rows, slots, pair, low, ids, other_ids, counts, *refs):
    images, refs = refs[:parts], refs[parts:]
    messages, (own, tiles, gram, products) = refs[: rows // 2], refs[rows // 2 :]
    n, columns, size = block_rows, products.shape[1], products.shape[2]
    place = Place(rows, block_rows, slots, columns)
    tiles[...] = tree([image[...] for image in images])
    products[...] = jnp.zeros_like(products)
    for i in range(n):
        value = shallow_product(
            split(tiles[place.tile(i)]),
            pair[2 * i * size : 2 * (i + 1) * size],
            low[i * size : (i + 1) * size],
        )
        scatter(place, value, (ids, other_ids), counts, i, products)
    fill(place, messages, products, tiles, own)
    whole = joined([split(tiles[place.tile(i)]) for i in range(n)], 1)
    packed = folded(product(whole, whole, 1), size)
    gram[...] = packed
    for message in messages:
        message[n * columns :] = packed


def eliminated(gram, rest):
    n, width = gram.shape[0], rest.shape[1]
    groups = [[gram[g : g + 8], rest[g : g + 8]] for g in range(0, n, 8)]
    height = lax.broadcasted_iota(jnp.int32, (8, 1), 0)
    for first in range(0, n, PANEL):
        columns = [
            [jnp.broadcast_to(group[0][:, first + t : first + t + 1], (8, 128)) for group in groups]
            for t in range(PANEL)
        ]
        for t in range(PANEL):
            k = first + t
            gk, sk = k // 8, k % 8
            pivot = columns[t][gk][sk : sk + 1]
            inverse = 1.0 / pivot
            root = lax.rsqrt(pivot)
            source = [x[sk : sk + 1] for x in groups[gk]]
            steps = {}
            for g in range(gk, len(groups)):
                m = columns[t][g] * inverse
                steps[g] = jnp.where(height > sk, m, 0.0) if g == gk else m
            for u in range(t + 1, PANEL):
                head = columns[u][gk][sk : sk + 1]
                for g in range(gk, len(groups)):
                    columns[u][g] = columns[u][g] - steps[g] * head
            for g in range(gk, len(groups)):
                groups[g] = [x - wide(steps[g], x.shape[1]) * s for x, s in zip(groups[g], source)]
            groups[gk][1] = jnp.where(height == sk, groups[gk][1] * wide(root, width), groups[gk][1])
    return jnp.concatenate([group[1] for group in groups], axis=0)


def wide(x, lanes):
    if lanes <= x.shape[1]:
        return x[:, :lanes]
    return jnp.concatenate([x] * (lanes // x.shape[1]), axis=1)


def identity(n):
    rows = lax.broadcasted_iota(jnp.int32, (n, n), 0)
    return jnp.where(rows == lax.broadcasted_iota(jnp.int32, (n, n), 1), 1.0, 0.0)


def factor_kernel(total, gram, tiles, inverse, prior):
    columns = inverse.shape[0]
    lower = eliminated(unfolded(gram[...], columns) / total, identity(columns))
    inverse[...] = lower
    parts = [split(tiles[i : i + columns]) for i in range(0, tiles.shape[0], columns)]
    prior[...] = product(split(lower), joined(parts, 1))


def gram_kernel(inverse, prior, *refs):
    images, (image, out) = refs[:-2], refs[-2:]
    columns = inverse.shape[0]
    new = split(tree([part[...] for part in images]))
    rows = range(0, new[0].shape[0], columns)
    value = product(split(inverse[...]), [jnp.concatenate([x[i : i + columns] for i in rows], axis=1) for x in new])
    image[...] = value
    value = split(value)
    both = product(joined([value, split(prior[...])], 0), value, 1)
    out[...] = folded(both, out.shape[1])


def last_kernel(rows, total, image, mine, *refs):
    half = rows // 2
    received, handed, (basis, ritz) = refs[:half], refs[half : rows - 1], refs[rows - 1 :]
    columns = ritz.shape[0]
    place = Place(rows, 0, 0, columns)
    parts = place.by_distance(mine[...], [m[...] for m in received], [m[...] for m in handed])
    both = unfolded(tree(parts) / total, columns)
    ritz[...] = both[columns:]
    basis[...] = eliminated(both[:columns], image[...])


def body(blocks, partner_ids, counts, start):
    block_rows, slots, size, _ = blocks.shape
    columns = start.shape[1]
    rows, parts = lax.axis_size("row"), lax.axis_size("nbr")
    half = rows // 2
    all_blocks = block_rows * rows
    total = float(all_blocks * size)
    extra = columns * columns // size

    def flat(height):
        return jax.ShapeDtypeStruct((height, size), F32)

    tall = block_rows * columns
    tile, square = flat(tall), jax.ShapeDtypeStruct((columns, columns), F32)
    across = jax.ShapeDtypeStruct(start.shape[::-1], F32)
    table = pltpu.SMEM(partner_ids.shape, jnp.int32)
    work = pltpu.VMEM((all_blocks, columns, size), F32)

    def call(kernel, name, specs, outs, scratch=()):
        return pl.pallas_call(
            kernel,
            name=name,
            in_specs=specs,
            out_specs=[VMEM if isinstance(out, jax.ShapeDtypeStruct) else SMEM for out in outs],
            out_shape=outs,
            scratch_shapes=scratch,
            compiler_params=PARAMS,
        )

    def round_over_rows(messages):
        received = [swap_rows(m, 2 * k - 1, 2 * k) for k, m in enumerate(messages[:-1], 1)]
        last = swap_rows(messages[-1], rows - 1, rows - 1, 1)
        return received + [last] + [swap(m, "nbr", 1) for m in received]

    def sum_over_pairs(image):
        return [image] + [swap(image, "nbr", s + 0) for s in range(2, parts, 2)]

    other = swap(blocks, "nbr", 1)
    other_ids = swap(partner_ids, "nbr", 1)
    held, ids, counts, tiles = call(
        load_kernel,
        "load",
        [HBM] * 4,
        [jax.ShapeDtypeStruct(blocks.shape, F32), table, pltpu.SMEM(counts.shape, jnp.int32), tile],
        [DMA((3 + block_rows,))],
    )(*[pltpu.with_memory_space_constraint(x, pltpu.HBM) for x in (blocks, partner_ids, counts, start.T)])
    (started,) = call(
        functools.partial(own_kernel, rows),
        "own_transposed",
        [VMEM, SMEM, SMEM, VMEM],
        [jax.ShapeDtypeStruct(work.shape, F32)],
    )(held, ids, counts, tiles)
    *messages, own = call(
        functools.partial(first_kernel, rows),
        "first_transposed",
        [VMEM, VMEM, SMEM, VMEM, VMEM],
        [tile] * (half + 1),
        [work],
    )(other, other_ids, counts, tiles, started)
    index = [VMEM, VMEM, SMEM, SMEM, SMEM]
    arrived = round_over_rows(messages)
    deep = 2 * block_rows * slots * size
    wide_row = 2 * slots * size
    direct_pair, direct_low, pair, low, other_ids = call(
        split_kernel,
        "split",
        [VMEM] * 4,
        [
            jax.ShapeDtypeStruct((deep, 2 * size), BF16),
            jax.ShapeDtypeStruct((deep, size), BF16),
            jax.ShapeDtypeStruct((2 * block_rows * size, wide_row), BF16),
            jax.ShapeDtypeStruct((block_rows * size, wide_row), BF16),
            table,
        ],
        [DMA((1,))],
    )(held, other, other_ids, own)
    parted = (direct_pair, direct_low, ids, other_ids, counts)
    direct = functools.partial(direct_kernel, rows, block_rows, slots)
    (image,) = call(direct, "first_direct", index + [VMEM] * (rows + 1), [tile], [work])(
        *parted, own, tiles, *arrived
    )
    images = sum_over_pairs(image)
    *messages, own, tiles, gram = call(
        functools.partial(second_kernel, rows, parts // 2, block_rows, slots),
        "second_transposed",
        index + [VMEM] * (parts // 2),
        [flat(tall + extra)] * half + [tile, tile, flat(extra)],
        [work],
    )(pair, low, ids, other_ids, counts, *images)
    arrived = round_over_rows(messages)
    image, gram = call(direct, "second_direct", index + [VMEM] * (rows + 2), [tile, flat(extra)], [work])(
        *parted, own, tiles, *arrived, gram
    )
    images = sum_over_pairs(image)
    inverse, prior = call(functools.partial(factor_kernel, total), "factor", [VMEM] * 2, [square, across])(gram, tiles)
    image, both = call(gram_kernel, "gram", [VMEM] * (parts // 2 + 2), [across, flat(2 * extra)])(
        inverse, prior, *images
    )
    arrived = round_over_rows([both] * half)
    basis, ritz = call(
        functools.partial(last_kernel, rows, total), "last", [VMEM] * (rows + 1), [across, square]
    )(image, both, *arrived)
    return basis.T, ritz


def solution(mesh):
    return jax.shard_map(
        body,
        mesh=mesh,
        in_specs=(
            P(("dom", "row"), "nbr", None, None),
            P(("dom", "row"), "nbr"),
            P(("dom", "row")),
            P(("dom", "row"), None),
        ),
        out_specs=(P(("dom", "row"), None), P("dom", None)),
        check_vma=False,
    )
```

```python
import functools

import jax
import jax.numpy as jnp
from jax import lax
from jax.experimental import pallas as pl
from jax.experimental.pallas import tpu as pltpu
from jax.sharding import PartitionSpec as P

F32 = jnp.float32
BF16 = jnp.bfloat16
VMEM = pl.BlockSpec(memory_space=pltpu.VMEM)
SMEM = pl.BlockSpec(memory_space=pltpu.SMEM)
HBM = pl.BlockSpec(memory_space=pltpu.HBM)
DMA = pltpu.SemaphoreType.DMA
PARAMS = pltpu.CompilerParams(vmem_limit_bytes=8 * 2**20)
PANEL = 16


def tree(parts):
    while len(parts) > 1:
        parts = [parts[i] + parts[i + 1] for i in range(0, len(parts), 2)]
    return parts[0]


def split(x):
    high = x.astype(BF16)
    rest = x - high.astype(F32)
    middle = rest.astype(BF16)
    return high, middle, (rest - middle.astype(F32)).astype(BF16)


def dot(a, b, contract=0):
    return lax.dot_general(a, b, (((1,), (contract,)), ((), ())), preferred_element_type=F32)


def product(a_parts, b_parts, contract=0):
    n = a_parts[0].shape[0]
    stacked = jnp.concatenate(a_parts, axis=0)
    high = dot(stacked, b_parts[0], contract)
    middle = dot(stacked[: 2 * n], b_parts[1], contract)
    low = dot(a_parts[0], b_parts[2], contract)
    return high[:n] + ((high[n : 2 * n] + middle[:n]) + ((high[2 * n :] + middle[n:]) + low))


def shallow_product(a_parts, b_pair, b_low):
    n = a_parts[0].shape[0]
    stacked = jnp.concatenate(a_parts, axis=0)
    most = dot(jnp.concatenate([stacked, stacked], axis=1), b_pair)
    low = dot(a_parts[0], b_low)
    return most[:n] + (most[n : 2 * n] + (most[2 * n :] + low))


def narrow_product(a_parts, b_pair, b_low):
    n, width = a_parts[0].shape[0], b_low.shape[1]
    most = dot(jnp.concatenate(a_parts, axis=0), b_pair)
    high, middle = most[:, :width], most[:, width:]
    low = dot(a_parts[0], b_low)
    return high[:n] + ((high[n : 2 * n] + middle[:n]) + ((high[2 * n :] + middle[n : 2 * n]) + low))


def joined(parts, axis):
    return [jnp.concatenate(level, axis=axis) for level in zip(*parts)]


def folded(x, lanes):
    fold = lanes // x.shape[1]
    height = x.shape[0] // fold
    return jnp.concatenate([x[g * height : (g + 1) * height] for g in range(fold)], axis=1)


def unfolded(x, columns):
    return jnp.concatenate([x[:, g : g + columns] for g in range(0, x.shape[1], columns)], axis=0)


def swap(x, axis, distance):
    return lax.ppermute(x, axis, [(i, i ^ distance) for i in range(lax.axis_size(axis))])


def swap_rows(x, even, odd, across=0):
    rows, parts = lax.axis_size("row"), lax.axis_size("nbr")
    pairs = [
        (r * parts + n, (r ^ (odd if n % 2 else even)) * parts + (n ^ across)) for r in range(rows) for n in range(parts)
    ]
    return lax.ppermute(x, ("row", "nbr"), pairs)


def shares(rows, common):
    rest = [d for d in range(1, rows) if d != common]
    return list(zip(rest[::2], rest[1::2]))


class Place:
    def __init__(self, rows, block_rows, slots, columns, common=None):
        self.row = lax.axis_index("row")
        self.part = lax.axis_index("nbr")
        self.odd = self.part & 1
        self.block_rows, self.slots = block_rows, slots
        self.first_row = self.row * self.block_rows
        self.rows, self.common = rows, rows - 1 if common is None else common
        pairs = shares(rows, self.common)
        self.peers = [self.row ^ jnp.where(self.odd == 0, a, b) for a, b in pairs] + [self.row ^ self.common]
        self.others_peers = [self.row ^ jnp.where(self.odd == 0, b, a) for a, b in pairs]
        self.columns = columns

    def column(self, ids, m, i, p):
        own, other = ids
        return jnp.where(self.odd == m, own[i, p], other[i, p])

    def weight(self, column, counts, m, i, p):
        used = (self.part - self.odd + m) * self.slots + p < counts[i]
        return jnp.where(used, jnp.where(column == self.first_row + i, 0.5, 1.0), 0.0).astype(F32)

    def tile(self, i):
        return slice(i * self.columns, (i + 1) * self.columns)

    def by_distance(self, mine, received, handed):
        ordered = {0: mine, self.common: received[-1]}
        for (even, odd), a, b in zip(shares(self.rows, self.common), received, handed):
            ordered[even], ordered[odd] = jnp.where(self.odd == 0, a, b), jnp.where(self.odd == 0, b, a)
        return [ordered[d] for d in range(self.rows)]


def stacked_blocks(blocks):
    high, middle, low = joined([split(b) for b in blocks], 1)
    return jnp.concatenate([high, middle], axis=0), low


def scatter(place, value, ids, counts, i, out):
    size = out.shape[2]
    for m in range(2):
        for p in range(place.slots):
            at = (m * place.slots + p) * size
            j = place.column(ids, m, i, p)
            out[j] += value[:, at : at + size] * place.weight(j, counts, m, i, p)


def direct_products(place, pair, low, ids, counts, whole, i):
    far = []
    for m in range(2):
        for p in range(place.slots):
            j = place.column(ids, m, i, p)
            far.append(split(whole[j] * place.weight(j, counts, m, i, p)))
    at = slice(i * len(far) * pair.shape[1] // 2, (i + 1) * len(far) * pair.shape[1] // 2)
    return narrow_product(joined(far, 1), pair[at], low[at])


def fill(place, messages, products, tiles, own):
    n = place.block_rows
    for i in range(n):
        tile = tiles[place.tile(i)]
        for peer, out in zip(place.peers, messages):
            out[place.tile(i)] = jnp.where(place.row < peer, products[peer * n + i], tile)
        own[place.tile(i)] = products[place.first_row + i]


def load_kernel(blocks, ids, counts, start, held, ids_s, counts_s, tiles, sems):
    size, columns = blocks.shape[2], start.shape[0]
    copies = [
        pltpu.make_async_copy(blocks, held, sems.at[0]),
        pltpu.make_async_copy(ids, ids_s, sems.at[1]),
        pltpu.make_async_copy(counts, counts_s, sems.at[2]),
    ]
    for i in range(blocks.shape[0]):
        source = start.at[:, i * size : (i + 1) * size]
        copies.append(pltpu.make_async_copy(source, tiles.at[i * columns : (i + 1) * columns], sems.at[3 + i]))
    for copy in copies:
        copy.start()
    for copy in copies:
        copy.wait()


def own_kernel(rows, held, ids, counts, tiles, products):
    place = Place(rows, *held.shape[:2], products.shape[1])
    size = products.shape[2]
    products[...] = jnp.zeros_like(products)
    for i in range(place.block_rows):
        stored = stacked_blocks([held[i, p] for p in range(place.slots)])
        value = shallow_product(split(tiles[place.tile(i)]), *stored)
        for p in range(place.slots):
            j = ids[i, p]
            products[j] += value[:, p * size : (p + 1) * size] * place.weight(j, counts, place.odd, i, p)


def first_kernel(rows, other, other_ids, counts, tiles, started, *refs):
    messages, (own, products) = refs[:-2], refs[-2:]
    size = products.shape[2]
    place = Place(rows, *other.shape[:2], products.shape[1])
    terms = []
    for i in range(place.block_rows):
        stored = stacked_blocks([other[i, p] for p in range(place.slots)])
        value = shallow_product(split(tiles[place.tile(i)]), *stored)
        for p in range(place.slots):
            used = (place.part + 1 - 2 * place.odd) * place.slots + p < counts[i]
            j = jnp.broadcast_to(other_ids[i : i + 1, p : p + 1], (8, size))
            c = jnp.where(j == place.first_row + i, 0.5, 1.0)
            terms.append((jnp.where(used, j, -1), c, value[:, p * size : (p + 1) * size]))
    copies = place.columns // 8
    for block in range(products.shape[0]):
        total = jnp.zeros_like(started[block])
        for j, c, value in terms:
            total += jnp.concatenate([jnp.where(j == block, c, 0.0)] * copies, axis=0) * value
        products[block] = started[block] + total
    fill(place, messages, products, tiles, own)


def split_kernel(held, other, other_ids, after, direct_pair, direct_low, pair, low, other_s, sem):
    block_rows, slots, size, _ = held.shape
    odd = lax.axis_index("nbr") & 1
    copy = pltpu.make_async_copy(other_ids, other_s, sem.at[0])
    copy.start()
    at = 0
    for i in range(block_rows):
        stored = [jnp.where(odd == m, held[i, p], other[i, p]) for m in range(2) for p in range(slots)]
        for b in stored:
            high, middle, rest = split(b.T)
            direct_pair[at : at + size, :size] = high
            direct_pair[at : at + size, size:] = middle
            direct_low[at : at + size] = rest
            at += size
        pair[2 * i * size : 2 * (i + 1) * size], low[i * size : (i + 1) * size] = stacked_blocks(stored)
    copy.wait()


def direct_kernel(rows, block_rows, slots, pair, low, ids, other_ids, counts, own, tiles, *refs):
    half = rows // 2
    received, handed, refs = refs[:half], refs[half : rows - 1], refs[rows - 1 :]
    *gram, whole = refs
    n, columns = block_rows, whole.shape[1]
    place = Place(rows, block_rows, slots, columns)
    for i in range(n):
        whole[place.first_row + i] = tiles[place.tile(i)]
        for peer, message in zip(place.peers + place.others_peers, received + handed):
            whole[peer * n + i] = message[place.tile(i)]
    if len(gram) == 1:
        (out,) = gram
    else:
        mine, out, total = gram
        tall = n * columns
        total[...] = tree(place.by_distance(mine[...], [m[tall:] for m in received], [m[tall:] for m in handed]))
    for i in range(n):
        at = place.tile(i)
        arrived = place.by_distance(own[at], [m[at] for m in received], [m[at] for m in handed])
        value = arrived[0]
        for s in range(1, rows):
            value += jnp.where(place.row > (place.row ^ s), arrived[s], 0.0)
        out[at] = value + direct_products(place, pair, low, (ids, other_ids), counts, whole, i)


def second_kernel(rows, parts, block_rows, slots, pair, low, ids, other_ids, counts, *refs):
    images, refs = refs[:parts], refs[parts:]
    messages, (own, tiles, gram, products) = refs[: rows // 2], refs[rows // 2 :]
    n, columns, size = block_rows, products.shape[1], products.shape[2]
    place = Place(rows, block_rows, slots, columns)
    tiles[...] = tree([image[...] for image in images])
    products[...] = jnp.zeros_like(products)
    for i in range(n):
        value = shallow_product(
            split(tiles[place.tile(i)]),
            pair[2 * i * size : 2 * (i + 1) * size],
            low[i * size : (i + 1) * size],
        )
        scatter(place, value, (ids, other_ids), counts, i, products)
    fill(place, messages, products, tiles, own)
    whole = joined([split(tiles[place.tile(i)]) for i in range(n)], 1)
    packed = folded(product(whole, whole, 1), size)
    gram[...] = packed
    for message in messages:
        message[n * columns :] = packed


def eliminated(gram, rest):
    n, width = gram.shape[0], rest.shape[1]
    groups = [[gram[g : g + 8], rest[g : g + 8]] for g in range(0, n, 8)]
    height = lax.broadcasted_iota(jnp.int32, (8, 1), 0)
    for first in range(0, n, PANEL):
        columns = [
            [jnp.broadcast_to(group[0][:, first + t : first + t + 1], (8, 128)) for group in groups]
            for t in range(PANEL)
        ]
        for t in range(PANEL):
            k = first + t
            gk, sk = k // 8, k % 8
            pivot = columns[t][gk][sk : sk + 1]
            inverse = 1.0 / pivot
            root = lax.rsqrt(pivot)
            source = [x[sk : sk + 1] for x in groups[gk]]
            steps = {}
            for g in range(gk, len(groups)):
                m = columns[t][g] * inverse
                steps[g] = jnp.where(height > sk, m, 0.0) if g == gk else m
            for u in range(t + 1, PANEL):
                head = columns[u][gk][sk : sk + 1]
                for g in range(gk, len(groups)):
                    columns[u][g] = columns[u][g] - steps[g] * head
            for g in range(gk, len(groups)):
                groups[g] = [x - wide(steps[g], x.shape[1]) * s for x, s in zip(groups[g], source)]
            groups[gk][1] = jnp.where(height == sk, groups[gk][1] * wide(root, width), groups[gk][1])
    return jnp.concatenate([group[1] for group in groups], axis=0)


def wide(x, lanes):
    if lanes <= x.shape[1]:
        return x[:, :lanes]
    return jnp.concatenate([x] * (lanes // x.shape[1]), axis=1)


def identity(n):
    rows = lax.broadcasted_iota(jnp.int32, (n, n), 0)
    return jnp.where(rows == lax.broadcasted_iota(jnp.int32, (n, n), 1), 1.0, 0.0)


def factor_kernel(total, gram, tiles, inverse, prior):
    columns = inverse.shape[0]
    lower = eliminated(unfolded(gram[...], columns) / total, identity(columns))
    inverse[...] = lower
    parts = [split(tiles[i : i + columns]) for i in range(0, tiles.shape[0], columns)]
    prior[...] = product(split(lower), joined(parts, 1))


def gram_kernel(inverse, prior, *refs):
    images, (image, out) = refs[:-2], refs[-2:]
    columns = inverse.shape[0]
    new = split(tree([part[...] for part in images]))
    rows = range(0, new[0].shape[0], columns)
    value = product(split(inverse[...]), [jnp.concatenate([x[i : i + columns] for i in rows], axis=1) for x in new])
    image[...] = value
    value = split(value)
    both = product(joined([value, split(prior[...])], 0), value, 1)
    out[...] = folded(both, out.shape[1])


def last_kernel(rows, total, image, mine, *refs):
    half = rows // 2
    received, handed, (basis, ritz) = refs[:half], refs[half : rows - 1], refs[rows - 1 :]
    columns = ritz.shape[0]
    place = Place(rows, 0, 0, columns, rows - 2)
    parts = place.by_distance(mine[...], [m[...] for m in received], [m[...] for m in handed])
    both = unfolded(tree(parts) / total, columns)
    ritz[...] = both[columns:]
    basis[...] = eliminated(both[:columns], image[...])


def body(blocks, partner_ids, counts, start):
    block_rows, slots, size, _ = blocks.shape
    columns = start.shape[1]
    rows, parts = lax.axis_size("row"), lax.axis_size("nbr")
    half = rows // 2
    all_blocks = block_rows * rows
    total = float(all_blocks * size)
    extra = columns * columns // size

    def flat(height):
        return jax.ShapeDtypeStruct((height, size), F32)

    tall = block_rows * columns
    tile, square = flat(tall), jax.ShapeDtypeStruct((columns, columns), F32)
    across = jax.ShapeDtypeStruct(start.shape[::-1], F32)
    table = pltpu.SMEM(partner_ids.shape, jnp.int32)
    work = pltpu.VMEM((all_blocks, columns, size), F32)

    def call(kernel, name, specs, outs, scratch=()):
        return pl.pallas_call(
            kernel,
            name=name,
            in_specs=specs,
            out_specs=[VMEM if isinstance(out, jax.ShapeDtypeStruct) else SMEM for out in outs],
            out_shape=outs,
            scratch_shapes=scratch,
            compiler_params=PARAMS,
        )

    def round_over_rows(messages, common):
        received = [swap_rows(m, *pair) for m, pair in zip(messages, shares(rows, common))]
        last = swap_rows(messages[-1], common, common, 1)
        return received + [last] + [swap(m, "nbr", 1) for m in received]

    def sum_over_pairs(image):
        return [image] + [swap(image, "nbr", s + 0) for s in range(2, parts, 2)]

    other = swap(blocks, "nbr", 1)
    other_ids = swap(partner_ids, "nbr", 1)
    held, ids, counts, tiles = call(
        load_kernel,
        "load",
        [HBM] * 4,
        [jax.ShapeDtypeStruct(blocks.shape, F32), table, pltpu.SMEM(counts.shape, jnp.int32), tile],
        [DMA((3 + block_rows,))],
    )(*[pltpu.with_memory_space_constraint(x, pltpu.HBM) for x in (blocks, partner_ids, counts, start.T)])
    (started,) = call(
        functools.partial(own_kernel, rows),
        "own_transposed",
        [VMEM, SMEM, SMEM, VMEM],
        [jax.ShapeDtypeStruct(work.shape, F32)],
    )(held, ids, counts, tiles)
    *messages, own = call(
        functools.partial(first_kernel, rows),
        "first_transposed",
        [VMEM, VMEM, SMEM, VMEM, VMEM],
        [tile] * (half + 1),
        [work],
    )(other, other_ids, counts, tiles, started)
    index = [VMEM, VMEM, SMEM, SMEM, SMEM]
    arrived = round_over_rows(messages, rows - 1)
    deep = 2 * block_rows * slots * size
    wide_row = 2 * slots * size
    direct_pair, direct_low, pair, low, other_ids = call(
        split_kernel,
        "split",
        [VMEM] * 4,
        [
            jax.ShapeDtypeStruct((deep, 2 * size), BF16),
            jax.ShapeDtypeStruct((deep, size), BF16),
            jax.ShapeDtypeStruct((2 * block_rows * size, wide_row), BF16),
            jax.ShapeDtypeStruct((block_rows * size, wide_row), BF16),
            table,
        ],
        [DMA((1,))],
    )(held, other, other_ids, own)
    parted = (direct_pair, direct_low, ids, other_ids, counts)
    direct = functools.partial(direct_kernel, rows, block_rows, slots)
    (image,) = call(direct, "first_direct", index + [VMEM] * (rows + 1), [tile], [work])(
        *parted, own, tiles, *arrived
    )
    images = sum_over_pairs(image)
    *messages, own, tiles, gram = call(
        functools.partial(second_kernel, rows, parts // 2, block_rows, slots),
        "second_transposed",
        index + [VMEM] * (parts // 2),
        [flat(tall + extra)] * half + [tile, tile, flat(extra)],
        [work],
    )(pair, low, ids, other_ids, counts, *images)
    arrived = round_over_rows(messages, rows - 1)
    image, gram = call(direct, "second_direct", index + [VMEM] * (rows + 2), [tile, flat(extra)], [work])(
        *parted, own, tiles, *arrived, gram
    )
    images = sum_over_pairs(image)
    inverse, prior = call(functools.partial(factor_kernel, total), "factor", [VMEM] * 2, [square, across])(gram, tiles)
    image, both = call(gram_kernel, "gram", [VMEM] * (parts // 2 + 2), [across, flat(2 * extra)])(
        inverse, prior, *images
    )
    arrived = round_over_rows([both] * half, rows - 2)
    basis, ritz = call(
        functools.partial(last_kernel, rows, total), "last", [VMEM] * (rows + 1), [across, square]
    )(image, both, *arrived)
    return basis.T, ritz


def solution(mesh):
    return jax.shard_map(
        body,
        mesh=mesh,
        in_specs=(
            P(("dom", "row"), "nbr", None, None),
            P(("dom", "row"), "nbr"),
            P(("dom", "row")),
            P(("dom", "row"), None),
        ),
        out_specs=(P(("dom", "row"), None), P("dom", None)),
        check_vma=False,
    )
```

```python
import functools

import jax
import jax.numpy as jnp
from jax import lax
from jax.experimental import pallas as pl
from jax.experimental.pallas import tpu as pltpu
from jax.sharding import PartitionSpec as P

F32 = jnp.float32
BF16 = jnp.bfloat16
VMEM = pl.BlockSpec(memory_space=pltpu.VMEM)
SMEM = pl.BlockSpec(memory_space=pltpu.SMEM)
HBM = pl.BlockSpec(memory_space=pltpu.HBM)
DMA = pltpu.SemaphoreType.DMA
PARAMS = pltpu.CompilerParams(vmem_limit_bytes=8 * 2**20)
PANEL = 16


def tree(parts):
    while len(parts) > 1:
        parts = [parts[i] + parts[i + 1] for i in range(0, len(parts), 2)]
    return parts[0]


def split(x):
    high = x.astype(BF16)
    rest = x - high.astype(F32)
    middle = rest.astype(BF16)
    return high, middle, (rest - middle.astype(F32)).astype(BF16)


def dot(a, b, contract=0):
    return lax.dot_general(a, b, (((1,), (contract,)), ((), ())), preferred_element_type=F32)


def product(a_parts, b_parts, contract=0):
    n = a_parts[0].shape[0]
    stacked = jnp.concatenate(a_parts, axis=0)
    high = dot(stacked, b_parts[0], contract)
    middle = dot(stacked[: 2 * n], b_parts[1], contract)
    low = dot(a_parts[0], b_parts[2], contract)
    return high[:n] + ((high[n : 2 * n] + middle[:n]) + ((high[2 * n :] + middle[n:]) + low))


def shallow_product(a_parts, b_pair, b_low):
    n = a_parts[0].shape[0]
    stacked = jnp.concatenate(a_parts, axis=0)
    most = dot(jnp.concatenate([stacked, stacked], axis=1), b_pair)
    low = dot(a_parts[0], b_low)
    return most[:n] + (most[n : 2 * n] + (most[2 * n :] + low))


def narrow_product(a_parts, b_pair, b_low):
    n, width = a_parts[0].shape[0], b_low.shape[1]
    most = dot(jnp.concatenate(a_parts, axis=0), b_pair)
    high, middle = most[:, :width], most[:, width:]
    low = dot(a_parts[0], b_low)
    return high[:n] + ((high[n : 2 * n] + middle[:n]) + ((high[2 * n :] + middle[n : 2 * n]) + low))


def joined(parts, axis):
    return [jnp.concatenate(level, axis=axis) for level in zip(*parts)]


def folded(x, lanes):
    fold = lanes // x.shape[1]
    height = x.shape[0] // fold
    return jnp.concatenate([x[g * height : (g + 1) * height] for g in range(fold)], axis=1)


def unfolded(x, columns):
    return jnp.concatenate([x[:, g : g + columns] for g in range(0, x.shape[1], columns)], axis=0)


def swap(x, axis, distance):
    return lax.ppermute(x, axis, [(i, i ^ distance) for i in range(lax.axis_size(axis))])


def swap_rows(x, even, odd, across=None, alternate=False):
    rows, parts = lax.axis_size("row"), lax.axis_size("nbr")
    pairs = []
    for r in range(rows):
        for n in range(parts):
            d = odd if (n + alternate * bin(r).count("1")) % 2 else even
            m = n ^ (alternate * bin(d).count("1") % 2 if across is None else across)
            pairs.append((r * parts + n, (r ^ d) * parts + m))
    return lax.ppermute(x, ("row", "nbr"), pairs)


def shares(rows, common):
    rest = [d for d in range(1, rows) if d != common]
    return list(zip(rest[::2], rest[1::2]))


class Place:
    def __init__(self, rows, block_rows, slots, columns, common=None):
        self.row = lax.axis_index("row")
        self.part = lax.axis_index("nbr")
        self.odd = self.part & 1
        self.block_rows, self.slots = block_rows, slots
        self.first_row = self.row * self.block_rows
        self.rows, self.common = rows, rows - 1 if common is None else common
        pairs = shares(rows, self.common)
        self.role = self.odd
        for k in range(0 if common is None else (rows - 1).bit_length()):
            self.role = self.role ^ ((self.row >> k) & 1)
        self.peers = [self.row ^ jnp.where(self.role == 0, a, b) for a, b in pairs] + [self.row ^ self.common]
        self.others_peers = [self.row ^ jnp.where(self.role == 0, b, a) for a, b in pairs]
        self.columns = columns

    def column(self, ids, m, i, p):
        own, other = ids
        return jnp.where(self.odd == m, own[i, p], other[i, p])

    def weight(self, column, counts, m, i, p):
        used = (self.part - self.odd + m) * self.slots + p < counts[i]
        return jnp.where(used, jnp.where(column == self.first_row + i, 0.5, 1.0), 0.0).astype(F32)

    def tile(self, i):
        return slice(i * self.columns, (i + 1) * self.columns)

    def by_distance(self, mine, received, handed):
        ordered = {0: mine, self.common: received[-1]}
        for (even, odd), a, b in zip(shares(self.rows, self.common), received, handed):
            ordered[even], ordered[odd] = jnp.where(self.role == 0, a, b), jnp.where(self.role == 0, b, a)
        return [ordered[d] for d in range(self.rows)]


def stacked_blocks(blocks):
    high, middle, low = joined([split(b) for b in blocks], 1)
    return jnp.concatenate([high, middle], axis=0), low


def scatter(place, value, ids, counts, i, out):
    size = out.shape[2]
    for m in range(2):
        for p in range(place.slots):
            at = (m * place.slots + p) * size
            j = place.column(ids, m, i, p)
            out[j] += value[:, at : at + size] * place.weight(j, counts, m, i, p)


def direct_products(place, pair, low, ids, counts, whole, i):
    far = []
    for m in range(2):
        for p in range(place.slots):
            j = place.column(ids, m, i, p)
            far.append(split(whole[j] * place.weight(j, counts, m, i, p)))
    at = slice(i * len(far) * pair.shape[1] // 2, (i + 1) * len(far) * pair.shape[1] // 2)
    return narrow_product(joined(far, 1), pair[at], low[at])


def fill(place, messages, products, tiles, own):
    n = place.block_rows
    for i in range(n):
        tile = tiles[place.tile(i)]
        for peer, out in zip(place.peers, messages):
            out[place.tile(i)] = jnp.where(place.row < peer, products[peer * n + i], tile)
        own[place.tile(i)] = products[place.first_row + i]


def load_kernel(blocks, ids, counts, start, held, ids_s, counts_s, tiles, sems):
    size, columns = blocks.shape[2], start.shape[0]
    copies = [
        pltpu.make_async_copy(blocks, held, sems.at[0]),
        pltpu.make_async_copy(ids, ids_s, sems.at[1]),
        pltpu.make_async_copy(counts, counts_s, sems.at[2]),
    ]
    for i in range(blocks.shape[0]):
        source = start.at[:, i * size : (i + 1) * size]
        copies.append(pltpu.make_async_copy(source, tiles.at[i * columns : (i + 1) * columns], sems.at[3 + i]))
    for copy in copies:
        copy.start()
    for copy in copies:
        copy.wait()


def own_kernel(rows, held, ids, counts, tiles, products):
    place = Place(rows, *held.shape[:2], products.shape[1])
    size = products.shape[2]
    products[...] = jnp.zeros_like(products)
    for i in range(place.block_rows):
        stored = stacked_blocks([held[i, p] for p in range(place.slots)])
        value = shallow_product(split(tiles[place.tile(i)]), *stored)
        for p in range(place.slots):
            j = ids[i, p]
            products[j] += value[:, p * size : (p + 1) * size] * place.weight(j, counts, place.odd, i, p)


def first_kernel(rows, other, other_ids, counts, tiles, started, *refs):
    messages, (own, products) = refs[:-2], refs[-2:]
    size = products.shape[2]
    place = Place(rows, *other.shape[:2], products.shape[1])
    terms = []
    for i in range(place.block_rows):
        stored = stacked_blocks([other[i, p] for p in range(place.slots)])
        value = shallow_product(split(tiles[place.tile(i)]), *stored)
        for p in range(place.slots):
            used = (place.part + 1 - 2 * place.odd) * place.slots + p < counts[i]
            j = jnp.broadcast_to(other_ids[i : i + 1, p : p + 1], (8, size))
            c = jnp.where(j == place.first_row + i, 0.5, 1.0)
            terms.append((jnp.where(used, j, -1), c, value[:, p * size : (p + 1) * size]))
    copies = place.columns // 8
    for block in range(products.shape[0]):
        total = jnp.zeros_like(started[block])
        for j, c, value in terms:
            total += jnp.concatenate([jnp.where(j == block, c, 0.0)] * copies, axis=0) * value
        products[block] = started[block] + total
    fill(place, messages, products, tiles, own)


def split_kernel(held, other, other_ids, after, direct_pair, direct_low, pair, low, other_s, sem):
    block_rows, slots, size, _ = held.shape
    odd = lax.axis_index("nbr") & 1
    copy = pltpu.make_async_copy(other_ids, other_s, sem.at[0])
    copy.start()
    at = 0
    for i in range(block_rows):
        stored = [jnp.where(odd == m, held[i, p], other[i, p]) for m in range(2) for p in range(slots)]
        for b in stored:
            high, middle, rest = split(b.T)
            direct_pair[at : at + size, :size] = high
            direct_pair[at : at + size, size:] = middle
            direct_low[at : at + size] = rest
            at += size
        pair[2 * i * size : 2 * (i + 1) * size], low[i * size : (i + 1) * size] = stacked_blocks(stored)
    copy.wait()


def direct_kernel(rows, block_rows, slots, pair, low, ids, other_ids, counts, own, tiles, *refs):
    half = rows // 2
    received, handed, refs = refs[:half], refs[half : rows - 1], refs[rows - 1 :]
    *gram, whole = refs
    n, columns = block_rows, whole.shape[1]
    place = Place(rows, block_rows, slots, columns)
    for i in range(n):
        whole[place.first_row + i] = tiles[place.tile(i)]
        for peer, message in zip(place.peers + place.others_peers, received + handed):
            whole[peer * n + i] = message[place.tile(i)]
    if len(gram) == 1:
        (out,) = gram
    else:
        mine, out, total = gram
        tall = n * columns
        total[...] = tree(place.by_distance(mine[...], [m[tall:] for m in received], [m[tall:] for m in handed]))
    for i in range(n):
        at = place.tile(i)
        arrived = place.by_distance(own[at], [m[at] for m in received], [m[at] for m in handed])
        value = arrived[0]
        for s in range(1, rows):
            value += jnp.where(place.row > (place.row ^ s), arrived[s], 0.0)
        out[at] = value + direct_products(place, pair, low, (ids, other_ids), counts, whole, i)


def second_kernel(rows, parts, block_rows, slots, pair, low, ids, other_ids, counts, *refs):
    images, refs = refs[:parts], refs[parts:]
    messages, (own, tiles, gram, products) = refs[: rows // 2], refs[rows // 2 :]
    n, columns, size = block_rows, products.shape[1], products.shape[2]
    place = Place(rows, block_rows, slots, columns)
    tiles[...] = tree([image[...] for image in images])
    products[...] = jnp.zeros_like(products)
    for i in range(n):
        value = shallow_product(
            split(tiles[place.tile(i)]),
            pair[2 * i * size : 2 * (i + 1) * size],
            low[i * size : (i + 1) * size],
        )
        scatter(place, value, (ids, other_ids), counts, i, products)
    fill(place, messages, products, tiles, own)
    whole = joined([split(tiles[place.tile(i)]) for i in range(n)], 1)
    packed = folded(product(whole, whole, 1), size)
    gram[...] = packed
    for message in messages:
        message[n * columns :] = packed


def eliminated(gram, rest):
    n, width = gram.shape[0], rest.shape[1]
    groups = [[gram[g : g + 8], rest[g : g + 8]] for g in range(0, n, 8)]
    height = lax.broadcasted_iota(jnp.int32, (8, 1), 0)
    for first in range(0, n, PANEL):
        columns = [
            [jnp.broadcast_to(group[0][:, first + t : first + t + 1], (8, 128)) for group in groups]
            for t in range(PANEL)
        ]
        for t in range(PANEL):
            k = first + t
            gk, sk = k // 8, k % 8
            pivot = columns[t][gk][sk : sk + 1]
            inverse = 1.0 / pivot
            root = lax.rsqrt(pivot)
            source = [x[sk : sk + 1] for x in groups[gk]]
            steps = {}
            for g in range(gk, len(groups)):
                m = columns[t][g] * inverse
                steps[g] = jnp.where(height > sk, m, 0.0) if g == gk else m
            for u in range(t + 1, PANEL):
                head = columns[u][gk][sk : sk + 1]
                for g in range(gk, len(groups)):
                    columns[u][g] = columns[u][g] - steps[g] * head
            for g in range(gk, len(groups)):
                groups[g] = [x - wide(steps[g], x.shape[1]) * s for x, s in zip(groups[g], source)]
            groups[gk][1] = jnp.where(height == sk, groups[gk][1] * wide(root, width), groups[gk][1])
    return jnp.concatenate([group[1] for group in groups], axis=0)


def wide(x, lanes):
    if lanes <= x.shape[1]:
        return x[:, :lanes]
    return jnp.concatenate([x] * (lanes // x.shape[1]), axis=1)


def identity(n):
    rows = lax.broadcasted_iota(jnp.int32, (n, n), 0)
    return jnp.where(rows == lax.broadcasted_iota(jnp.int32, (n, n), 1), 1.0, 0.0)


def factor_kernel(total, gram, tiles, inverse, prior):
    columns = inverse.shape[0]
    lower = eliminated(unfolded(gram[...], columns) / total, identity(columns))
    inverse[...] = lower
    parts = [split(tiles[i : i + columns]) for i in range(0, tiles.shape[0], columns)]
    prior[...] = product(split(lower), joined(parts, 1))


def gram_kernel(inverse, prior, *refs):
    images, (image, out) = refs[:-2], refs[-2:]
    columns = inverse.shape[0]
    new = split(tree([part[...] for part in images]))
    rows = range(0, new[0].shape[0], columns)
    value = product(split(inverse[...]), [jnp.concatenate([x[i : i + columns] for i in rows], axis=1) for x in new])
    image[...] = value
    value = split(value)
    both = product(joined([value, split(prior[...])], 0), value, 1)
    out[...] = folded(both, out.shape[1])


def last_kernel(rows, total, image, mine, *refs):
    half = rows // 2
    received, handed, (basis, ritz) = refs[:half], refs[half : rows - 1], refs[rows - 1 :]
    columns = ritz.shape[0]
    place = Place(rows, 0, 0, columns, rows - 2)
    parts = place.by_distance(mine[...], [m[...] for m in received], [m[...] for m in handed])
    both = unfolded(tree(parts) / total, columns)
    ritz[...] = both[columns:]
    basis[...] = eliminated(both[:columns], image[...])


def body(blocks, partner_ids, counts, start):
    block_rows, slots, size, _ = blocks.shape
    columns = start.shape[1]
    rows, parts = lax.axis_size("row"), lax.axis_size("nbr")
    half = rows // 2
    all_blocks = block_rows * rows
    total = float(all_blocks * size)
    extra = columns * columns // size

    def flat(height):
        return jax.ShapeDtypeStruct((height, size), F32)

    tall = block_rows * columns
    tile, square = flat(tall), jax.ShapeDtypeStruct((columns, columns), F32)
    across = jax.ShapeDtypeStruct(start.shape[::-1], F32)
    table = pltpu.SMEM(partner_ids.shape, jnp.int32)
    work = pltpu.VMEM((all_blocks, columns, size), F32)

    def call(kernel, name, specs, outs, scratch=()):
        return pl.pallas_call(
            kernel,
            name=name,
            in_specs=specs,
            out_specs=[VMEM if isinstance(out, jax.ShapeDtypeStruct) else SMEM for out in outs],
            out_shape=outs,
            scratch_shapes=scratch,
            compiler_params=PARAMS,
        )

    def round_over_rows(messages, common):
        received = [swap_rows(m, *pair, alternate=common == rows - 2) for m, pair in zip(messages, shares(rows, common))]
        last = swap_rows(messages[-1], common, common, 1)
        return received + [last] + [swap(m, "nbr", 1) for m in received]

    def sum_over_pairs(image):
        return [image] + [swap(image, "nbr", s + 0) for s in range(2, parts, 2)]

    other = swap(blocks, "nbr", 1)
    other_ids = swap(partner_ids, "nbr", 1)
    held, ids, counts, tiles = call(
        load_kernel,
        "load",
        [HBM] * 4,
        [jax.ShapeDtypeStruct(blocks.shape, F32), table, pltpu.SMEM(counts.shape, jnp.int32), tile],
        [DMA((3 + block_rows,))],
    )(*[pltpu.with_memory_space_constraint(x, pltpu.HBM) for x in (blocks, partner_ids, counts, start.T)])
    (started,) = call(
        functools.partial(own_kernel, rows),
        "own_transposed",
        [VMEM, SMEM, SMEM, VMEM],
        [jax.ShapeDtypeStruct(work.shape, F32)],
    )(held, ids, counts, tiles)
    *messages, own = call(
        functools.partial(first_kernel, rows),
        "first_transposed",
        [VMEM, VMEM, SMEM, VMEM, VMEM],
        [tile] * (half + 1),
        [work],
    )(other, other_ids, counts, tiles, started)
    index = [VMEM, VMEM, SMEM, SMEM, SMEM]
    arrived = round_over_rows(messages, rows - 1)
    deep = 2 * block_rows * slots * size
    wide_row = 2 * slots * size
    direct_pair, direct_low, pair, low, other_ids = call(
        split_kernel,
        "split",
        [VMEM] * 4,
        [
            jax.ShapeDtypeStruct((deep, 2 * size), BF16),
            jax.ShapeDtypeStruct((deep, size), BF16),
            jax.ShapeDtypeStruct((2 * block_rows * size, wide_row), BF16),
            jax.ShapeDtypeStruct((block_rows * size, wide_row), BF16),
            table,
        ],
        [DMA((1,))],
    )(held, other, other_ids, own)
    parted = (direct_pair, direct_low, ids, other_ids, counts)
    direct = functools.partial(direct_kernel, rows, block_rows, slots)
    (image,) = call(direct, "first_direct", index + [VMEM] * (rows + 1), [tile], [work])(
        *parted, own, tiles, *arrived
    )
    images = sum_over_pairs(image)
    *messages, own, tiles, gram = call(
        functools.partial(second_kernel, rows, parts // 2, block_rows, slots),
        "second_transposed",
        index + [VMEM] * (parts // 2),
        [flat(tall + extra)] * half + [tile, tile, flat(extra)],
        [work],
    )(pair, low, ids, other_ids, counts, *images)
    arrived = round_over_rows(messages, rows - 1)
    image, gram = call(direct, "second_direct", index + [VMEM] * (rows + 2), [tile, flat(extra)], [work])(
        *parted, own, tiles, *arrived, gram
    )
    images = sum_over_pairs(image)
    inverse, prior = call(functools.partial(factor_kernel, total), "factor", [VMEM] * 2, [square, across])(gram, tiles)
    image, both = call(gram_kernel, "gram", [VMEM] * (parts // 2 + 2), [across, flat(2 * extra)])(
        inverse, prior, *images
    )
    arrived = round_over_rows([both] * half, rows - 2)
    basis, ritz = call(
        functools.partial(last_kernel, rows, total), "last", [VMEM] * (rows + 1), [across, square]
    )(image, both, *arrived)
    return basis.T, ritz


def solution(mesh):
    return jax.shard_map(
        body,
        mesh=mesh,
        in_specs=(
            P(("dom", "row"), "nbr", None, None),
            P(("dom", "row"), "nbr"),
            P(("dom", "row")),
            P(("dom", "row"), None),
        ),
        out_specs=(P(("dom", "row"), None), P("dom", None)),
        check_vma=False,
    )
```

```python
import functools

import jax
import jax.numpy as jnp
from jax import lax
from jax.experimental import pallas as pl
from jax.experimental.pallas import tpu as pltpu
from jax.sharding import PartitionSpec as P

F32 = jnp.float32
BF16 = jnp.bfloat16
VMEM = pl.BlockSpec(memory_space=pltpu.VMEM)
SMEM = pl.BlockSpec(memory_space=pltpu.SMEM)
HBM = pl.BlockSpec(memory_space=pltpu.HBM)
DMA = pltpu.SemaphoreType.DMA
PARAMS = pltpu.CompilerParams(vmem_limit_bytes=8 * 2**20)
PANEL = 16


def tree(parts):
    while len(parts) > 1:
        parts = [parts[i] + parts[i + 1] for i in range(0, len(parts), 2)]
    return parts[0]


def split(x):
    high = x.astype(BF16)
    rest = x - high.astype(F32)
    middle = rest.astype(BF16)
    return high, middle, (rest - middle.astype(F32)).astype(BF16)


def dot(a, b, contract=0):
    return lax.dot_general(a, b, (((1,), (contract,)), ((), ())), preferred_element_type=F32)


def product(a_parts, b_parts, contract=0):
    n = a_parts[0].shape[0]
    stacked = jnp.concatenate(a_parts, axis=0)
    high = dot(stacked, b_parts[0], contract)
    middle = dot(stacked[: 2 * n], b_parts[1], contract)
    low = dot(a_parts[0], b_parts[2], contract)
    return high[:n] + ((high[n : 2 * n] + middle[:n]) + ((high[2 * n :] + middle[n:]) + low))


def shallow_product(a_parts, b_pair, b_low):
    n = a_parts[0].shape[0]
    stacked = jnp.concatenate(a_parts, axis=0)
    most = dot(jnp.concatenate([stacked, stacked], axis=1), b_pair)
    low = dot(a_parts[0], b_low)
    return most[:n] + (most[n : 2 * n] + (most[2 * n :] + low))


def narrow_product(a_parts, b_pair, b_low):
    n, width = a_parts[0].shape[0], b_low.shape[1]
    most = dot(jnp.concatenate(a_parts, axis=0), b_pair)
    high, middle = most[:, :width], most[:, width:]
    low = dot(a_parts[0], b_low)
    return high[:n] + ((high[n : 2 * n] + middle[:n]) + ((high[2 * n :] + middle[n : 2 * n]) + low))


def joined(parts, axis):
    return [jnp.concatenate(level, axis=axis) for level in zip(*parts)]


def folded(x, lanes):
    fold = lanes // x.shape[1]
    height = x.shape[0] // fold
    return jnp.concatenate([x[g * height : (g + 1) * height] for g in range(fold)], axis=1)


def unfolded(x, columns):
    return jnp.concatenate([x[:, g : g + columns] for g in range(0, x.shape[1], columns)], axis=0)


def swap(x, axis, distance):
    return lax.ppermute(x, axis, [(i, i ^ distance) for i in range(lax.axis_size(axis))])


def swap_rows(x, even, odd, across=None, alternate=False):
    rows, parts = lax.axis_size("row"), lax.axis_size("nbr")
    pairs = []
    for r in range(rows):
        for n in range(parts):
            d = odd if (n + alternate * bin(r).count("1")) % 2 else even
            m = n ^ (alternate * bin(d).count("1") % 2 if across is None else across)
            pairs.append((r * parts + n, (r ^ d) * parts + m))
    return lax.ppermute(x, ("row", "nbr"), pairs)


def shares(rows, common):
    rest = [d for d in range(1, rows) if d != common]
    return list(zip(rest[::2], rest[1::2]))


class Place:
    def __init__(self, rows, block_rows, slots, columns, common=None):
        self.row = lax.axis_index("row")
        self.part = lax.axis_index("nbr")
        self.odd = self.part & 1
        self.block_rows, self.slots = block_rows, slots
        self.first_row = self.row * self.block_rows
        self.rows, self.common = rows, rows - 1 if common is None else common
        pairs = shares(rows, self.common)
        self.role = self.odd
        for k in range(0 if common is None else (rows - 1).bit_length()):
            self.role = self.role ^ ((self.row >> k) & 1)
        self.peers = [self.row ^ jnp.where(self.role == 0, a, b) for a, b in pairs] + [self.row ^ self.common]
        self.others_peers = [self.row ^ jnp.where(self.role == 0, b, a) for a, b in pairs]
        self.columns = columns

    def column(self, ids, m, i, p):
        own, other = ids
        return jnp.where(self.odd == m, own[i, p], other[i, p])

    def weight(self, column, counts, m, i, p):
        used = (self.part - self.odd + m) * self.slots + p < counts[i]
        return jnp.where(used, jnp.where(column == self.first_row + i, 0.5, 1.0), 0.0).astype(F32)

    def tile(self, i):
        return slice(i * self.columns, (i + 1) * self.columns)

    def by_distance(self, mine, received, handed):
        ordered = {0: mine, self.common: received[-1]}
        for (even, odd), a, b in zip(shares(self.rows, self.common), received, handed):
            ordered[even], ordered[odd] = jnp.where(self.role == 0, a, b), jnp.where(self.role == 0, b, a)
        return [ordered[d] for d in range(self.rows)]


def stacked_blocks(blocks):
    high, middle, low = joined([split(b) for b in blocks], 1)
    return jnp.concatenate([high, middle], axis=0), low


def scatter(place, value, ids, counts, i, out):
    size = out.shape[2]
    for m in range(2):
        for p in range(place.slots):
            at = (m * place.slots + p) * size
            j = place.column(ids, m, i, p)
            out[j] += value[:, at : at + size] * place.weight(j, counts, m, i, p)


def direct_products(place, pair, low, ids, counts, whole, i):
    far = []
    for m in range(2):
        for p in range(place.slots):
            j = place.column(ids, m, i, p)
            far.append(split(whole[j] * place.weight(j, counts, m, i, p)))
    at = slice(i * len(far) * pair.shape[1] // 2, (i + 1) * len(far) * pair.shape[1] // 2)
    return narrow_product(joined(far, 1), pair[at], low[at])


def fill(place, messages, products, tiles, own):
    n = place.block_rows
    for i in range(n):
        tile = tiles[place.tile(i)]
        for peer, out in zip(place.peers, messages):
            out[place.tile(i)] = jnp.where(place.row < peer, products[peer * n + i], tile)
        own[place.tile(i)] = products[place.first_row + i]


def load_kernel(blocks, ids, counts, start, held, ids_s, counts_s, tiles, sems):
    size, columns = blocks.shape[2], start.shape[0]
    copies = [
        pltpu.make_async_copy(blocks, held, sems.at[0]),
        pltpu.make_async_copy(ids, ids_s, sems.at[1]),
        pltpu.make_async_copy(counts, counts_s, sems.at[2]),
    ]
    for i in range(blocks.shape[0]):
        source = start.at[:, i * size : (i + 1) * size]
        copies.append(pltpu.make_async_copy(source, tiles.at[i * columns : (i + 1) * columns], sems.at[3 + i]))
    for copy in copies:
        copy.start()
    for copy in copies:
        copy.wait()


def own_kernel(rows, held, ids, counts, tiles, products):
    place = Place(rows, *held.shape[:2], products.shape[1])
    size = products.shape[2]
    products[...] = jnp.zeros_like(products)
    for i in range(place.block_rows):
        stored = stacked_blocks([held[i, p] for p in range(place.slots)])
        value = shallow_product(split(tiles[place.tile(i)]), *stored)
        for p in range(place.slots):
            j = ids[i, p]
            products[j] += value[:, p * size : (p + 1) * size] * place.weight(j, counts, place.odd, i, p)


def first_kernel(rows, other, other_ids, counts, tiles, started, *refs):
    messages, (own, products) = refs[:-2], refs[-2:]
    size = products.shape[2]
    place = Place(rows, *other.shape[:2], products.shape[1])
    terms = []
    for i in range(place.block_rows):
        stored = stacked_blocks([other[i, p] for p in range(place.slots)])
        value = shallow_product(split(tiles[place.tile(i)]), *stored)
        for p in range(place.slots):
            used = (place.part + 1 - 2 * place.odd) * place.slots + p < counts[i]
            j = jnp.broadcast_to(other_ids[i : i + 1, p : p + 1], (8, size))
            c = jnp.where(j == place.first_row + i, 0.5, 1.0)
            terms.append((jnp.where(used, j, -1), c, value[:, p * size : (p + 1) * size]))
    copies = place.columns // 8
    for block in range(products.shape[0]):
        total = jnp.zeros_like(started[block])
        for j, c, value in terms:
            total += jnp.concatenate([jnp.where(j == block, c, 0.0)] * copies, axis=0) * value
        products[block] = started[block] + total
    fill(place, messages, products, tiles, own)


def split_kernel(held, other, other_ids, after, direct_pair, direct_low, pair, low, other_s, sem):
    block_rows, slots, size, _ = held.shape
    odd = lax.axis_index("nbr") & 1
    copy = pltpu.make_async_copy(other_ids, other_s, sem.at[0])
    copy.start()
    at = 0
    for i in range(block_rows):
        stored = [jnp.where(odd == m, held[i, p], other[i, p]) for m in range(2) for p in range(slots)]
        for b in stored:
            high, middle, rest = split(b.T)
            direct_pair[at : at + size, :size] = high
            direct_pair[at : at + size, size:] = middle
            direct_low[at : at + size] = rest
            at += size
        pair[2 * i * size : 2 * (i + 1) * size], low[i * size : (i + 1) * size] = stacked_blocks(stored)
    copy.wait()


def direct_kernel(rows, block_rows, slots, pair, low, ids, other_ids, counts, own, tiles, *refs):
    half = rows // 2
    received, handed, refs = refs[:half], refs[half : rows - 1], refs[rows - 1 :]
    *gram, whole = refs
    n, columns = block_rows, whole.shape[1]
    place = Place(rows, block_rows, slots, columns)
    for i in range(n):
        whole[place.first_row + i] = tiles[place.tile(i)]
        for peer, message in zip(place.peers + place.others_peers, received + handed):
            whole[peer * n + i] = message[place.tile(i)]
    if len(gram) == 1:
        (out,) = gram
    else:
        mine, out, total = gram
        tall = n * columns
        total[...] = tree(place.by_distance(mine[...], [m[tall:] for m in received], [m[tall:] for m in handed]))
    for i in range(n):
        at = place.tile(i)
        arrived = place.by_distance(own[at], [m[at] for m in received], [m[at] for m in handed])
        value = arrived[0]
        for s in range(1, rows):
            value += jnp.where(place.row > (place.row ^ s), arrived[s], 0.0)
        out[at] = value + direct_products(place, pair, low, (ids, other_ids), counts, whole, i)


def second_kernel(rows, parts, block_rows, slots, pair, low, ids, other_ids, counts, *refs):
    images, refs = refs[:parts], refs[parts:]
    messages, (own, tiles, gram, products) = refs[: rows // 2], refs[rows // 2 :]
    n, columns, size = block_rows, products.shape[1], products.shape[2]
    place = Place(rows, block_rows, slots, columns)
    tiles[...] = tree([image[...] for image in images])
    products[...] = jnp.zeros_like(products)
    for i in range(n):
        value = shallow_product(
            split(tiles[place.tile(i)]),
            pair[2 * i * size : 2 * (i + 1) * size],
            low[i * size : (i + 1) * size],
        )
        scatter(place, value, (ids, other_ids), counts, i, products)
    fill(place, messages, products, tiles, own)
    whole = joined([split(tiles[place.tile(i)]) for i in range(n)], 1)
    packed = folded(product(whole, whole, 1), size)
    gram[...] = packed
    for message in messages:
        message[n * columns :] = packed


def eliminated(gram, rest):
    n, width = gram.shape[0], rest.shape[1]
    groups = [[gram[g : g + 8], rest[g : g + 8]] for g in range(0, n, 8)]
    height = lax.broadcasted_iota(jnp.int32, (8, 1), 0)
    for first in range(0, n, PANEL):
        columns = [
            [jnp.broadcast_to(group[0][:, first + t : first + t + 1], (8, 128)) for group in groups]
            for t in range(PANEL)
        ]
        for t in range(PANEL):
            k = first + t
            gk, sk = k // 8, k % 8
            pivot = columns[t][gk][sk : sk + 1]
            inverse = 1.0 / pivot
            root = lax.rsqrt(pivot)
            source = [x[sk : sk + 1] for x in groups[gk]]
            steps = {}
            for g in range(gk, len(groups)):
                m = columns[t][g] * inverse
                steps[g] = jnp.where(height > sk, m, 0.0) if g == gk else m
            for u in range(t + 1, PANEL):
                head = columns[u][gk][sk : sk + 1]
                for g in range(gk, len(groups)):
                    columns[u][g] = columns[u][g] - steps[g] * head
            for g in range(gk, len(groups)):
                groups[g] = [x - wide(steps[g], x.shape[1]) * s for x, s in zip(groups[g], source)]
            groups[gk][1] = jnp.where(height == sk, groups[gk][1] * wide(root, width), groups[gk][1])
    return jnp.concatenate([group[1] for group in groups], axis=0)


def wide(x, lanes):
    if lanes <= x.shape[1]:
        return x[:, :lanes]
    return jnp.concatenate([x] * (lanes // x.shape[1]), axis=1)


def identity(n):
    rows = lax.broadcasted_iota(jnp.int32, (n, n), 0)
    return jnp.where(rows == lax.broadcasted_iota(jnp.int32, (n, n), 1), 1.0, 0.0)


def factor_kernel(total, gram, tiles, inverse, prior):
    columns = inverse.shape[0]
    lower = eliminated(unfolded(gram[...], columns) / total, identity(columns))
    inverse[...] = lower
    parts = [split(tiles[i : i + columns]) for i in range(0, tiles.shape[0], columns)]
    prior[...] = product(split(lower), joined(parts, 1))


def gram_kernel(inverse, prior, *refs):
    images, (image, out) = refs[:-2], refs[-2:]
    columns = inverse.shape[0]
    new = split(tree([part[...] for part in images]))
    rows = range(0, new[0].shape[0], columns)
    value = product(split(inverse[...]), [jnp.concatenate([x[i : i + columns] for i in rows], axis=1) for x in new])
    image[...] = value
    value = split(value)
    both = product(joined([value, split(prior[...])], 0), value, 1)
    out[...] = folded(both, out.shape[1])


def last_kernel(rows, total, image, mine, *refs):
    half = rows // 2
    received, handed, (basis, ritz) = refs[:half], refs[half : rows - 1], refs[rows - 1 :]
    columns = ritz.shape[0]
    place = Place(rows, 0, 0, columns, 1)
    parts = place.by_distance(mine[...], [m[...] for m in received], [m[...] for m in handed])
    both = unfolded(tree(parts) / total, columns)
    ritz[...] = both[columns:]
    basis[...] = eliminated(both[:columns], image[...])


def body(blocks, partner_ids, counts, start):
    block_rows, slots, size, _ = blocks.shape
    columns = start.shape[1]
    rows, parts = lax.axis_size("row"), lax.axis_size("nbr")
    half = rows // 2
    all_blocks = block_rows * rows
    total = float(all_blocks * size)
    extra = columns * columns // size

    def flat(height):
        return jax.ShapeDtypeStruct((height, size), F32)

    tall = block_rows * columns
    tile, square = flat(tall), jax.ShapeDtypeStruct((columns, columns), F32)
    across = jax.ShapeDtypeStruct(start.shape[::-1], F32)
    table = pltpu.SMEM(partner_ids.shape, jnp.int32)
    work = pltpu.VMEM((all_blocks, columns, size), F32)

    def call(kernel, name, specs, outs, scratch=()):
        return pl.pallas_call(
            kernel,
            name=name,
            in_specs=specs,
            out_specs=[VMEM if isinstance(out, jax.ShapeDtypeStruct) else SMEM for out in outs],
            out_shape=outs,
            scratch_shapes=scratch,
            compiler_params=PARAMS,
        )

    def round_over_rows(messages, common):
        received = [swap_rows(m, *pair, alternate=common == 1) for m, pair in zip(messages, shares(rows, common))]
        last = swap_rows(messages[-1], common, common, 1)
        return received + [last] + [swap(m, "nbr", 1) for m in received]

    def sum_over_pairs(image):
        return [image] + [swap(image, "nbr", s + 0) for s in range(2, parts, 2)]

    other = swap(blocks, "nbr", 1)
    other_ids = swap(partner_ids, "nbr", 1)
    held, ids, counts, tiles = call(
        load_kernel,
        "load",
        [HBM] * 4,
        [jax.ShapeDtypeStruct(blocks.shape, F32), table, pltpu.SMEM(counts.shape, jnp.int32), tile],
        [DMA((3 + block_rows,))],
    )(*[pltpu.with_memory_space_constraint(x, pltpu.HBM) for x in (blocks, partner_ids, counts, start.T)])
    (started,) = call(
        functools.partial(own_kernel, rows),
        "own_transposed",
        [VMEM, SMEM, SMEM, VMEM],
        [jax.ShapeDtypeStruct(work.shape, F32)],
    )(held, ids, counts, tiles)
    *messages, own = call(
        functools.partial(first_kernel, rows),
        "first_transposed",
        [VMEM, VMEM, SMEM, VMEM, VMEM],
        [tile] * (half + 1),
        [work],
    )(other, other_ids, counts, tiles, started)
    index = [VMEM, VMEM, SMEM, SMEM, SMEM]
    arrived = round_over_rows(messages, rows - 1)
    deep = 2 * block_rows * slots * size
    wide_row = 2 * slots * size
    direct_pair, direct_low, pair, low, other_ids = call(
        split_kernel,
        "split",
        [VMEM] * 4,
        [
            jax.ShapeDtypeStruct((deep, 2 * size), BF16),
            jax.ShapeDtypeStruct((deep, size), BF16),
            jax.ShapeDtypeStruct((2 * block_rows * size, wide_row), BF16),
            jax.ShapeDtypeStruct((block_rows * size, wide_row), BF16),
            table,
        ],
        [DMA((1,))],
    )(held, other, other_ids, own)
    parted = (direct_pair, direct_low, ids, other_ids, counts)
    direct = functools.partial(direct_kernel, rows, block_rows, slots)
    (image,) = call(direct, "first_direct", index + [VMEM] * (rows + 1), [tile], [work])(
        *parted, own, tiles, *arrived
    )
    images = sum_over_pairs(image)
    *messages, own, tiles, gram = call(
        functools.partial(second_kernel, rows, parts // 2, block_rows, slots),
        "second_transposed",
        index + [VMEM] * (parts // 2),
        [flat(tall + extra)] * half + [tile, tile, flat(extra)],
        [work],
    )(pair, low, ids, other_ids, counts, *images)
    arrived = round_over_rows(messages, rows - 1)
    image, gram = call(direct, "second_direct", index + [VMEM] * (rows + 2), [tile, flat(extra)], [work])(
        *parted, own, tiles, *arrived, gram
    )
    images = sum_over_pairs(image)
    inverse, prior = call(functools.partial(factor_kernel, total), "factor", [VMEM] * 2, [square, across])(gram, tiles)
    image, both = call(gram_kernel, "gram", [VMEM] * (parts // 2 + 2), [across, flat(2 * extra)])(
        inverse, prior, *images
    )
    arrived = round_over_rows([both] * half, 1)
    basis, ritz = call(
        functools.partial(last_kernel, rows, total), "last", [VMEM] * (rows + 1), [across, square]
    )(image, both, *arrived)
    return basis.T, ritz


def solution(mesh):
    return jax.shard_map(
        body,
        mesh=mesh,
        in_specs=(
            P(("dom", "row"), "nbr", None, None),
            P(("dom", "row"), "nbr"),
            P(("dom", "row")),
            P(("dom", "row"), None),
        ),
        out_specs=(P(("dom", "row"), None), P("dom", None)),
        check_vma=False,
    )
```
